256 devices in a mesh: leaf: 128 (over x, y, z), rhs: 2 (over core).
Axes of the slice: x: 4, y: 4, z: 8, core: 2. Of those that a mesh axis runs over, the one named last changes fastest.
Arguments:
- right_sides: float32 [16, 262144], P('rhs', 'leaf'), may hold values from -6 to 6
- point_order: int32 [262144], P('leaf'), may hold values from 0 to 262143, as said below
- leaf_basis: bfloat16 [2048, 64, 128], P('leaf'), may hold values from -0.5 to 0.5
- transfer: bfloat16 [1920, 64, 128], P('leaf'), may hold values from -0.5 to 0.5
- coupling: bfloat16 [3968, 64, 512], P('leaf'), may hold values from -0.25 to 0.25
- far_list: int32 [3968, 8], P('leaf'), may hold values from 0 to 2047, as said below
- far_count: int32 [3968], P('leaf'), may hold values from 0 to 8
- coarse_transfer: bfloat16 [96, 64, 128], replicated, may hold values from -0.5 to 0.5
- coarse_coupling: bfloat16 [96, 64, 192], replicated, may hold values from -0.4375 to 0.4375
- coarse_list: int32 [96, 3], replicated, may hold values from 0 to 63, as said below
- coarse_count: int32 [96], replicated, may hold values from 0 to 3
- near_block: bfloat16 [2048, 28, 128, 128], P('leaf', 'rhs'), may hold values from -0.125 to 0.125
- near_list: int32 [2048, 28], P('leaf', 'rhs'), may hold values from 0 to 2047, as said below
- near_count: int32 [2048], P('leaf'), may hold values from 1 to 27
Outputs:
- product: float32 [16, 262144], P('rhs', 'leaf')
The draws below stay inside these ranges and needn't reach their ends.
Inputs may be any that keep to these rules, and one draw needn't show every extreme that they name: `point_order`: each aligned block of 2048 entries is a permutation of that block's own positions. `far_list`: leaf j is the cell (j // 16, y, z) of a grid of 128 x 4 x 4 cells, y taken from the even and z from the odd bits of j mod 16; a node is the box of its leaves. Slots below far_count of node j at level h <= D (w nodes a block) hold distinct nodes of level h whose boxes do not touch node j's box while their parents' boxes touch or equal the parent's box; every entry equals j + k with |k| <= 3 w; unused slots hold j. `coarse_list`: slots below coarse_count of node j at level D + g hold distinct nodes of that level equal to j + k with 2 <= |k| <= 3 and parents at most one step from j's parent; unused slots hold j. `near_list`: slot 0 of leaf j is j; slots 1 to near_count - 1 hold distinct other leaves whose cells touch leaf j's cell in the grid described for far_list; later slots hold j.
All inputs are finite; a program needn't handle non-finite values.
Results may differ from the reference program's by a relative error of at most 0.017.
Values may be sent and summed in bfloat16 or wider, within the bound.
A program may use at most 128 MiB of HBM per device.

```python
import jax
import jax.numpy as jnp
import numpy as np
from jax import lax

LEAF = 128
RANK = 64
RHS = 16
SIDE = 4
LEAF_DEV = 16
NEAR = 28
FAR = 8
FARC = 3
TOP = 2
LEAVES = 2048
POINTS = 262144
PACK = 3968
UPPER = 1920
COARSE = 96
N_LEAF = 128


def cell_of(local):
    cell_y = jnp.zeros_like(local)
    cell_z = jnp.zeros_like(local)
    for bit_place in range(LEAF_DEV.bit_length() - 1):
        bit_value = local >> bit_place & 1
        if bit_place % 2 == 0:
            cell_y = cell_y + (bit_value << bit_place // 2)
        else:
            cell_z = cell_z + (bit_value << bit_place // 2)
    return (cell_y, cell_z)


def index_of(cell_y, cell_z):
    local = jnp.zeros_like(cell_y)
    for bit_place in range(LEAF_DEV.bit_length() - 1):
        if bit_place % 2 == 0:
            local = local + ((cell_y >> bit_place // 2 & 1) << bit_place)
        else:
            local = local + ((cell_z >> bit_place // 2 & 1) << bit_place)
    return local


def near_layout(key):
    key = jax.random.fold_in(key, 41)
    rate_key, keep_key, order_key = jax.random.split(key, 3)
    leaves_all = N_LEAF * LEAF_DEV
    leaf_ids = jnp.arange(leaves_all, dtype=jnp.int32)
    slab_here = leaf_ids // LEAF_DEV
    cell_y, cell_z = cell_of(leaf_ids % LEAF_DEV)
    moves = np.array([(move_x, move_y, move_z) for move_x in (-1, 0, 1) for move_y in (-1, 0, 1) for move_z in (-1, 0, 1) if (move_x, move_y, move_z) != (0, 0, 0)], dtype=np.int32)
    other_slab = slab_here[:, None] + jnp.asarray(moves[:, 0])[None, :]
    other_y = cell_y[:, None] + jnp.asarray(moves[:, 1])[None, :]
    other_z = cell_z[:, None] + jnp.asarray(moves[:, 2])[None, :]
    inside = (other_slab >= 0) & (other_slab < N_LEAF) & (other_y >= 0) & (other_y < SIDE) & (other_z >= 0) & (other_z < SIDE)
    device_rate = jax.random.randint(rate_key, (N_LEAF,), 2, 9)
    device_rate = jnp.where(jnp.arange(N_LEAF) == 1, 8, device_rate)
    kept = jax.random.randint(keep_key, (leaves_all, 26), 0, 8) < device_rate[slab_here][:, None]
    valid = inside & kept
    other_ids = jnp.clip(other_slab, 0, N_LEAF - 1) * LEAF_DEV + index_of(jnp.clip(other_y, 0, SIDE - 1), jnp.clip(other_z, 0, SIDE - 1))
    slot_number = jnp.arange(26, dtype=jnp.int32)[None, :]
    score = jnp.where(valid, jax.random.randint(order_key, (leaves_all, 26), 0, 1 << 20) * 32 + slot_number, (1 << 26) + slot_number)
    order = jnp.argsort(score, axis=1)
    kept_width = min(NEAR - 1, 26)
    picked = jnp.take_along_axis(other_ids, order[:, :kept_width], axis=1)
    live = jnp.sum(valid.astype(jnp.int32), axis=1)
    slot_used = jnp.arange(kept_width)[None, :] < live[:, None]
    rest = jnp.where(slot_used, picked, leaf_ids[:, None])
    filler = jnp.broadcast_to(leaf_ids[:, None], (leaves_all, NEAR - 1 - kept_width))
    listed = jnp.concatenate([leaf_ids[:, None], rest, filler], axis=1)
    return (listed.astype(jnp.int32), (live + 1).astype(jnp.int32))


def local_layout():
    packs = 2 * LEAF_DEV - 1
    rows_all = jnp.arange(N_LEAF * packs, dtype=jnp.int32)
    owner = rows_all // packs
    within = rows_all % packs
    row_width = jnp.zeros_like(rows_all)
    row_first = jnp.zeros_like(rows_all)
    row_height = jnp.zeros_like(rows_all)
    for height in range(LEAF_DEV.bit_length()):
        node_width = LEAF_DEV >> height
        first_row = 2 * LEAF_DEV - 2 * node_width
        inside = (within >= first_row) & (within < first_row + node_width)
        row_width = jnp.where(inside, node_width, row_width)
        row_first = jnp.where(inside, first_row, row_first)
        row_height = jnp.where(inside, height, row_height)
    return (owner, within, row_width, within - row_first, row_height)


def far_layout(key):
    key = jax.random.fold_in(key, 51)
    limit_key, order_key = jax.random.split(key)
    tree_depth = LEAF_DEV.bit_length() - 1
    owner, within, row_width, local, row_height = local_layout()
    row_total = owner.shape[0]
    node_index = owner * row_width + local
    leaves_each = LEAF_DEV // row_width
    start_y, start_z = cell_of(local * leaves_each)
    ones = jnp.ones_like(row_height)
    size_y = jnp.left_shift(ones, (row_height + 1) // 2)
    size_z = jnp.left_shift(ones, row_height // 2)
    grid_y = SIDE // size_y
    grid_z = SIDE // size_z
    node_y = start_y // size_y
    node_z = start_z // size_z
    spans = np.arange(-3, 4)
    moves = np.array([(move_x, move_y, move_z) for move_x in spans for move_y in spans for move_z in spans], dtype=np.int32)
    move_x = jnp.asarray(moves[:, 0])[None, :]
    move_y = jnp.asarray(moves[:, 1])[None, :]
    move_z = jnp.asarray(moves[:, 2])[None, :]
    other_x = owner[:, None] + move_x
    other_y = node_y[:, None] + move_y
    other_z = node_z[:, None] + move_z
    inside = (other_x >= 0) & (other_x < N_LEAF) & (other_y >= 0) & (other_y < grid_y[:, None]) & (other_z >= 0) & (other_z < grid_z[:, None])
    apart = jnp.asarray(np.max(np.abs(moves), axis=1) >= 2)[None, :]
    split_x = (row_height == tree_depth)[:, None]
    split_y = ((row_height != tree_depth) & (row_height % 2 == 0))[:, None]
    split_z = ((row_height != tree_depth) & (row_height % 2 == 1))[:, None]

    def parent_of(coord, flag):
        return jnp.where(flag, jnp.floor_divide(coord, 2), coord)
    close_x = jnp.abs(parent_of(other_x, split_x) - parent_of(owner[:, None], split_x)) <= 1
    close_y = jnp.abs(parent_of(other_y, split_y) - parent_of(node_y[:, None], split_y)) <= 1
    close_z = jnp.abs(parent_of(other_z, split_z) - parent_of(node_z[:, None], split_z)) <= 1
    valid = inside & apart & close_x & close_y & close_z
    first_leaf = index_of(jnp.clip(other_y, 0, SIDE - 1) * size_y[:, None], jnp.clip(other_z, 0, SIDE - 1) * size_z[:, None])
    other_node = jnp.clip(other_x, 0, N_LEAF - 1) * row_width[:, None] + first_leaf // leaves_each[:, None]
    slot_limit = jax.random.randint(limit_key, (row_total,), 1, FAR + 1)
    slot_limit = jnp.where(within == 0, FAR, slot_limit)
    counts = jnp.minimum(jnp.sum(valid.astype(jnp.int32), axis=1), slot_limit)
    move_number = jnp.arange(moves.shape[0], dtype=jnp.int32)[None, :]
    score = jnp.where(valid, jax.random.randint(order_key, valid.shape, 0, 1 << 20) * 512 + move_number, (1 << 30) + move_number)
    order = jnp.argsort(score, axis=1)
    picked = jnp.take_along_axis(other_node, order[:, :FAR], axis=1)
    slot_used = jnp.arange(FAR)[None, :] < counts[:, None]
    listed = jnp.where(slot_used, picked, node_index[:, None])
    return (listed.astype(jnp.int32), counts.astype(jnp.int32))


def coarse_layout():
    rows_all = jnp.arange(COARSE, dtype=jnp.int32)
    row_width = jnp.zeros_like(rows_all)
    row_first = jnp.zeros_like(rows_all)
    for height in range(1, TOP + 1):
        node_width = N_LEAF >> height
        first_row = N_LEAF - 2 * node_width
        inside = (rows_all >= first_row) & (rows_all < first_row + node_width)
        row_width = jnp.where(inside, node_width, row_width)
        row_first = jnp.where(inside, first_row, row_first)
    return (rows_all - row_first, row_width)


def coarse_partners(key):
    key = jax.random.fold_in(key, 61)
    limit_key, order_key = jax.random.split(key)
    node_index, row_width = coarse_layout()
    moves = jnp.arange(-3, 4, dtype=jnp.int32)[None, :]
    other = node_index[:, None] + moves
    inside = (other >= 0) & (other < row_width[:, None])
    apart = jnp.abs(moves) >= 2
    close = jnp.abs(jnp.floor_divide(other, 2) - (node_index // 2)[:, None]) <= 1
    valid = inside & apart & close
    slot_limit = jax.random.randint(limit_key, (COARSE,), 1, FARC + 1)
    slot_limit = jnp.where(jnp.arange(COARSE) == 2, FARC, slot_limit)
    counts = jnp.minimum(jnp.sum(valid.astype(jnp.int32), axis=1), slot_limit)
    move_number = jnp.arange(7, dtype=jnp.int32)[None, :]
    score = jnp.where(valid, jax.random.randint(order_key, valid.shape, 0, 1 << 20) * 8 + move_number, (1 << 26) + move_number)
    order = jnp.argsort(score, axis=1)
    picked = jnp.take_along_axis(other, order[:, :FARC], axis=1)
    slot_used = jnp.arange(FARC)[None, :] < counts[:, None]
    listed = jnp.where(slot_used, picked, node_index[:, None])
    return (listed.astype(jnp.int32), counts.astype(jnp.int32))


def draw_point_order(key, part):
    key = jax.random.fold_in(key, 11)
    own_points = LEAF * LEAF_DEV
    keys_all = jax.random.split(key, N_LEAF)
    shuffled = jax.vmap(lambda one_key: jax.random.permutation(one_key, own_points))(keys_all)
    shifted = shuffled + own_points * jnp.arange(N_LEAF)[:, None]
    return shifted.reshape(-1).astype(jnp.int32)


def draw_far_list(key, part):
    shared = far_layout(key)
    return shared[0]


def draw_far_count(key, part):
    shared = far_layout(key)
    return shared[1]


def draw_coarse_list(key, part):
    shared = coarse_partners(key)
    return shared[0]


def draw_coarse_count(key, part):
    shared = coarse_partners(key)
    return shared[1]


def draw_near_list(key, part):
    shared = near_layout(key)
    return shared[0]


def draw_near_count(key, part):
    shared = near_layout(key)
    return shared[1]


def shard_levels(own_key, shape, cuts, least, largest):
    factor_of = 1.0
    for axis_at, parts in cuts:
        draws = jax.random.uniform(jax.random.fold_in(jax.random.fold_in(own_key, 6), axis_at), (parts,), jnp.float32, least / len(cuts), largest / len(cuts))
        factor_of = factor_of * jnp.repeat(jnp.exp(draws), shape[axis_at] // parts).reshape((-1,) + (1,) * (len(shape) - 1 - axis_at))
    return factor_of


def noise(key, dims, deviation, most, shards=(), kind=jnp.bfloat16):
    loudness = shard_levels(key, dims, shards, -0.22, 0.18) if shards else 1.0
    values = jax.random.normal(key, dims, jnp.float32) * deviation * loudness
    return jnp.minimum(jnp.maximum(values, -most), most).astype(kind)


def setup_inputs(seed: int = 0) -> dict:
    key_list = jax.random.split(jax.random.key(seed), 15)
    right_sides = noise(key_list[0], (RHS, POINTS), 1.0, 6.0, ((0, 2), (1, 128)), jnp.float32)
    point_order = draw_point_order(jax.random.fold_in(key_list[14], 71), 0)
    leaf_basis = noise(key_list[2], (LEAVES, RANK, LEAF), LEAF ** -0.5, 0.5, ((0, 128),))
    transfer = noise(key_list[3], (UPPER, RANK, 2 * RANK), (2 * RANK) ** -0.5, 0.5, ((0, 128),))
    coupling = noise(key_list[4], (PACK, RANK, FAR * RANK), (FAR * RANK) ** -0.5, 0.25, ((0, 128),))
    far_list = draw_far_list(jax.random.fold_in(key_list[14], 71), 0)
    far_count = draw_far_count(jax.random.fold_in(key_list[14], 71), 0)
    coarse_transfer = noise(key_list[7], (COARSE, RANK, 2 * RANK), (2 * RANK) ** -0.5, 0.5)
    coarse_coupling = noise(key_list[8], (COARSE, RANK, FARC * RANK), (FARC * RANK) ** -0.5, 0.4375)
    coarse_list = draw_coarse_list(jax.random.fold_in(key_list[14], 71), 0)
    coarse_count = draw_coarse_count(jax.random.fold_in(key_list[14], 71), 0)
    near_block = noise(key_list[11], (LEAVES, NEAR, LEAF, LEAF), (LEAF * NEAR // 2) ** -0.5, 0.125, ((0, 128), (1, 2)))
    near_list = draw_near_list(jax.random.fold_in(key_list[14], 71), 0)
    near_count = draw_near_count(jax.random.fold_in(key_list[14], 71), 0)
    return dict(right_sides=right_sides, point_order=point_order, leaf_basis=leaf_basis, transfer=transfer, coupling=coupling, far_list=far_list, far_count=far_count, coarse_transfer=coarse_transfer, coarse_coupling=coarse_coupling, coarse_list=coarse_list, coarse_count=coarse_count, near_block=near_block, near_list=near_list, near_count=near_count)


def lift_terms(matrices, vectors):
    return jnp.einsum("nab,rnb->rna", matrices.astype(jnp.float32), vectors.astype(jnp.float32))


def lower_terms(matrices, vectors):
    return jnp.einsum("nab,rna->rnb", matrices.astype(jnp.float32), vectors.astype(jnp.float32))


def couple_far(matrices, window, slot_ids, counts):
    live_mask = jnp.arange(slot_ids.shape[1])[None, :] < counts[:, None]
    picked = window[:, slot_ids] * live_mask[None, :, :, None].astype(window.dtype)
    picked = picked.reshape(window.shape[0], slot_ids.shape[0], slot_ids.shape[1] * window.shape[2])
    return lift_terms(matrices, picked)


def take_rows(table, first_row, node_width):
    return table[:, first_row:first_row + node_width].reshape((-1,) + table.shape[2:])


def reference(right_sides, point_order, leaf_basis, transfer, coupling, far_list, far_count, coarse_transfer, coarse_coupling, coarse_list, coarse_count, near_block, near_list, near_count):
    tree_depth = LEAF_DEV.bit_length() - 1
    packs = 2 * LEAF_DEV - 1
    points = right_sides[:, point_order].astype(jnp.bfloat16)
    leaf_rows = points.reshape(RHS, N_LEAF * LEAF_DEV, LEAF)
    coupling_rows = coupling.reshape(N_LEAF, packs, RANK, FAR * RANK)
    list_rows = far_list.reshape(N_LEAF, packs, FAR)
    count_rows = far_count.reshape(N_LEAF, packs)
    upper_rows = transfer.reshape(N_LEAF, LEAF_DEV - 1, RANK, 2 * RANK)
    coeffs = [lift_terms(leaf_basis, leaf_rows).astype(jnp.bfloat16)]
    parents = [None]
    for height in range(1, tree_depth + 1):
        node_width = LEAF_DEV >> height
        matrices = take_rows(upper_rows, LEAF_DEV - 2 * node_width, node_width)
        parents.append(matrices)
        coeffs.append(lift_terms(matrices, coeffs[-1].reshape(RHS, -1, 2 * RANK)).astype(jnp.bfloat16))
    for height in range(1, TOP + 1):
        node_width = N_LEAF >> height
        first_row = N_LEAF - 2 * node_width
        matrices = coarse_transfer[first_row:first_row + node_width]
        parents.append(matrices)
        coeffs.append(lift_terms(matrices, coeffs[-1].reshape(RHS, -1, 2 * RANK)).astype(jnp.bfloat16))
    incoming = []
    for height in range(tree_depth + 1):
        node_width = LEAF_DEV >> height
        first_row = 2 * LEAF_DEV - 2 * node_width
        incoming.append(couple_far(take_rows(coupling_rows, first_row, node_width), coeffs[height], take_rows(list_rows, first_row, node_width), take_rows(count_rows, first_row, node_width)))
    for height in range(1, TOP + 1):
        node_width = N_LEAF >> height
        first_row = N_LEAF - 2 * node_width
        rows_here = slice(first_row, first_row + node_width)
        incoming.append(couple_far(coarse_coupling[rows_here], coeffs[tree_depth + height], coarse_list[rows_here], coarse_count[rows_here]))
    field = incoming[-1].astype(jnp.bfloat16)
    for height in range(tree_depth + TOP - 1, -1, -1):
        down = lower_terms(parents[height + 1], field).reshape(RHS, -1, RANK)
        field = (incoming[height] + down).astype(jnp.bfloat16)
    far_part = lower_terms(leaf_basis, field).reshape(RHS, -1)

    def near_group(operands):
        blocks_here, ids_here, counts_here = operands
        live_mask = jnp.arange(NEAR)[None, :] < counts_here[:, None]
        picked = leaf_rows[:, ids_here] * live_mask[None, :, :, None].astype(jnp.bfloat16)
        return jnp.einsum("jsab,rjsb->rja", blocks_here.astype(jnp.float32), picked.astype(jnp.float32))

    near_all = lax.map(near_group, (near_block.reshape(N_LEAF, LEAF_DEV, NEAR, LEAF, LEAF), near_list.reshape(N_LEAF, LEAF_DEV, NEAR), near_count.reshape(N_LEAF, LEAF_DEV)))
    near_part = jnp.transpose(near_all, (1, 0, 2, 3)).reshape(RHS, -1)
    return far_part + near_part
```

```python
import jax
import jax.numpy as jnp
from jax import lax
from jax.experimental import pallas as pl
from jax.experimental.pallas import tpu as pltpu
from jax.sharding import PartitionSpec as P

MESH = pl.DeviceIdType.MESH
F32 = jnp.float32
BF16 = jnp.bfloat16

DEVICES = 128
LEAVES = 16
RANK = 64
LANES = 128
COLS = 8
SLOTS = 14
FAR = 8
PAIRS = 15
ROWS = 2 * LEAVES
ZERO = 3 * ROWS
NEAR_ZERO = 3 * LEAVES
HALF = DEVICES // 2
QUARTER = DEVICES // 4


def dot_nt(left, right):
    return lax.dot_general(left, right, (((1,), (1,)), ((), ())), preferred_element_type=F32)


def dot_nn(left, right):
    return lax.dot_general(left, right, (((1,), (0,)), ((), ())), preferred_element_type=F32)


def wrap(value, size):
    return lax.rem(value + size, size)


def kernel(
    rs_h,
    order_h,
    basis_h,
    transfer_h,
    coupling_h,
    flist_h,
    fcount_h,
    ctr_h,
    ccp_h,
    clist_h,
    ccount_h,
    near_h,
    nlist_h,
    ncount_h,
    out_v,
    rs_v,
    order_v,
    basis_v,
    transfer_v,
    coupling_v,
    near_v,
    flist_v,
    fcount_v,
    nlist_v,
    ncount_v,
    ctr_v,
    ccp_v,
    clist_s,
    ccount_s,
    fid_v,
    nid_v,
    fid_s,
    nid_s,
    xs_v,
    us_v,
    xr_v,
    ur_v,
    cs_v,
    cr_v,
    xw_v,
    table_v,
    up_v,
    gu_v,
    fu_v,
    ysend_v,
    yrecv_v,
    in_sem,
    near_sem,
    id_sem,
    xsend_sem,
    xrecv_sem,
    usend_sem,
    urecv_sem,
    csend_sem,
    crecv_sem,
    ysend_sem,
    yrecv_sem,
):
    me = lax.axis_index("leaf")
    core = lax.axis_index("rhs")
    other = 1 - core
    quad = lax.div(me, 4)
    in_quad = lax.rem(me, 4)
    duo = lax.div(me, 2)
    in_duo = lax.rem(me, 2)
    turn = 1 - 2 * in_duo
    duo_turn = 1 - 2 * lax.rem(duo, 2)
    quad_turn = 1 - 2 * lax.rem(quad, 2)
    quad_from = [wrap(quad + d, QUARTER) for d in (-2, 2, 3 * quad_turn)]
    duo_from = [wrap(duo + d, HALF) for d in (-2, 2, 3 * duo_turn)]
    quad_to = [quad_from[1], quad_from[0], quad_from[2]]
    duo_to = [duo_from[1], duo_from[0], duo_from[2]]
    one_to = [wrap(me + d, DEVICES) for d in (2, -2, 3 * turn)]
    root_sends = []
    for n in range(3):
        for i in range(4):
            root_sends.append((4 * quad_to[n] + i, 4 * n + in_quad))
    for n in range(3):
        for i in range(2):
            root_sends.append((2 * duo_to[n] + i, 12 + 2 * n + in_duo))
    for n in range(3):
        root_sends.append((one_to[n], 18 + n))
    left = wrap(me - 1, DEVICES)
    right = wrap(me + 1, DEVICES)
    point_sends = [(right, core, 0), (left, core, 1), (right, other, 2), (left, other, 3), (me, other, 4)]

    def fetch(source, target, sem):
        copy = pltpu.make_async_copy(source, target, sem)
        copy.start()
        return copy

    get_order = fetch(order_h, order_v, in_sem.at[0])
    get_rs = fetch(rs_h, rs_v, in_sem.at[1])
    get_basis = fetch(basis_h, basis_v, in_sem.at[2])
    get_transfer = fetch(transfer_h, transfer_v, in_sem.at[3])
    get_lists = [
        fetch(nlist_h, nlist_v, in_sem.at[4]),
        fetch(ncount_h, ncount_v, in_sem.at[5]),
        fetch(flist_h, flist_v, in_sem.at[6]),
        fetch(fcount_h, fcount_v, in_sem.at[7]),
    ]
    get_coarse = [fetch(clist_h, clist_s, in_sem.at[8]), fetch(ccount_h, ccount_s, in_sem.at[9])]
    for device_at, device_core in [(to, core) for to, _ in root_sends] + [(to, at) for to, at, _ in point_sends]:
        pl.semaphore_signal(
            pltpu.get_barrier_semaphore(),
            inc=1,
            device_id=(device_at, device_core),
            device_id_type=MESH,
        )
    for j in range(4):
        fetch(near_h.at[j], near_v.at[j], near_sem.at[j])
    for n in range(3):
        fetch(ctr_h.at[pl.ds(2 * quad_from[n], 2)], ctr_v.at[pl.ds(2 * n, 2)], in_sem.at[10])
        fetch(ctr_h.at[pl.ds(duo_from[n], 1)], ctr_v.at[pl.ds(6 + n, 1)], in_sem.at[10])
        fetch(ctr_h.at[pl.ds(HALF + quad_from[n], 1)], ctr_v.at[pl.ds(9 + n, 1)], in_sem.at[10])
    fetch(ctr_h.at[pl.ds(duo, 1)], ctr_v.at[pl.ds(12, 1)], in_sem.at[10])
    fetch(ctr_h.at[pl.ds(HALF + quad, 1)], ctr_v.at[pl.ds(13, 1)], in_sem.at[10])
    fetch(ccp_h.at[pl.ds(duo, 1)], ccp_v.at[pl.ds(0, 1)], in_sem.at[11])
    fetch(ccp_h.at[pl.ds(HALF + quad, 1)], ccp_v.at[pl.ds(1, 1)], in_sem.at[11])
    for j in range(4, LEAVES):
        fetch(near_h.at[j], near_v.at[j], near_sem.at[j])
    get_coupling = fetch(coupling_h, coupling_v, in_sem.at[12])

    low = lax.broadcasted_iota(jnp.int32, (COLS, LANES), 1) < RANK
    low16 = lax.broadcasted_iota(jnp.int32, (2 * COLS, LANES), 1) < RANK
    top16 = lax.broadcasted_iota(jnp.int32, (2 * COLS, LANES), 0) < COLS
    diagonal = low16 == top16

    def both(first, second):
        return jnp.concatenate([first, second], axis=0)

    def meet(first, second):
        return jnp.where(low, first, second)

    def flip(pair):
        return pltpu.roll(pair, RANK, 1)

    def join(product):
        return jnp.where(low, product[:COLS], product[COLS:])

    get_order.wait()
    get_rs.wait()
    place = order_v[...] - me * (LEAVES * LANES)
    for j in range(0, LEAVES, 2):
        blocks = []
        for i in (j, j + 1):
            here = jnp.broadcast_to(place[i : i + 1], (COLS, LANES))
            chunk = here // LANES
            lane = here % LANES
            block = jnp.take_along_axis(rs_v[:, 0:LANES], lane, axis=1, mode="promise_in_bounds")
            for c in range(1, LEAVES):
                found = jnp.take_along_axis(
                    rs_v[:, c * LANES : (c + 1) * LANES], lane, axis=1, mode="promise_in_bounds"
                )
                block = jnp.where(chunk == c, found, block)
            blocks.append(block)
        xs_v[j // 2] = both(*blocks).astype(BF16)

    pl.semaphore_wait(pltpu.get_barrier_semaphore(), len(root_sends) + len(point_sends))

    def remote(source, target, send_sem, recv_sem, device_at, device_core):
        return pltpu.make_async_remote_copy(
            src_ref=source,
            dst_ref=target,
            send_sem=send_sem,
            recv_sem=recv_sem,
            device_id=(device_at, device_core),
            device_id_type=MESH,
        )

    sent = []
    for device_at, device_core, slot in point_sends:
        copy = remote(
            xs_v, xr_v.at[slot], xsend_sem.at[slot], xrecv_sem.at[slot], device_at, device_core
        )
        copy.start()
        sent.append(copy)

    get_basis.wait()
    get_transfer.wait()
    own = ROWS
    for p in range(LEAVES // 2):
        matrices = basis_v[2 * p : 2 * p + 2].reshape(LANES, LANES)
        pair = join(dot_nt(xs_v[p], matrices))
        up_v[p] = pair
        table_v[own + 2 * p] = pair
        table_v[own + 2 * p + 1] = flip(pair)
    first = 0
    for width in (8, 4, 2):
        for p in range(width // 2):
            tile = both(up_v[first + 2 * p], up_v[first + 2 * p + 1]).astype(BF16)
            us_v[first // 2 + p] = tile
            row = first + 2 * p
            matrices = transfer_v[row : row + 2].reshape(LANES, LANES)
            pair = join(dot_nt(tile, matrices))
            at = first + width + p
            up_v[at] = pair
            table_v[own + 2 * at] = pair
            table_v[own + 2 * at + 1] = flip(pair)
        first += width
    last = both(up_v[14], jnp.zeros((COLS, LANES), F32)).astype(BF16)
    us_v[7] = last
    sides = []
    for slot, device_at in ((0, right), (1, left)):
        copy = remote(us_v, ur_v.at[slot], usend_sem.at[slot], urecv_sem.at[slot], device_at, core)
        copy.start()
        sides.append(copy)
    root = transfer_v[14]
    cs_v[...] = dot_nt(last, both(root, root))[:COLS].astype(BF16).astype(F32)
    for device_at, slot in root_sends:
        remote(cs_v, cr_v.at[slot], csend_sem, crecv_sem, device_at, core).start()

    for copy in get_lists:
        copy.wait()
    square = lax.broadcasted_iota(jnp.int32, (LEAVES, LEAVES), 0) == lax.broadcasted_iota(
        jnp.int32, (LEAVES, LEAVES), 1
    )
    counts = jnp.broadcast_to(ncount_v[...], (LEAVES, LEAVES))
    counts = jnp.sum(jnp.where(square, counts, 0), axis=1, keepdims=True)
    slot_at = lax.broadcasted_iota(jnp.int32, (LEAVES, SLOTS), 1) + core * SLOTS
    nid_v[...] = jnp.where(slot_at < counts, nlist_v[...] - (me - 1) * LEAVES, NEAR_ZERO)
    node = lax.broadcasted_iota(jnp.int32, (FAR, ROWS - 1), 1)
    slot_at = lax.broadcasted_iota(jnp.int32, (FAR, ROWS - 1), 0)
    entry = flist_v[...]
    row = jnp.zeros_like(entry)
    for height in range(4):
        width = LEAVES >> height
        start = ROWS - 2 * width
        side = entry // width - me + 1
        inside = (node >= start) & (node < start + width)
        row = jnp.where(inside, side * ROWS + start + entry % width, row)
    row = row + jnp.where(slot_at % 2 == 0, 0, 1 - 2 * (row % 2))
    step = entry - me
    root_row = jnp.where(step == -2, 0, jnp.where(step == 2, 1, 2))
    row = jnp.where(node == ROWS - 2, root_row, row)
    live = slot_at < fcount_v[...]
    fid_v[...] = jnp.where(live, row, jnp.where(node == ROWS - 2, 3, ZERO))
    put_near = fetch(nid_v, nid_s, id_sem.at[0])
    put_far = fetch(fid_v, fid_s, id_sem.at[1])
    zero = jnp.zeros((COLS, LANES), F32)
    table_v[ZERO] = zero
    xw_v[NEAR_ZERO] = jnp.zeros((2 * COLS, LANES), BF16)
    put_near.wait()
    put_far.wait()

    for copy in sent:
        copy.wait()

    def arrange(base, mine, theirs):
        for p in range(LEAVES // 2):
            a = mine[p].astype(F32)
            b = theirs[p].astype(F32)
            xw_v[base + 2 * p] = both(a[:COLS], b[:COLS]).astype(BF16)
            xw_v[base + 2 * p + 1] = both(a[COLS:], b[COLS:]).astype(BF16)

    arrange(0, xr_v.at[0], xr_v.at[2])
    arrange(LEAVES, xs_v, xr_v.at[4])
    arrange(2 * LEAVES, xr_v.at[1], xr_v.at[3])

    def near_leaf(j, carry):
        pltpu.make_async_copy(near_h.at[j], near_v.at[j], near_sem.at[j]).wait()
        total = jnp.zeros((2 * COLS, LANES), F32)
        for s in range(SLOTS):
            total += dot_nt(xw_v[nid_s[j, s]], near_v[j, s])
        yown = total[:COLS]
        out_v[:, pl.ds(pl.multiple_of(j * LANES, LANES), LANES)] = yown
        ysend_v[j] = total[COLS:]
        return carry

    lax.fori_loop(0, LEAVES, near_leaf, 0)
    send_near = remote(ysend_v, yrecv_v, ysend_sem, yrecv_sem, me, other)
    send_near.start()

    for copy in sides:
        copy.wait()
    for slot, base in ((0, 0), (1, 2 * ROWS)):
        for t in range(8):
            tile = ur_v[slot, t].astype(F32)
            for half in range(2):
                pair = tile[half * COLS : (half + 1) * COLS]
                table_v[base + 4 * t + 2 * half] = pair
                table_v[base + 4 * t + 2 * half + 1] = flip(pair)

    get_coupling.wait()

    def couple(p, carry):
        total = jnp.zeros((2 * COLS, LANES), F32)
        matrices = coupling_v[pl.ds(2 * p, 2)].reshape(LANES, FAR * RANK)
        for t in range(FAR // 2):
            picked = both(
                meet(table_v[fid_s[2 * t, 2 * p]], table_v[fid_s[2 * t + 1, 2 * p]]),
                meet(table_v[fid_s[2 * t, 2 * p + 1]], table_v[fid_s[2 * t + 1, 2 * p + 1]]),
            ).astype(BF16)
            total += dot_nt(picked, matrices[:, t * LANES : (t + 1) * LANES])
        gu_v[p] = join(total)
        return carry

    lax.fori_loop(0, PAIRS, couple, 0)

    pltpu.make_async_copy(ctr_h.at[pl.ds(0, 14)], ctr_v, in_sem.at[10]).wait()
    pltpu.make_async_copy(ccp_h.at[pl.ds(0, 2)], ccp_v, in_sem.at[11]).wait()
    for copy in get_coarse:
        copy.wait()
    everyone = remote(cr_v, cr_v, csend_sem, crecv_sem, me, other)
    everyone.wait_send()
    everyone.wait_recv()
    for k in range(3):
        up_v[4 * k + 3] = zero
    for n in range(3):
        pair = both(meet(cr_v[4 * n], cr_v[4 * n + 1]), meet(cr_v[4 * n + 2], cr_v[4 * n + 3]))
        upper = join(dot_nt(pair.astype(BF16), ctr_v[2 * n : 2 * n + 2].reshape(LANES, LANES)))
        matrix = ctr_v[9 + n]
        up_v[n] = dot_nt(both(upper, upper).astype(BF16), both(matrix, matrix))[:COLS]
        pair = meet(cr_v[12 + 2 * n], cr_v[13 + 2 * n])
        matrix = ctr_v[6 + n]
        up_v[4 + n] = dot_nt(both(pair, pair).astype(BF16), both(matrix, matrix))[:COLS]
        up_v[8 + n] = cr_v[18 + n]

    def upper_terms(matrix, at, node_here, base):
        rows = []
        for s in range(3):
            step = clist_s[s, at] - node_here
            row = jnp.where(step == -2, 0, jnp.where(step == 2, 1, 2))
            rows.append(base + jnp.where(s < ccount_s[at], row, 3))
        pair = meet(up_v[rows[0]], up_v[rows[1]])
        third = up_v[rows[2]]
        total = dot_nt(both(pair, pair).astype(BF16), matrix[:, :LANES])
        total += dot_nt(both(third, third)[:, :RANK].astype(BF16), matrix[:, LANES:])
        return total

    g6 = upper_terms(ccp_v[1], HALF + quad, quad, 0)
    g5 = upper_terms(ccp_v[0], duo, duo, 4)

    def pick_child(product, side):
        return jnp.where(side == 0, product, pltpu.roll(product, RANK, 1))[:, :RANK]

    field = g6.astype(BF16)
    field = g5 + pick_child(dot_nn(field, ctr_v[13]), lax.rem(duo, 2))
    field = field.astype(BF16)
    matrix = coupling_v[ROWS - 2]
    pair = meet(up_v[8 + fid_s[0, ROWS - 2]], up_v[8 + fid_s[1, ROWS - 2]])
    third = up_v[8 + fid_s[2, ROWS - 2]]
    g4 = dot_nt(both(pair, pair).astype(BF16), matrix[:, :LANES])
    g4 += dot_nt(both(third, third)[:, :RANK].astype(BF16), matrix[:, LANES : LANES + RANK])
    field = g4 + pick_child(dot_nn(field, ctr_v[12]), in_duo)
    fu_v[14] = gu_v[14] + dot_nn(field.astype(BF16), transfer_v[14])[:COLS]
    for first, width in ((12, 2), (8, 4), (0, 8)):
        for p in range(width // 2):
            pair = fu_v[first + width + p]
            spread = jnp.where(diagonal, both(pair, pair), 0.0).astype(BF16)
            row = first + 2 * p
            down = dot_nn(spread, transfer_v[row : row + 2].reshape(LANES, LANES))
            fu_v[row] = gu_v[row] + down[:COLS]
            fu_v[row + 1] = gu_v[row + 1] + down[COLS:]
    send_near.wait()
    for p in range(LEAVES // 2):
        pair = fu_v[p]
        spread = jnp.where(diagonal, both(pair, pair), 0.0).astype(BF16)
        far = dot_nn(spread, basis_v[2 * p : 2 * p + 2].reshape(LANES, LANES))
        for half in range(2):
            j = 2 * p + half
            columns = slice(j * LANES, (j + 1) * LANES)
            out_v[:, columns] += far[half * COLS : (half + 1) * COLS] + yrecv_v[j]


def body(
    right_sides,
    point_order,
    leaf_basis,
    transfer,
    coupling,
    far_list,
    far_count,
    coarse_transfer,
    coarse_coupling,
    coarse_list,
    coarse_count,
    near_block,
    near_list,
    near_count,
):
    tile = (2 * COLS, LANES)
    dma = pltpu.SemaphoreType.DMA
    return pl.pallas_call(
        kernel,
        out_shape=jax.ShapeDtypeStruct((COLS, LEAVES * LANES), F32),
        in_specs=[pl.BlockSpec(memory_space=pltpu.HBM)] * 14,
        out_specs=pl.BlockSpec(memory_space=pltpu.VMEM),
        scratch_shapes=[
            pltpu.VMEM((COLS, LEAVES * LANES), F32),
            pltpu.VMEM((LEAVES, LANES), jnp.int32),
            pltpu.VMEM((LEAVES, RANK, LANES), BF16),
            pltpu.VMEM((LEAVES - 1, RANK, LANES), BF16),
            pltpu.VMEM((ROWS - 1, RANK, FAR * RANK), BF16),
            pltpu.VMEM((LEAVES, SLOTS, LANES, LANES), BF16),
            pltpu.VMEM((FAR, ROWS - 1), jnp.int32),
            pltpu.VMEM((1, ROWS - 1), jnp.int32),
            pltpu.VMEM((LEAVES, SLOTS), jnp.int32),
            pltpu.VMEM((1, LEAVES), jnp.int32),
            pltpu.VMEM((14, RANK, LANES), BF16),
            pltpu.VMEM((2, RANK, 3 * RANK), BF16),
            pltpu.SMEM((3, 96), jnp.int32),
            pltpu.SMEM((96,), jnp.int32),
            pltpu.VMEM((FAR, ROWS - 1), jnp.int32),
            pltpu.VMEM((LEAVES, SLOTS), jnp.int32),
            pltpu.SMEM((FAR, ROWS - 1), jnp.int32),
            pltpu.SMEM((LEAVES, SLOTS), jnp.int32),
            pltpu.VMEM((LEAVES // 2,) + tile, BF16),
            pltpu.VMEM((LEAVES // 2,) + tile, BF16),
            pltpu.VMEM((5, LEAVES // 2) + tile, BF16),
            pltpu.VMEM((2, LEAVES // 2) + tile, BF16),
            pltpu.VMEM((COLS, LANES), F32),
            pltpu.VMEM((21, COLS, LANES), F32),
            pltpu.VMEM((3 * LEAVES + 1,) + tile, BF16),
            pltpu.VMEM((ZERO + 1, COLS, LANES), F32),
            pltpu.VMEM((PAIRS, COLS, LANES), F32),
            pltpu.VMEM((PAIRS, COLS, LANES), F32),
            pltpu.VMEM((PAIRS, COLS, LANES), F32),
            pltpu.VMEM((LEAVES, COLS, LANES), F32),
            pltpu.VMEM((LEAVES, COLS, LANES), F32),
            dma((13,)),
            dma((LEAVES,)),
            dma((2,)),
            dma((5,)),
            dma((5,)),
            dma((2,)),
            dma((2,)),
            dma,
            dma,
            dma,
            dma,
        ],
        compiler_params=pltpu.CompilerParams(
            collective_id=0, has_side_effects=True, vmem_limit_bytes=56 << 20
        ),
    )(
        right_sides,
        point_order.reshape(LEAVES, LANES),
        leaf_basis,
        transfer,
        coupling,
        far_list.T,
        far_count.reshape(1, ROWS - 1),
        coarse_transfer,
        coarse_coupling,
        coarse_list.T,
        coarse_count,
        near_block,
        near_list,
        near_count.reshape(1, LEAVES),
    )


def solution(mesh):
    return jax.shard_map(
        body,
        mesh=mesh,
        in_specs=(
            P("rhs", "leaf"),
            P("leaf"),
            P("leaf", None, None),
            P("leaf", None, None),
            P("leaf", None, None),
            P("leaf", None),
            P("leaf"),
            P(),
            P(),
            P(),
            P(),
            P("leaf", "rhs", None, None),
            P("leaf", "rhs"),
            P("leaf"),
        ),
        out_specs=P("rhs", "leaf"),
        check_vma=False,
    )
```

```python
import jax
import jax.numpy as jnp
from jax import lax
from jax.experimental import pallas as pl
from jax.experimental.pallas import tpu as pltpu
from jax.sharding import PartitionSpec as P

MESH = pl.DeviceIdType.MESH
F32 = jnp.float32
BF16 = jnp.bfloat16

DEVICES = 128
LEAVES = 16
RANK = 64
LANES = 128
COLS = 8
SLOTS = 14
FAR = 8
PAIRS = 15
ROWS = 2 * LEAVES
ZERO = 3 * ROWS
NEAR_ZERO = 3 * LEAVES
NEAR_STEP = 8
HALF = DEVICES // 2
QUARTER = DEVICES // 4


def dot_nt(left, right):
    return lax.dot_general(left, right, (((1,), (1,)), ((), ())), preferred_element_type=F32)


def dot_nn(left, right):
    return lax.dot_general(left, right, (((1,), (0,)), ((), ())), preferred_element_type=F32)


def wrap(value, size):
    return lax.rem(value + size, size)


def within(value, size):
    return (value >= 0) & (value < size)


def when(flag, do):
    if flag is None:
        do()
    else:
        pl.when(flag)(do)


def kernel(
    rs_h,
    order_h,
    basis_h,
    transfer_h,
    coupling_h,
    flist_h,
    fcount_h,
    ctr_h,
    ccp_h,
    clist_h,
    ccount_h,
    near_h,
    nlist_h,
    ncount_h,
    out_v,
    rs_v,
    order_v,
    basis_v,
    transfer_v,
    coupling_v,
    near_v,
    flist_v,
    fcount_v,
    nlist_v,
    ncount_v,
    ctr_v,
    ccp_v,
    clist_s,
    ccount_s,
    fid_v,
    nid_v,
    fid_s,
    nid_s,
    xs_v,
    us_v,
    xr_v,
    ur_v,
    cs_v,
    cr_v,
    xw_v,
    table_v,
    up_v,
    gu_v,
    reach_v,
    rise_v,
    fall_v,
    yown_v,
    ysend_v,
    yrecv_v,
    in_sem,
    near_sem,
    id_sem,
    xsend_sem,
    xrecv_sem,
    usend_sem,
    urecv_sem,
    csend_sem,
    crecv_sem,
    ysend_sem,
    yrecv_sem,
):
    me = lax.axis_index("leaf")
    core = lax.axis_index("rhs")
    other = 1 - core
    quad = lax.div(me, 4)
    in_quad = lax.rem(me, 4)
    duo = lax.div(me, 2)
    in_duo = lax.rem(me, 2)
    turn = 1 - 2 * in_duo
    duo_turn = 1 - 2 * lax.rem(duo, 2)
    quad_turn = 1 - 2 * lax.rem(quad, 2)
    quad_from = [wrap(quad + d, QUARTER) for d in (-2, 2, 3 * quad_turn)]
    duo_from = [wrap(duo + d, HALF) for d in (-2, 2, 3 * duo_turn)]
    groups = []
    for n, (send_by, get_by) in enumerate(((2, -2), (-2, 2), (0, 0))):
        for base, size, node, node_turn, nodes, place_in in (
            (0, 4, quad, quad_turn, QUARTER, in_quad),
            (12, 2, duo, duo_turn, HALF, in_duo),
            (18, 1, me, turn, DEVICES, 0),
        ):
            to = node + (send_by if n < 2 else 3 * node_turn)
            source = node + (get_by if n < 2 else 3 * node_turn)
            groups.append(
                (base + size * n, size, size * to, place_in, within(to, nodes), within(source, nodes))
            )
    left = me - 1
    right = me + 1
    has_left = left >= 0
    has_right = right < DEVICES
    point_sends = [
        (right, core, 0, has_right, 1),
        (left, core, 1, has_left, 0),
        (right, other, 2, has_right, 3),
        (left, other, 3, has_left, 2),
        (me, other, 4, None, 4),
    ]

    def fetch(source, target, sem):
        copy = pltpu.make_async_copy(source, target, sem)
        copy.start()
        return copy

    get_order = fetch(order_h, order_v, in_sem.at[0])
    get_rs = fetch(rs_h, rs_v, in_sem.at[1])
    get_basis = fetch(basis_h, basis_v, in_sem.at[2])
    get_transfer = fetch(transfer_h, transfer_v, in_sem.at[3])
    get_lists = [
        fetch(nlist_h, nlist_v, in_sem.at[4]),
        fetch(ncount_h, ncount_v, in_sem.at[5]),
        fetch(flist_h, flist_v, in_sem.at[6]),
        fetch(fcount_h, fcount_v, in_sem.at[7]),
    ]
    get_coarse = [fetch(clist_h, clist_s, in_sem.at[8]), fetch(ccount_h, ccount_s, in_sem.at[9])]
    def greet(device_at, device_core):
        pl.semaphore_signal(
            pltpu.get_barrier_semaphore(),
            inc=1,
            device_id=(device_at, device_core),
            device_id_type=MESH,
        )

    peers = 1
    for device_at, device_core, _, there, _ in point_sends:
        when(there, lambda: greet(device_at, device_core))
        if there is not None:
            peers = peers + jnp.where(there, 1, 0)
    for _, size, to, _, there, source_there in groups:

        def greet_all():
            for i in range(size):
                greet(to + i, core)

        when(there, greet_all)
        peers = peers + jnp.where(source_there, size, 0)
    for j in range(4):
        fetch(near_h.at[j], near_v.at[j], near_sem.at[j])
    for n in range(3):
        fetch(ctr_h.at[pl.ds(2 * quad_from[n], 2)], ctr_v.at[pl.ds(2 * n, 2)], in_sem.at[10])
        fetch(ctr_h.at[pl.ds(duo_from[n], 1)], ctr_v.at[pl.ds(6 + n, 1)], in_sem.at[10])
        fetch(ctr_h.at[pl.ds(HALF + quad_from[n], 1)], ctr_v.at[pl.ds(9 + n, 1)], in_sem.at[10])
    fetch(ctr_h.at[pl.ds(duo, 1)], ctr_v.at[pl.ds(12, 1)], in_sem.at[10])
    fetch(ctr_h.at[pl.ds(HALF + quad, 1)], ctr_v.at[pl.ds(13, 1)], in_sem.at[10])
    fetch(ccp_h.at[pl.ds(duo, 1)], ccp_v.at[pl.ds(0, 1)], in_sem.at[11])
    fetch(ccp_h.at[pl.ds(HALF + quad, 1)], ccp_v.at[pl.ds(1, 1)], in_sem.at[11])
    for j in range(4, LEAVES):
        fetch(near_h.at[j], near_v.at[j], near_sem.at[j])
    get_coupling = fetch(coupling_h, coupling_v, in_sem.at[12])

    low = lax.broadcasted_iota(jnp.int32, (COLS, LANES), 1) < RANK
    low16 = lax.broadcasted_iota(jnp.int32, (2 * COLS, LANES), 1) < RANK
    top16 = lax.broadcasted_iota(jnp.int32, (2 * COLS, LANES), 0) < COLS
    diagonal = low16 == top16

    def both(first, second):
        return jnp.concatenate([first, second], axis=0)

    def meet(first, second):
        return jnp.where(low, first, second)

    def flip(pair):
        return pltpu.roll(pair, RANK, 1)

    def join(product):
        return jnp.where(low, product[:COLS], product[COLS:])

    get_order.wait()
    get_rs.wait()
    place = order_v[...] - me * (LEAVES * LANES)
    for j in range(0, LEAVES, 2):
        blocks = []
        for i in (j, j + 1):
            here = jnp.broadcast_to(place[i : i + 1], (COLS, LANES))
            chunk = here // LANES
            lane = here % LANES
            block = jnp.take_along_axis(rs_v[:, 0:LANES], lane, axis=1, mode="promise_in_bounds")
            for c in range(1, LEAVES):
                found = jnp.take_along_axis(
                    rs_v[:, c * LANES : (c + 1) * LANES], lane, axis=1, mode="promise_in_bounds"
                )
                block = jnp.where(chunk == c, found, block)
            blocks.append(block)
        xs_v[j // 2] = both(*blocks).astype(BF16)

    get_basis.wait()
    get_transfer.wait()
    own = ROWS
    for p in range(LEAVES // 2):
        matrices = basis_v[2 * p : 2 * p + 2].reshape(LANES, LANES)
        pair = join(dot_nt(xs_v[p], matrices))
        up_v[p] = pair
        table_v[own + 2 * p] = pair
        table_v[own + 2 * p + 1] = flip(pair)
    first = 0
    for width in (8, 4, 2):
        for p in range(width // 2):
            tile = both(up_v[first + 2 * p], up_v[first + 2 * p + 1]).astype(BF16)
            us_v[first // 2 + p] = tile
            row = first + 2 * p
            matrices = transfer_v[row : row + 2].reshape(LANES, LANES)
            pair = join(dot_nt(tile, matrices))
            at = first + width + p
            up_v[at] = pair
            table_v[own + 2 * at] = pair
            table_v[own + 2 * at + 1] = flip(pair)
        first += width
    last = both(up_v[14], jnp.zeros((COLS, LANES), F32)).astype(BF16)
    us_v[7] = last
    root = transfer_v[14]
    cs_v[...] = dot_nt(last, both(root, root))[:COLS].astype(BF16).astype(F32)
    for copy in get_lists:
        copy.wait()
    square = lax.broadcasted_iota(jnp.int32, (LEAVES, LEAVES), 0) == lax.broadcasted_iota(
        jnp.int32, (LEAVES, LEAVES), 1
    )
    counts = jnp.broadcast_to(ncount_v[...], (LEAVES, LEAVES))
    counts = jnp.sum(jnp.where(square, counts, 0), axis=1, keepdims=True)
    slot_at = lax.broadcasted_iota(jnp.int32, (LEAVES, SLOTS), 1) + core * SLOTS
    nid_v[...] = jnp.where(slot_at < counts, nlist_v[...] - (me - 1) * LEAVES, NEAR_ZERO)
    node = lax.broadcasted_iota(jnp.int32, (FAR, ROWS - 1), 1)
    slot_at = lax.broadcasted_iota(jnp.int32, (FAR, ROWS - 1), 0)
    entry = flist_v[...]
    row = jnp.zeros_like(entry)
    for height in range(4):
        width = LEAVES >> height
        start = ROWS - 2 * width
        side = entry // width - me + 1
        inside = (node >= start) & (node < start + width)
        row = jnp.where(inside, side * ROWS + start + entry % width, row)
    row = row + jnp.where(slot_at % 2 == 0, 0, 1 - 2 * (row % 2))
    step = entry - me
    root_row = jnp.where(step == -2, 0, jnp.where(step == 2, 1, 2))
    row = jnp.where(node == ROWS - 2, root_row, row)
    live = slot_at < fcount_v[...]
    fid_v[...] = jnp.where(live, row, jnp.where(node == ROWS - 2, 3, ZERO))
    put_near = fetch(nid_v, nid_s, id_sem.at[0])
    put_far = fetch(fid_v, fid_s, id_sem.at[1])
    zero = jnp.zeros((COLS, LANES), F32)
    table_v[ZERO] = zero
    xw_v[NEAR_ZERO] = jnp.zeros((2 * COLS, LANES), BF16)

    def remote(source, target, send_sem, recv_sem, device_at, device_core):
        return pltpu.make_async_remote_copy(
            src_ref=source,
            dst_ref=target,
            send_sem=send_sem,
            recv_sem=recv_sem,
            device_id=(device_at, device_core),
            device_id_type=MESH,
        )

    def send_points(slot, device_at, device_core):
        return remote(
            xs_v, xr_v.at[slot], xsend_sem.at[slot], xrecv_sem.at[slot], device_at, device_core
        )

    def send_side(slot, device_at):
        return remote(us_v, ur_v.at[slot], usend_sem.at[slot], urecv_sem.at[slot], device_at, core)

    pl.semaphore_wait(pltpu.get_barrier_semaphore(), peers)
    side_sends = ((0, right, has_right, 1), (1, left, has_left, 0))
    for slot, device_at, there, _ in side_sends:
        when(there, lambda: send_side(slot, device_at).start())
    for device_at, device_core, slot, there, _ in point_sends:
        when(there, lambda: send_points(slot, device_at, device_core).start())
    for k, (first, size, to, place_in, there, _) in enumerate(groups):

        def send_root():
            for i in range(size):
                target = cr_v.at[first + place_in]
                remote(cs_v, target, csend_sem.at[k], crecv_sem.at[k], to + i, core).start()

        when(there, send_root)
    put_near.wait()
    put_far.wait()

    def spread(pair, mask):
        return jnp.where(mask, both(pair, pair), 0.0).astype(BF16)

    low128 = lax.broadcasted_iota(jnp.int32, (LANES, LANES), 1) < RANK
    top128 = lax.broadcasted_iota(jnp.int32, (LANES, LANES), 0) < RANK
    diagonal128 = low128 == top128
    chains = {14: transfer_v[14].astype(F32)}
    for first, width in ((12, 2), (8, 4), (0, 8)):
        for p in range(width // 2):
            row = first + 2 * p
            matrices = transfer_v[row : row + 2].reshape(LANES, LANES)
            product = dot_nn(spread(chains[first + width + p], diagonal128), matrices)
            chains[row] = product[:RANK]
            chains[row + 1] = product[RANK:]
    for p in range(LEAVES // 2):
        matrices = basis_v[2 * p : 2 * p + 2].reshape(LANES, LANES)
        product = dot_nn(spread(chains[p], diagonal128), matrices).astype(BF16)
        reach_v[:, 2 * p * LANES : (2 * p + 1) * LANES] = product[:RANK]
        reach_v[:, (2 * p + 1) * LANES : (2 * p + 2) * LANES] = product[RANK:]
    pltpu.make_async_copy(ctr_h.at[pl.ds(0, 14)], ctr_v, in_sem.at[10]).wait()
    pltpu.make_async_copy(ccp_h.at[pl.ds(0, 2)], ccp_v, in_sem.at[11]).wait()
    for copy in get_coarse:
        copy.wait()
    for n in range(3):
        matrix = ctr_v[9 + n].astype(F32)
        product = dot_nn(
            spread(matrix, diagonal128), ctr_v[2 * n : 2 * n + 2].reshape(LANES, LANES)
        ).astype(BF16)
        rise_v[n, :, :LANES] = product[:RANK]
        rise_v[n, :, LANES:] = product[RANK:]
    duo_matrix = ctr_v[12].astype(F32)
    duo_matrix = jnp.where(in_duo == 0, duo_matrix, flip(duo_matrix)).astype(BF16)
    quad_matrix = ctr_v[13].astype(F32)
    quad_matrix = jnp.where(lax.rem(duo, 2) == 0, quad_matrix, flip(quad_matrix)).astype(BF16)
    fall_v[:RANK] = dot_nn(quad_matrix[:, :RANK], duo_matrix).astype(BF16)
    fall_v[RANK:] = duo_matrix

    def zero_side(slot):
        def fill():
            ur_v[slot] = jnp.zeros(ur_v.shape[1:], BF16)

        return fill

    for slot, device_at, there, source_slot in side_sends:
        pl.when(jnp.logical_not(there))(zero_side(source_slot))
        when(there, lambda: send_side(source_slot, device_at).wait_recv())
    for slot, base in ((0, 0), (1, 2 * ROWS)):
        for t in range(8):
            tile = ur_v[slot, t].astype(F32)
            for half in range(2):
                pair = tile[half * COLS : (half + 1) * COLS]
                table_v[base + 4 * t + 2 * half] = pair
                table_v[base + 4 * t + 2 * half + 1] = flip(pair)

    get_coupling.wait()

    for p in range(PAIRS):
        matrices = coupling_v[2 * p : 2 * p + 2].reshape(LANES, FAR * RANK)
        picked = []
        for node in (2 * p, 2 * p + 1):
            picked.append(
                jnp.concatenate(
                    [
                        meet(table_v[fid_s[2 * t, node]], table_v[fid_s[2 * t + 1, node]])
                        for t in range(FAR // 2)
                    ],
                    axis=1,
                )
            )
        gu_v[p] = join(dot_nt(both(*picked).astype(BF16), matrices))

    fields = {14: gu_v[14]}
    for first, width in ((12, 2), (8, 4), (0, 8)):
        for p in range(width // 2):
            row = first + 2 * p
            matrices = transfer_v[row : row + 2].reshape(LANES, LANES)
            down = dot_nn(spread(fields[first + width + p], diagonal), matrices)
            fields[row] = gu_v[row] + down[:COLS]
            fields[row + 1] = gu_v[row + 1] + down[COLS:]
    for p in range(LEAVES // 2):
        matrices = basis_v[2 * p : 2 * p + 2].reshape(LANES, LANES)
        far = dot_nn(spread(fields[p], diagonal), matrices)
        out_v[:, 2 * p * LANES : (2 * p + 1) * LANES] = far[:COLS]
        out_v[:, (2 * p + 1) * LANES : (2 * p + 2) * LANES] = far[COLS:]

    def zero_points(slot):
        def fill():
            xr_v[slot] = jnp.zeros(xr_v.shape[1:], BF16)

        return fill

    for device_at, device_core, slot, there, source_slot in point_sends:
        fill = zero_points(source_slot)
        if there is not None:
            pl.when(jnp.logical_not(there))(fill)
        when(there, lambda: send_points(source_slot, device_at, device_core).wait_recv())

    def arrange(base, mine, theirs):
        for p in range(LEAVES // 2):
            a = mine[p].astype(F32)
            b = theirs[p].astype(F32)
            xw_v[base + 2 * p] = both(a[:COLS], b[:COLS]).astype(BF16)
            xw_v[base + 2 * p + 1] = both(a[COLS:], b[COLS:]).astype(BF16)

    arrange(0, xr_v.at[0], xr_v.at[2])
    arrange(LEAVES, xs_v, xr_v.at[4])
    arrange(2 * LEAVES, xr_v.at[1], xr_v.at[3])

    for j in range(LEAVES):
        pltpu.make_async_copy(near_h.at[j], near_v.at[j], near_sem.at[j]).wait()

    def near_leaves(step, carry):
        for i in range(NEAR_STEP):
            j = step * NEAR_STEP + i
            points = jnp.concatenate([xw_v[nid_s[j, s]] for s in range(SLOTS)], axis=1)
            blocks = jnp.concatenate([near_v[j, s] for s in range(SLOTS)], axis=1)
            total = dot_nt(points, blocks)
            yown_v[j] = total[:COLS]
            ysend_v[j] = total[COLS:]
        return carry

    lax.fori_loop(0, LEAVES // NEAR_STEP, near_leaves, 0)
    send_near = remote(ysend_v, yrecv_v, ysend_sem, yrecv_sem, me, other)
    send_near.start()

    for k, (first, size, to, _, there, source_there) in enumerate(groups):
        arrived = cr_v.at[pl.ds(first, size)]

        def zero_group():
            arrived[...] = jnp.zeros((size, COLS, LANES), F32)

        pl.when(jnp.logical_not(source_there))(zero_group)
        group = remote(arrived, arrived, csend_sem.at[k], crecv_sem.at[k], me, other)
        when(source_there, group.wait_recv)
    for k in range(3):
        up_v[4 * k + 3] = zero
    for n in range(3):
        pairs = [meet(cr_v[4 * n + i], cr_v[4 * n + i + 1]) for i in (0, 2)]
        children = jnp.concatenate(pairs, axis=1)
        matrix = rise_v[n]
        up_v[n] = dot_nt(both(children, children).astype(BF16), both(matrix, matrix))[:COLS]
        pair = meet(cr_v[12 + 2 * n], cr_v[13 + 2 * n])
        matrix = ctr_v[6 + n]
        up_v[4 + n] = dot_nt(both(pair, pair).astype(BF16), both(matrix, matrix))[:COLS]
        up_v[8 + n] = cr_v[18 + n]

    def upper_rows(at, node_here, base):
        rows = []
        for s in range(3):
            step = clist_s[s, at] - node_here
            row = jnp.where(step == -2, 0, jnp.where(step == 2, 1, 2))
            rows.append(base + jnp.where(s < ccount_s[at], row, 3))
        return meet(up_v[rows[0]], up_v[rows[1]]), up_v[rows[2]]

    pair6, third6 = upper_rows(HALF + quad, quad, 0)
    pair5, third5 = upper_rows(duo, duo, 4)
    total = dot_nt(both(pair6, pair5).astype(BF16), both(ccp_v[1, :, :LANES], ccp_v[0, :, :LANES]))
    total += dot_nt(
        both(third6, third5)[:, :RANK].astype(BF16), both(ccp_v[1, :, LANES:], ccp_v[0, :, LANES:])
    )
    matrix = coupling_v[ROWS - 2]
    pair = meet(up_v[8 + fid_s[0, ROWS - 2]], up_v[8 + fid_s[1, ROWS - 2]])
    third = up_v[8 + fid_s[2, ROWS - 2]]
    field = dot_nt(both(pair, pair).astype(BF16), matrix[:, :LANES])
    field += dot_nt(both(third, third)[:, :RANK].astype(BF16), matrix[:, LANES : LANES + RANK])
    above = join(total)
    field += dot_nn(both(above, above).astype(BF16), fall_v[...])[:, :RANK]
    far = dot_nn(field.astype(BF16), reach_v[...])[:COLS]

    for device_at, device_core, slot, there, _ in point_sends:
        when(there, lambda: send_points(slot, device_at, device_core).wait_send())
    for slot, device_at, there, _ in side_sends:
        when(there, lambda: send_side(slot, device_at).wait_send())
    for k, (first, size, to, _, there, _) in enumerate(groups):
        left_group = cr_v.at[pl.ds(first, size)]
        group = remote(left_group, left_group, csend_sem.at[k], crecv_sem.at[k], me, other)
        when(there, group.wait_send)
    send_near.wait()
    for j in range(LEAVES):
        columns = slice(j * LANES, (j + 1) * LANES)
        out_v[:, columns] += far[:, columns] + yown_v[j] + yrecv_v[j]


def body(
    right_sides,
    point_order,
    leaf_basis,
    transfer,
    coupling,
    far_list,
    far_count,
    coarse_transfer,
    coarse_coupling,
    coarse_list,
    coarse_count,
    near_block,
    near_list,
    near_count,
):
    tile = (2 * COLS, LANES)
    dma = pltpu.SemaphoreType.DMA
    return pl.pallas_call(
        kernel,
        out_shape=pltpu.VMEM((COLS, LEAVES * LANES), F32),
        in_specs=[pl.BlockSpec(memory_space=pltpu.HBM)] * 14,
        out_specs=pl.BlockSpec(memory_space=pltpu.VMEM),
        scratch_shapes=[
            pltpu.VMEM((COLS, LEAVES * LANES), F32),
            pltpu.VMEM((LEAVES, LANES), jnp.int32),
            pltpu.VMEM((LEAVES, RANK, LANES), BF16),
            pltpu.VMEM((LEAVES - 1, RANK, LANES), BF16),
            pltpu.VMEM((ROWS - 1, RANK, FAR * RANK), BF16),
            pltpu.VMEM((LEAVES, SLOTS, LANES, LANES), BF16),
            pltpu.VMEM((FAR, ROWS - 1), jnp.int32),
            pltpu.VMEM((1, ROWS - 1), jnp.int32),
            pltpu.VMEM((LEAVES, SLOTS), jnp.int32),
            pltpu.VMEM((1, LEAVES), jnp.int32),
            pltpu.VMEM((14, RANK, LANES), BF16),
            pltpu.VMEM((2, RANK, 3 * RANK), BF16),
            pltpu.SMEM((3, 96), jnp.int32),
            pltpu.SMEM((96,), jnp.int32),
            pltpu.VMEM((FAR, ROWS - 1), jnp.int32),
            pltpu.VMEM((LEAVES, SLOTS), jnp.int32),
            pltpu.SMEM((FAR, ROWS - 1), jnp.int32),
            pltpu.SMEM((LEAVES, SLOTS), jnp.int32),
            pltpu.VMEM((LEAVES // 2,) + tile, BF16),
            pltpu.VMEM((LEAVES // 2,) + tile, BF16),
            pltpu.VMEM((5, LEAVES // 2) + tile, BF16),
            pltpu.VMEM((2, LEAVES // 2) + tile, BF16),
            pltpu.VMEM((COLS, LANES), F32),
            pltpu.VMEM((21, COLS, LANES), F32),
            pltpu.VMEM((3 * LEAVES + 1,) + tile, BF16),
            pltpu.VMEM((ZERO + 1, COLS, LANES), F32),
            pltpu.VMEM((PAIRS, COLS, LANES), F32),
            pltpu.VMEM((PAIRS, COLS, LANES), F32),
            pltpu.VMEM((RANK, LEAVES * LANES), BF16),
            pltpu.VMEM((3, RANK, 2 * LANES), BF16),
            pltpu.VMEM((LANES, LANES), BF16),
            pltpu.VMEM((LEAVES, COLS, LANES), F32),
            pltpu.VMEM((LEAVES, COLS, LANES), F32),
            pltpu.VMEM((LEAVES, COLS, LANES), F32),
            dma((13,)),
            dma((LEAVES,)),
            dma((2,)),
            dma((5,)),
            dma((5,)),
            dma((2,)),
            dma((2,)),
            dma((9,)),
            dma((9,)),
            dma,
            dma,
        ],
        compiler_params=pltpu.CompilerParams(
            collective_id=0, has_side_effects=True, vmem_limit_bytes=56 << 20
        ),
    )(
        right_sides,
        point_order.reshape(LEAVES, LANES),
        leaf_basis,
        transfer,
        coupling,
        far_list.T,
        far_count.reshape(1, ROWS - 1),
        coarse_transfer,
        coarse_coupling,
        coarse_list.T,
        coarse_count,
        near_block,
        near_list,
        near_count.reshape(1, LEAVES),
    )


def solution(mesh):
    return jax.shard_map(
        body,
        mesh=mesh,
        in_specs=(
            P("rhs", "leaf"),
            P("leaf"),
            P("leaf", None, None),
            P("leaf", None, None),
            P("leaf", None, None),
            P("leaf", None),
            P("leaf"),
            P(),
            P(),
            P(),
            P(),
            P("leaf", "rhs", None, None),
            P("leaf", "rhs"),
            P("leaf"),
        ),
        out_specs=P("rhs", "leaf"),
        check_vma=False,
    )
```

```python
import jax
import jax.numpy as jnp
from jax import lax
from jax.experimental import pallas as pl
from jax.experimental.pallas import tpu as pltpu
from jax.sharding import PartitionSpec as P

MESH = pl.DeviceIdType.MESH
F32 = jnp.float32
BF16 = jnp.bfloat16

DEVICES = 128
LEAVES = 16
RANK = 64
LANES = 128
COLS = 8
SLOTS = 14
FAR = 8
PAIRS = 15
ROWS = 2 * LEAVES
ZERO = 3 * ROWS
NEAR_ZERO = 3 * LEAVES
NEAR_STEP = 8
HALF = DEVICES // 2
QUARTER = DEVICES // 4


def dot_nt(left, right):
    return lax.dot_general(left, right, (((1,), (1,)), ((), ())), preferred_element_type=F32)


def dot_nn(left, right):
    return lax.dot_general(left, right, (((1,), (0,)), ((), ())), preferred_element_type=F32)


def wrap(value, size):
    return lax.rem(value + size, size)


def within(value, size):
    return (value >= 0) & (value < size)


def when(flag, do):
    if flag is None:
        do()
    else:
        pl.when(flag)(do)


def kernel(
    rs_h,
    order_h,
    basis_h,
    transfer_h,
    coupling_h,
    flist_h,
    fcount_h,
    ctr_h,
    ccp_h,
    clist_h,
    ccount_h,
    near_h,
    nlist_h,
    ncount_h,
    out_v,
    rs_v,
    order_v,
    basis_v,
    transfer_v,
    coupling_v,
    near_v,
    flist_v,
    fcount_v,
    nlist_v,
    ncount_v,
    ctr_v,
    ccp_v,
    clist_s,
    ccount_s,
    fid_v,
    nid_v,
    fid_s,
    nid_s,
    xs_v,
    us_v,
    xr_v,
    ur_v,
    cs_v,
    cr_v,
    xw_v,
    table_v,
    up_v,
    gu_v,
    reach_v,
    rise_v,
    fall_v,
    yown_v,
    ysend_v,
    yrecv_v,
    in_sem,
    near_sem,
    id_sem,
    xsend_sem,
    xrecv_sem,
    usend_sem,
    urecv_sem,
    csend_sem,
    crecv_sem,
    ysend_sem,
    yrecv_sem,
    near_ready,
    far_ready,
):
    me = lax.axis_index("leaf")
    core = lax.axis_index("rhs")
    other = 1 - core
    quad = lax.div(me, 4)
    in_quad = lax.rem(me, 4)
    duo = lax.div(me, 2)
    in_duo = lax.rem(me, 2)
    turn = 1 - 2 * in_duo
    duo_turn = 1 - 2 * lax.rem(duo, 2)
    quad_turn = 1 - 2 * lax.rem(quad, 2)
    quad_from = [wrap(quad + d, QUARTER) for d in (-2, 2, 3 * quad_turn)]
    duo_from = [wrap(duo + d, HALF) for d in (-2, 2, 3 * duo_turn)]
    groups = []
    for n, (send_by, get_by) in enumerate(((2, -2), (-2, 2), (0, 0))):
        for base, size, node, node_turn, nodes, place_in in (
            (0, 4, quad, quad_turn, QUARTER, in_quad),
            (12, 2, duo, duo_turn, HALF, in_duo),
            (18, 1, me, turn, DEVICES, 0),
        ):
            to = node + (send_by if n < 2 else 3 * node_turn)
            source = node + (get_by if n < 2 else 3 * node_turn)
            groups.append(
                (base + size * n, size, size * to, place_in, within(to, nodes), within(source, nodes))
            )
    left = me - 1
    right = me + 1
    has_left = left >= 0
    has_right = right < DEVICES
    point_sends = [
        (right, core, 0, has_right, 1),
        (left, core, 1, has_left, 0),
        (right, other, 2, has_right, 3),
        (left, other, 3, has_left, 2),
        (me, other, 4, None, 4),
    ]

    def fetch(source, target, sem):
        copy = pltpu.make_async_copy(source, target, sem)
        copy.start()
        return copy

    get_order = fetch(order_h, order_v, in_sem.at[0])
    get_rs = fetch(rs_h, rs_v, in_sem.at[1])
    get_basis = fetch(basis_h, basis_v, in_sem.at[2])
    get_transfer = fetch(transfer_h, transfer_v, in_sem.at[3])
    get_lists = [
        fetch(nlist_h, nlist_v, in_sem.at[4]),
        fetch(ncount_h, ncount_v, in_sem.at[5]),
        fetch(flist_h, flist_v, in_sem.at[6]),
        fetch(fcount_h, fcount_v, in_sem.at[7]),
    ]
    get_coarse = [fetch(clist_h, clist_s, in_sem.at[8]), fetch(ccount_h, ccount_s, in_sem.at[9])]
    def greet(device_at, device_core):
        pl.semaphore_signal(
            pltpu.get_barrier_semaphore(),
            inc=1,
            device_id=(device_at, device_core),
            device_id_type=MESH,
        )

    when(has_right, lambda: greet(right, 1))
    when(has_left, lambda: greet(left, 1))
    when(core == 0, lambda: greet(me, 1))
    near_peers = 1 + 2 * jnp.where(has_right, 1, 0) + 2 * jnp.where(has_left, 1, 0)
    far_peers = 0
    for _, size, to, _, there, source_there in groups:

        def greet_all():
            for i in range(size):
                greet(to + i, 0)

        when(there, greet_all)
        far_peers = far_peers + 2 * jnp.where(there, size, 0)
    for j in range(4):
        fetch(near_h.at[j], near_v.at[j], near_sem.at[j])
    for n in range(3):
        fetch(ctr_h.at[pl.ds(2 * quad_from[n], 2)], ctr_v.at[pl.ds(2 * n, 2)], in_sem.at[10])
        fetch(ctr_h.at[pl.ds(duo_from[n], 1)], ctr_v.at[pl.ds(6 + n, 1)], in_sem.at[10])
        fetch(ctr_h.at[pl.ds(HALF + quad_from[n], 1)], ctr_v.at[pl.ds(9 + n, 1)], in_sem.at[10])
    fetch(ctr_h.at[pl.ds(duo, 1)], ctr_v.at[pl.ds(12, 1)], in_sem.at[10])
    fetch(ctr_h.at[pl.ds(HALF + quad, 1)], ctr_v.at[pl.ds(13, 1)], in_sem.at[10])
    fetch(ccp_h.at[pl.ds(duo, 1)], ccp_v.at[pl.ds(0, 1)], in_sem.at[11])
    fetch(ccp_h.at[pl.ds(HALF + quad, 1)], ccp_v.at[pl.ds(1, 1)], in_sem.at[11])
    for j in range(4, LEAVES):
        fetch(near_h.at[j], near_v.at[j], near_sem.at[j])
    get_coupling = fetch(coupling_h, coupling_v, in_sem.at[12])

    low = lax.broadcasted_iota(jnp.int32, (COLS, LANES), 1) < RANK
    low16 = lax.broadcasted_iota(jnp.int32, (2 * COLS, LANES), 1) < RANK
    top16 = lax.broadcasted_iota(jnp.int32, (2 * COLS, LANES), 0) < COLS
    diagonal = low16 == top16

    def both(first, second):
        return jnp.concatenate([first, second], axis=0)

    def meet(first, second):
        return jnp.where(low, first, second)

    def flip(pair):
        return pltpu.roll(pair, RANK, 1)

    def join(product):
        return jnp.where(low, product[:COLS], product[COLS:])

    get_order.wait()
    get_rs.wait()
    place = order_v[...] - me * (LEAVES * LANES)
    for j in range(0, LEAVES, 2):
        blocks = []
        for i in (j, j + 1):
            here = jnp.broadcast_to(place[i : i + 1], (COLS, LANES))
            chunk = here // LANES
            lane = here % LANES
            block = jnp.take_along_axis(rs_v[:, 0:LANES], lane, axis=1, mode="promise_in_bounds")
            for c in range(1, LEAVES):
                found = jnp.take_along_axis(
                    rs_v[:, c * LANES : (c + 1) * LANES], lane, axis=1, mode="promise_in_bounds"
                )
                block = jnp.where(chunk == c, found, block)
            blocks.append(block)
        xs_v[j // 2] = both(*blocks).astype(BF16)

    def remote(source, target, send_sem, recv_sem, device_at, device_core):
        return pltpu.make_async_remote_copy(
            src_ref=source,
            dst_ref=target,
            send_sem=send_sem,
            recv_sem=recv_sem,
            device_id=(device_at, device_core),
            device_id_type=MESH,
        )

    def send_points(slot, device_at, device_core):
        return remote(
            xs_v, xr_v.at[slot], xsend_sem.at[slot], xrecv_sem.at[slot], device_at, device_core
        )

    def send_side(slot, device_at):
        return remote(us_v, ur_v.at[slot], usend_sem.at[slot], urecv_sem.at[slot], device_at, core)

    def tell(sem):
        pl.semaphore_signal(sem, inc=1, device_id=(me, other), device_id_type=MESH)

    def near_gate():
        pl.semaphore_wait(pltpu.get_barrier_semaphore(), near_peers)
        tell(near_ready)

    def far_gate():
        pl.semaphore_wait(pltpu.get_barrier_semaphore(), far_peers)
        tell(far_ready)

    when(core == 1, near_gate)
    when(core == 0, lambda: pl.semaphore_wait(near_ready, 1))
    for device_at, device_core, slot, there, _ in point_sends:
        when(there, lambda: send_points(slot, device_at, device_core).start())

    get_basis.wait()
    get_transfer.wait()
    own = ROWS
    for p in range(LEAVES // 2):
        matrices = basis_v[2 * p : 2 * p + 2].reshape(LANES, LANES)
        pair = join(dot_nt(xs_v[p], matrices))
        up_v[p] = pair
        table_v[own + 2 * p] = pair
        table_v[own + 2 * p + 1] = flip(pair)
    first = 0
    for width in (8, 4, 2):
        for p in range(width // 2):
            tile = both(up_v[first + 2 * p], up_v[first + 2 * p + 1]).astype(BF16)
            us_v[first // 2 + p] = tile
            row = first + 2 * p
            matrices = transfer_v[row : row + 2].reshape(LANES, LANES)
            pair = join(dot_nt(tile, matrices))
            at = first + width + p
            up_v[at] = pair
            table_v[own + 2 * at] = pair
            table_v[own + 2 * at + 1] = flip(pair)
        first += width
    last = both(up_v[14], jnp.zeros((COLS, LANES), F32)).astype(BF16)
    us_v[7] = last
    side_sends = ((0, right, has_right, 1), (1, left, has_left, 0))
    for slot, device_at, there, _ in side_sends:
        when(there, lambda: send_side(slot, device_at).start())
    root = transfer_v[14]
    cs_v[...] = dot_nt(last, both(root, root))[:COLS].astype(BF16).astype(F32)
    for copy in get_lists:
        copy.wait()
    square = lax.broadcasted_iota(jnp.int32, (LEAVES, LEAVES), 0) == lax.broadcasted_iota(
        jnp.int32, (LEAVES, LEAVES), 1
    )
    counts = jnp.broadcast_to(ncount_v[...], (LEAVES, LEAVES))
    counts = jnp.sum(jnp.where(square, counts, 0), axis=1, keepdims=True)
    slot_at = lax.broadcasted_iota(jnp.int32, (LEAVES, SLOTS), 1) + core * SLOTS
    nid_v[...] = jnp.where(slot_at < counts, nlist_v[...] - (me - 1) * LEAVES, NEAR_ZERO)
    node = lax.broadcasted_iota(jnp.int32, (FAR, ROWS - 1), 1)
    slot_at = lax.broadcasted_iota(jnp.int32, (FAR, ROWS - 1), 0)
    entry = flist_v[...]
    row = jnp.zeros_like(entry)
    for height in range(4):
        width = LEAVES >> height
        start = ROWS - 2 * width
        side = entry // width - me + 1
        inside = (node >= start) & (node < start + width)
        row = jnp.where(inside, side * ROWS + start + entry % width, row)
    row = row + jnp.where(slot_at % 2 == 0, 0, 1 - 2 * (row % 2))
    step = entry - me
    root_row = jnp.where(step == -2, 0, jnp.where(step == 2, 1, 2))
    row = jnp.where(node == ROWS - 2, root_row, row)
    live = slot_at < fcount_v[...]
    fid_v[...] = jnp.where(live, row, jnp.where(node == ROWS - 2, 3, ZERO))
    put_near = fetch(nid_v, nid_s, id_sem.at[0])
    put_far = fetch(fid_v, fid_s, id_sem.at[1])
    zero = jnp.zeros((COLS, LANES), F32)
    table_v[ZERO] = zero
    xw_v[NEAR_ZERO] = jnp.zeros((2 * COLS, LANES), BF16)

    put_near.wait()
    put_far.wait()

    def spread(pair, mask):
        return jnp.where(mask, both(pair, pair), 0.0).astype(BF16)

    low128 = lax.broadcasted_iota(jnp.int32, (LANES, LANES), 1) < RANK
    top128 = lax.broadcasted_iota(jnp.int32, (LANES, LANES), 0) < RANK
    diagonal128 = low128 == top128
    chains = {14: transfer_v[14].astype(F32)}
    for first, width in ((12, 2), (8, 4), (0, 8)):
        for p in range(width // 2):
            row = first + 2 * p
            matrices = transfer_v[row : row + 2].reshape(LANES, LANES)
            product = dot_nn(spread(chains[first + width + p], diagonal128), matrices)
            chains[row] = product[:RANK]
            chains[row + 1] = product[RANK:]
    for p in range(LEAVES // 2):
        matrices = basis_v[2 * p : 2 * p + 2].reshape(LANES, LANES)
        product = dot_nn(spread(chains[p], diagonal128), matrices).astype(BF16)
        reach_v[:, 2 * p * LANES : (2 * p + 1) * LANES] = product[:RANK]
        reach_v[:, (2 * p + 1) * LANES : (2 * p + 2) * LANES] = product[RANK:]
    pltpu.make_async_copy(ctr_h.at[pl.ds(0, 14)], ctr_v, in_sem.at[10]).wait()
    pltpu.make_async_copy(ccp_h.at[pl.ds(0, 2)], ccp_v, in_sem.at[11]).wait()
    for copy in get_coarse:
        copy.wait()
    for n in range(3):
        matrix = ctr_v[9 + n].astype(F32)
        product = dot_nn(
            spread(matrix, diagonal128), ctr_v[2 * n : 2 * n + 2].reshape(LANES, LANES)
        ).astype(BF16)
        rise_v[n, :, :LANES] = product[:RANK]
        rise_v[n, :, LANES:] = product[RANK:]
    duo_matrix = ctr_v[12].astype(F32)
    duo_matrix = jnp.where(in_duo == 0, duo_matrix, flip(duo_matrix)).astype(BF16)
    quad_matrix = ctr_v[13].astype(F32)
    quad_matrix = jnp.where(lax.rem(duo, 2) == 0, quad_matrix, flip(quad_matrix)).astype(BF16)
    fall_v[:RANK] = dot_nn(quad_matrix[:, :RANK], duo_matrix).astype(BF16)
    fall_v[RANK:] = duo_matrix

    when(core == 0, far_gate)
    when(core == 1, lambda: pl.semaphore_wait(far_ready, 1))
    for k, (first, size, to, place_in, there, _) in enumerate(groups):

        def send_root():
            for i in range(size):
                target = cr_v.at[first + place_in]
                remote(cs_v, target, csend_sem.at[k], crecv_sem.at[k], to + i, core).start()

        when(there, send_root)

    def zero_points(slot):
        def fill():
            xr_v[slot] = jnp.zeros(xr_v.shape[1:], BF16)

        return fill

    for device_at, device_core, slot, there, source_slot in point_sends:
        fill = zero_points(source_slot)
        if there is not None:
            pl.when(jnp.logical_not(there))(fill)
        when(there, lambda: send_points(source_slot, device_at, device_core).wait_recv())

    def arrange(base, mine, theirs):
        for p in range(LEAVES // 2):
            a = mine[p].astype(F32)
            b = theirs[p].astype(F32)
            xw_v[base + 2 * p] = both(a[:COLS], b[:COLS]).astype(BF16)
            xw_v[base + 2 * p + 1] = both(a[COLS:], b[COLS:]).astype(BF16)

    arrange(0, xr_v.at[0], xr_v.at[2])
    arrange(LEAVES, xs_v, xr_v.at[4])
    arrange(2 * LEAVES, xr_v.at[1], xr_v.at[3])

    for j in range(LEAVES):
        pltpu.make_async_copy(near_h.at[j], near_v.at[j], near_sem.at[j]).wait()

    def near_leaves(step, carry):
        for i in range(NEAR_STEP):
            j = step * NEAR_STEP + i
            points = jnp.concatenate([xw_v[nid_s[j, s]] for s in range(SLOTS)], axis=1)
            blocks = jnp.concatenate([near_v[j, s] for s in range(SLOTS)], axis=1)
            total = dot_nt(points, blocks)
            yown_v[j] = total[:COLS]
            ysend_v[j] = total[COLS:]
        return carry

    lax.fori_loop(0, LEAVES // NEAR_STEP, near_leaves, 0)
    send_near = remote(ysend_v, yrecv_v, ysend_sem, yrecv_sem, me, other)
    send_near.start()

    def zero_side(slot):
        def fill():
            ur_v[slot] = jnp.zeros(ur_v.shape[1:], BF16)

        return fill

    for slot, device_at, there, source_slot in side_sends:
        pl.when(jnp.logical_not(there))(zero_side(source_slot))
        when(there, lambda: send_side(source_slot, device_at).wait_recv())
    for slot, base in ((0, 0), (1, 2 * ROWS)):
        for t in range(8):
            tile = ur_v[slot, t].astype(F32)
            for half in range(2):
                pair = tile[half * COLS : (half + 1) * COLS]
                table_v[base + 4 * t + 2 * half] = pair
                table_v[base + 4 * t + 2 * half + 1] = flip(pair)

    get_coupling.wait()

    for p in range(PAIRS):
        matrices = coupling_v[2 * p : 2 * p + 2].reshape(LANES, FAR * RANK)
        picked = []
        for node in (2 * p, 2 * p + 1):
            picked.append(
                jnp.concatenate(
                    [
                        meet(table_v[fid_s[2 * t, node]], table_v[fid_s[2 * t + 1, node]])
                        for t in range(FAR // 2)
                    ],
                    axis=1,
                )
            )
        gu_v[p] = join(dot_nt(both(*picked).astype(BF16), matrices))

    fields = {14: gu_v[14]}
    for first, width in ((12, 2), (8, 4), (0, 8)):
        for p in range(width // 2):
            row = first + 2 * p
            matrices = transfer_v[row : row + 2].reshape(LANES, LANES)
            down = dot_nn(spread(fields[first + width + p], diagonal), matrices)
            fields[row] = gu_v[row] + down[:COLS]
            fields[row + 1] = gu_v[row + 1] + down[COLS:]
    for p in range(LEAVES // 2):
        matrices = basis_v[2 * p : 2 * p + 2].reshape(LANES, LANES)
        far = dot_nn(spread(fields[p], diagonal), matrices)
        out_v[:, 2 * p * LANES : (2 * p + 1) * LANES] = far[:COLS]
        out_v[:, (2 * p + 1) * LANES : (2 * p + 2) * LANES] = far[COLS:]

    for k, (first, size, to, _, there, source_there) in enumerate(groups):
        arrived = cr_v.at[pl.ds(first, size)]

        def zero_group():
            arrived[...] = jnp.zeros((size, COLS, LANES), F32)

        pl.when(jnp.logical_not(source_there))(zero_group)
        group = remote(arrived, arrived, csend_sem.at[k], crecv_sem.at[k], me, other)
        when(source_there, group.wait_recv)
    for k in range(3):
        up_v[4 * k + 3] = zero
    for n in range(3):
        pairs = [meet(cr_v[4 * n + i], cr_v[4 * n + i + 1]) for i in (0, 2)]
        children = jnp.concatenate(pairs, axis=1)
        matrix = rise_v[n]
        up_v[n] = dot_nt(both(children, children).astype(BF16), both(matrix, matrix))[:COLS]
        pair = meet(cr_v[12 + 2 * n], cr_v[13 + 2 * n])
        matrix = ctr_v[6 + n]
        up_v[4 + n] = dot_nt(both(pair, pair).astype(BF16), both(matrix, matrix))[:COLS]
        up_v[8 + n] = cr_v[18 + n]

    def upper_rows(at, node_here, base):
        rows = []
        for s in range(3):
            step = clist_s[s, at] - node_here
            row = jnp.where(step == -2, 0, jnp.where(step == 2, 1, 2))
            rows.append(base + jnp.where(s < ccount_s[at], row, 3))
        return meet(up_v[rows[0]], up_v[rows[1]]), up_v[rows[2]]

    pair6, third6 = upper_rows(HALF + quad, quad, 0)
    pair5, third5 = upper_rows(duo, duo, 4)
    total = dot_nt(both(pair6, pair5).astype(BF16), both(ccp_v[1, :, :LANES], ccp_v[0, :, :LANES]))
    total += dot_nt(
        both(third6, third5)[:, :RANK].astype(BF16), both(ccp_v[1, :, LANES:], ccp_v[0, :, LANES:])
    )
    matrix = coupling_v[ROWS - 2]
    pair = meet(up_v[8 + fid_s[0, ROWS - 2]], up_v[8 + fid_s[1, ROWS - 2]])
    third = up_v[8 + fid_s[2, ROWS - 2]]
    field = dot_nt(both(pair, pair).astype(BF16), matrix[:, :LANES])
    field += dot_nt(both(third, third)[:, :RANK].astype(BF16), matrix[:, LANES : LANES + RANK])
    above = join(total)
    field += dot_nn(both(above, above).astype(BF16), fall_v[...])[:, :RANK]
    far = dot_nn(field.astype(BF16), reach_v[...])[:COLS]

    for device_at, device_core, slot, there, _ in point_sends:
        when(there, lambda: send_points(slot, device_at, device_core).wait_send())
    for slot, device_at, there, _ in side_sends:
        when(there, lambda: send_side(slot, device_at).wait_send())
    for k, (first, size, to, _, there, _) in enumerate(groups):
        left_group = cr_v.at[pl.ds(first, size)]
        group = remote(left_group, left_group, csend_sem.at[k], crecv_sem.at[k], me, other)
        when(there, group.wait_send)
    send_near.wait()
    for j in range(LEAVES):
        columns = slice(j * LANES, (j + 1) * LANES)
        out_v[:, columns] += far[:, columns] + yown_v[j] + yrecv_v[j]


def body(
    right_sides,
    point_order,
    leaf_basis,
    transfer,
    coupling,
    far_list,
    far_count,
    coarse_transfer,
    coarse_coupling,
    coarse_list,
    coarse_count,
    near_block,
    near_list,
    near_count,
):
    tile = (2 * COLS, LANES)
    dma = pltpu.SemaphoreType.DMA
    return pl.pallas_call(
        kernel,
        out_shape=pltpu.VMEM((COLS, LEAVES * LANES), F32),
        in_specs=[pl.BlockSpec(memory_space=pltpu.HBM)] * 14,
        out_specs=pl.BlockSpec(memory_space=pltpu.VMEM),
        scratch_shapes=[
            pltpu.VMEM((COLS, LEAVES * LANES), F32),
            pltpu.VMEM((LEAVES, LANES), jnp.int32),
            pltpu.VMEM((LEAVES, RANK, LANES), BF16),
            pltpu.VMEM((LEAVES - 1, RANK, LANES), BF16),
            pltpu.VMEM((ROWS - 1, RANK, FAR * RANK), BF16),
            pltpu.VMEM((LEAVES, SLOTS, LANES, LANES), BF16),
            pltpu.VMEM((FAR, ROWS - 1), jnp.int32),
            pltpu.VMEM((1, ROWS - 1), jnp.int32),
            pltpu.VMEM((LEAVES, SLOTS), jnp.int32),
            pltpu.VMEM((1, LEAVES), jnp.int32),
            pltpu.VMEM((14, RANK, LANES), BF16),
            pltpu.VMEM((2, RANK, 3 * RANK), BF16),
            pltpu.SMEM((3, 96), jnp.int32),
            pltpu.SMEM((96,), jnp.int32),
            pltpu.VMEM((FAR, ROWS - 1), jnp.int32),
            pltpu.VMEM((LEAVES, SLOTS), jnp.int32),
            pltpu.SMEM((FAR, ROWS - 1), jnp.int32),
            pltpu.SMEM((LEAVES, SLOTS), jnp.int32),
            pltpu.VMEM((LEAVES // 2,) + tile, BF16),
            pltpu.VMEM((LEAVES // 2,) + tile, BF16),
            pltpu.VMEM((5, LEAVES // 2) + tile, BF16),
            pltpu.VMEM((2, LEAVES // 2) + tile, BF16),
            pltpu.VMEM((COLS, LANES), F32),
            pltpu.VMEM((21, COLS, LANES), F32),
            pltpu.VMEM((3 * LEAVES + 1,) + tile, BF16),
            pltpu.VMEM((ZERO + 1, COLS, LANES), F32),
            pltpu.VMEM((PAIRS, COLS, LANES), F32),
            pltpu.VMEM((PAIRS, COLS, LANES), F32),
            pltpu.VMEM((RANK, LEAVES * LANES), BF16),
            pltpu.VMEM((3, RANK, 2 * LANES), BF16),
            pltpu.VMEM((LANES, LANES), BF16),
            pltpu.VMEM((LEAVES, COLS, LANES), F32),
            pltpu.VMEM((LEAVES, COLS, LANES), F32),
            pltpu.VMEM((LEAVES, COLS, LANES), F32),
            dma((13,)),
            dma((LEAVES,)),
            dma((2,)),
            dma((5,)),
            dma((5,)),
            dma((2,)),
            dma((2,)),
            dma((9,)),
            dma((9,)),
            dma,
            dma,
            pltpu.SemaphoreType.REGULAR,
            pltpu.SemaphoreType.REGULAR,
        ],
        compiler_params=pltpu.CompilerParams(
            collective_id=0, has_side_effects=True, vmem_limit_bytes=56 << 20
        ),
    )(
        right_sides,
        point_order.reshape(LEAVES, LANES),
        leaf_basis,
        transfer,
        coupling,
        far_list.T,
        far_count.reshape(1, ROWS - 1),
        coarse_transfer,
        coarse_coupling,
        coarse_list.T,
        coarse_count,
        near_block,
        near_list,
        near_count.reshape(1, LEAVES),
    )


def solution(mesh):
    return jax.shard_map(
        body,
        mesh=mesh,
        in_specs=(
            P("rhs", "leaf"),
            P("leaf"),
            P("leaf", None, None),
            P("leaf", None, None),
            P("leaf", None, None),
            P("leaf", None),
            P("leaf"),
            P(),
            P(),
            P(),
            P(),
            P("leaf", "rhs", None, None),
            P("leaf", "rhs"),
            P("leaf"),
        ),
        out_specs=P("rhs", "leaf"),
        check_vma=False,
    )
```

```python
import jax
import jax.numpy as jnp
from jax import lax
from jax.experimental import pallas as pl
from jax.experimental.pallas import tpu as pltpu
from jax.sharding import PartitionSpec as P

MESH = pl.DeviceIdType.MESH
F32 = jnp.float32
BF16 = jnp.bfloat16

DEVICES = 128
LEAVES = 16
RANK = 64
LANES = 128
COLS = 8
SLOTS = 14
FAR = 8
PAIRS = 15
ROWS = 2 * LEAVES
ZERO = 3 * ROWS
NEAR_ZERO = 3 * LEAVES
COLUMN = 8
HALF = DEVICES // 2
QUARTER = DEVICES // 4


def near_slots(leaf, core):
    at_y = (leaf & 1) + 2 * (leaf >> 2 & 1)
    at_z = (leaf >> 1 & 1) + 2 * (leaf >> 3 & 1)
    touching = 3 * (2 if at_y in (0, 3) else 3) * (2 if at_z in (0, 3) else 3)
    return min(max(touching - core * SLOTS, 0), SLOTS)


def near_kinds(core):
    kinds = {}
    for leaf in range(LEAVES):
        kinds.setdefault(near_slots(leaf, core), []).append(leaf)
    return sorted((slots, leaves) for slots, leaves in kinds.items() if slots)


def dot_nt(left, right):
    return lax.dot_general(left, right, (((1,), (1,)), ((), ())), preferred_element_type=F32)


def dot_nn(left, right):
    return lax.dot_general(left, right, (((1,), (0,)), ((), ())), preferred_element_type=F32)


def wrap(value, size):
    return lax.rem(value + size, size)


def within(value, size):
    return (value >= 0) & (value < size)


def when(flag, do):
    if flag is None:
        do()
    else:
        pl.when(flag)(do)


def kernel(
    rs_h,
    order_h,
    basis_h,
    transfer_h,
    coupling_h,
    flist_h,
    fcount_h,
    ctr_h,
    ccp_h,
    clist_h,
    ccount_h,
    near_h,
    nlist_h,
    ncount_h,
    out_v,
    rs_v,
    order_v,
    basis_v,
    transfer_v,
    coupling_v,
    near_v,
    flist_v,
    fcount_v,
    nlist_v,
    ncount_v,
    ctr_v,
    ccp_v,
    clist_s,
    ccount_s,
    fid_v,
    nid_v,
    fid_s,
    nid_s,
    xs_v,
    us_v,
    xr_v,
    ur_v,
    cs_v,
    cr_v,
    xw_v,
    table_v,
    up_v,
    blank_v,
    spare_v,
    reach_v,
    rise_v,
    climb_v,
    yown_v,
    ysend_v,
    yrecv_v,
    in_sem,
    near_sem,
    send_sem,
    xrecv_sem,
    urecv_sem,
    csend_sem,
    crecv_sem,
    yrecv_sem,
    near_ready,
    far_ready,
):
    me = lax.axis_index("leaf")
    core = lax.axis_index("rhs")
    other = 1 - core
    quad = lax.div(me, 4)
    in_quad = lax.rem(me, 4)
    duo = lax.div(me, 2)
    in_duo = lax.rem(me, 2)
    turn = 1 - 2 * in_duo
    duo_turn = 1 - 2 * lax.rem(duo, 2)
    quad_turn = 1 - 2 * lax.rem(quad, 2)
    quad_from = [wrap(quad + d, QUARTER) for d in (-2, 2, 3 * quad_turn)]
    duo_from = [wrap(duo + d, HALF) for d in (-2, 2, 3 * duo_turn)]
    groups = []
    for n, (send_by, get_by) in enumerate(((2, -2), (-2, 2), (0, 0))):
        for base, size, node, node_turn, nodes, place_in in (
            (0, 4, quad, quad_turn, QUARTER, in_quad),
            (12, 2, duo, duo_turn, HALF, in_duo),
            (18, 1, me, turn, DEVICES, 0),
        ):
            to = node + (send_by if n < 2 else 3 * node_turn)
            source = node + (get_by if n < 2 else 3 * node_turn)
            groups.append(
                (base + size * n, size, size * to, place_in, within(to, nodes), within(source, nodes))
            )
    left = me - 1
    right = me + 1
    has_left = left >= 0
    has_right = right < DEVICES
    column_first = lax.rem(me, COLUMN) == 0
    left_near = has_left & jnp.logical_not(column_first)
    left_late = has_left & column_first
    to_left = (left, has_left, 2, 0, 0)
    to_right = (right, has_right, 0, 2, 1)

    def fetch(source, target, sem):
        copy = pltpu.make_async_copy(source, target, sem)
        copy.start()
        return copy

    get_order = fetch(order_h, order_v, in_sem.at[0])
    get_rs = fetch(rs_h, rs_v, in_sem.at[1])
    def greet(device_at, device_core):
        pl.semaphore_signal(
            pltpu.get_barrier_semaphore(),
            inc=1,
            device_id=(device_at, device_core),
            device_id_type=MESH,
        )

    when(has_right, lambda: greet(right, jnp.where(lax.rem(right, COLUMN) == 0, 0, 1)))
    when(has_left, lambda: greet(left, 1))
    when(core == 0, lambda: greet(me, 1))
    near_peers = 1 + 2 * jnp.where(has_right, 1, 0) + 2 * jnp.where(left_near, 1, 0)
    far_peers = 2 * jnp.where(left_late, 1, 0)
    for _, size, to, _, there, source_there in groups:

        def greet_all():
            for i in range(size):
                greet(to + i, 0)

        when(there, greet_all)
        far_peers = far_peers + 2 * jnp.where(there, size, 0)

    get_basis = fetch(basis_h, basis_v, in_sem.at[2])
    get_transfer = fetch(transfer_h, transfer_v, in_sem.at[3])
    get_lists = [
        fetch(nlist_h, nlist_v, in_sem.at[4]),
        fetch(ncount_h, ncount_v, in_sem.at[5]),
        fetch(flist_h, flist_v, in_sem.at[6]),
        fetch(fcount_h, fcount_v, in_sem.at[7]),
    ]
    for n in range(3):
        fetch(ctr_h.at[pl.ds(2 * quad_from[n], 2)], ctr_v.at[pl.ds(2 * n, 2)], in_sem.at[8])
        fetch(ctr_h.at[pl.ds(duo_from[n], 1)], ctr_v.at[pl.ds(6 + n, 1)], in_sem.at[8])
        fetch(ctr_h.at[pl.ds(HALF + quad_from[n], 1)], ctr_v.at[pl.ds(9 + n, 1)], in_sem.at[8])
    fetch(ctr_h.at[pl.ds(duo, 1)], ctr_v.at[pl.ds(12, 1)], in_sem.at[8])
    fetch(ctr_h.at[pl.ds(HALF + quad, 1)], ctr_v.at[pl.ds(13, 1)], in_sem.at[8])
    fetch(ccp_h.at[pl.ds(duo, 1)], ccp_v.at[pl.ds(0, 1)], in_sem.at[9])
    fetch(ccp_h.at[pl.ds(HALF + quad, 1)], ccp_v.at[pl.ds(1, 1)], in_sem.at[9])


    low = lax.broadcasted_iota(jnp.int32, (COLS, LANES), 1) < RANK
    low4 = lax.broadcasted_iota(jnp.int32, (COLS // 2, LANES), 1) < RANK
    low16 = lax.broadcasted_iota(jnp.int32, (2 * COLS, LANES), 1) < RANK
    top16 = lax.broadcasted_iota(jnp.int32, (2 * COLS, LANES), 0) < COLS
    diagonal = low16 == top16

    def both(first, second):
        return jnp.concatenate([first, second], axis=0)

    def meet(first, second):
        return jnp.where(low, first, second)

    def flip(pair):
        return pltpu.roll(pair, RANK, 1)

    def join(product):
        return jnp.where(low, product[:COLS], product[COLS:])

    get_order.wait()
    get_rs.wait()
    place = order_v[...] - me * (LEAVES * LANES)
    for j in range(0, LEAVES, 2):
        blocks = []
        for i in (j, j + 1):
            here = jnp.broadcast_to(place[i : i + 1], (COLS, LANES))
            chunk = here // LANES
            lane = here % LANES
            block = jnp.take_along_axis(rs_v[:, 0:LANES], lane, axis=1, mode="promise_in_bounds")
            for c in range(1, LEAVES):
                found = jnp.take_along_axis(
                    rs_v[:, c * LANES : (c + 1) * LANES], lane, axis=1, mode="promise_in_bounds"
                )
                block = jnp.where(chunk == c, found, block)
            blocks.append(block)
        xs_v[j // 2] = both(*blocks).astype(BF16)

    def remote(source, target, send_sem, recv_sem, device_at, device_core):
        return pltpu.make_async_remote_copy(
            src_ref=source,
            dst_ref=target,
            send_sem=send_sem,
            recv_sem=recv_sem,
            device_id=(device_at, device_core),
            device_id_type=MESH,
        )

    def send_points(side):
        device_at, _, slot, _, sem = side
        for to_core, step in ((core, 0), (other, 1)):
            remote(
                xs_v, xr_v.at[slot + step], send_sem.at[sem], xrecv_sem.at[slot // 2], device_at, to_core
            ).start()

    def send_pairs(side):
        device_at, _, slot, _, sem = side
        remote(us_v, ur_v.at[slot // 2], send_sem.at[sem], urecv_sem.at[slot // 2], device_at, core).start()

    def tell(sem):
        pl.semaphore_signal(sem, inc=1, device_id=(me, other), device_id_type=MESH)

    def near_gate():
        pl.semaphore_wait(pltpu.get_barrier_semaphore(), near_peers)
        tell(near_ready)

    def far_gate():
        pl.semaphore_wait(pltpu.get_barrier_semaphore(), far_peers)
        tell(far_ready)

    get_coarse = [fetch(clist_h, clist_s, in_sem.at[0]), fetch(ccount_h, ccount_s, in_sem.at[1])]

    blank_v[...] = jnp.zeros(blank_v.shape, F32)
    when(core == 1, near_gate)
    when(core == 0, lambda: pl.semaphore_wait(near_ready, 1))
    remote(xs_v, xr_v.at[4], send_sem.at[2], xrecv_sem.at[2], me, other).start()
    when(has_right, lambda: send_points(to_right))
    when(left_near, lambda: send_points(to_left))

    get_basis.wait()
    get_transfer.wait()
    def fetch_near(at):
        def do():
            for k, (slots, leaves) in enumerate(near_kinds(at)):
                for j in leaves:
                    used = pl.ds(0, slots)
                    fetch(near_h.at[j, used], near_v.at[j, used], near_sem.at[k])

        return do

    for at in range(2):
        when(core == at, fetch_near(at))
    get_coupling = fetch(coupling_h, coupling_v, in_sem.at[10])
    own = ROWS
    for p in range(LEAVES // 2):
        matrices = basis_v[2 * p : 2 * p + 2].reshape(LANES, LANES)
        pair = join(dot_nt(xs_v[p], matrices))
        up_v[p] = pair
        table_v[own + 2 * p] = pair
        table_v[own + 2 * p + 1] = flip(pair)
    first = 0
    for width in (8, 4, 2):
        for p in range(width // 2):
            tile = both(up_v[first + 2 * p], up_v[first + 2 * p + 1]).astype(BF16)
            us_v[first // 2 + p] = tile
            row = first + 2 * p
            matrices = transfer_v[row : row + 2].reshape(LANES, LANES)
            pair = join(dot_nt(tile, matrices))
            at = first + width + p
            up_v[at] = pair
            table_v[own + 2 * at] = pair
            table_v[own + 2 * at + 1] = flip(pair)
        first += width
    last = both(up_v[14], jnp.zeros((COLS, LANES), F32)).astype(BF16)
    us_v[7] = last
    when(has_right, lambda: send_pairs(to_right))
    when(left_near, lambda: send_pairs(to_left))
    root = transfer_v[14]
    mine = dot_nt(last, both(root, root))
    cs_v[...] = jnp.where(low4, mine[: COLS // 2], mine[COLS // 2 : COLS]).astype(BF16).astype(F32)
    for copy in get_lists:
        copy.wait()
    square = lax.broadcasted_iota(jnp.int32, (LEAVES, LEAVES), 0) == lax.broadcasted_iota(
        jnp.int32, (LEAVES, LEAVES), 1
    )
    counts = jnp.broadcast_to(ncount_v[...], (LEAVES, LEAVES))
    counts = jnp.sum(jnp.where(square, counts, 0), axis=1, keepdims=True)
    slot_at = lax.broadcasted_iota(jnp.int32, (LEAVES, SLOTS), 1) + core * SLOTS
    nid_v[...] = jnp.where(slot_at < counts, nlist_v[...] - (me - 1) * LEAVES, NEAR_ZERO)
    node = lax.broadcasted_iota(jnp.int32, (FAR, ROWS - 1), 1)
    slot_at = lax.broadcasted_iota(jnp.int32, (FAR, ROWS - 1), 0)
    entry = flist_v[...]
    row = jnp.zeros_like(entry)
    for height in range(4):
        width = LEAVES >> height
        start = ROWS - 2 * width
        side = entry // width - me + 1
        inside = (node >= start) & (node < start + width)
        row = jnp.where(inside, side * ROWS + start + entry % width, row)
    row = row + jnp.where(slot_at % 2 == 0, 0, 1 - 2 * (row % 2))
    step = entry - me
    root_row = jnp.where(step == -2, 0, jnp.where(step == 2, 1, 2))
    row = jnp.where(node == ROWS - 2, root_row, row)
    live = slot_at < fcount_v[...]
    fid_v[...] = jnp.where(live, row, jnp.where(node == ROWS - 2, 3, ZERO))
    put_near = fetch(nid_v, nid_s, in_sem.at[4])
    put_far = fetch(fid_v, fid_s, in_sem.at[6])
    zero = jnp.zeros((COLS, LANES), F32)
    table_v[ZERO] = zero
    xw_v[NEAR_ZERO] = jnp.zeros((2 * COLS, LANES), BF16)

    def spread(pair, mask):
        return jnp.where(mask, both(pair, pair), 0.0).astype(BF16)

    low128 = lax.broadcasted_iota(jnp.int32, (LANES, LANES), 1) < RANK
    top128 = lax.broadcasted_iota(jnp.int32, (LANES, LANES), 0) < RANK
    diagonal128 = low128 == top128
    low64 = low128[:RANK]

    def compose():
        chains = {14: transfer_v[14].astype(F32)}
        for first, width in ((12, 2), (8, 4), (0, 8)):
            for p in range(width // 2):
                row = first + 2 * p
                matrices = transfer_v[row : row + 2].reshape(LANES, LANES)
                product = dot_nn(spread(chains[first + width + p], diagonal128), matrices)
                chains[row] = product[:RANK]
                chains[row + 1] = product[RANK:]
        for p in range(LEAVES // 2):
            matrices = basis_v[2 * p : 2 * p + 2].reshape(LANES, LANES)
            product = dot_nn(spread(chains[p], diagonal128), matrices).astype(BF16)
            reach_v[:, 2 * p * LANES : (2 * p + 1) * LANES] = product[:RANK]
            reach_v[:, (2 * p + 1) * LANES : (2 * p + 2) * LANES] = product[RANK:]
        pltpu.make_async_copy(ctr_h.at[pl.ds(0, 14)], ctr_v, in_sem.at[8]).wait()
        pltpu.make_async_copy(ccp_h.at[pl.ds(0, 2)], ccp_v, in_sem.at[9]).wait()
        for copy in get_coarse:
            copy.wait()
        for n in range(3):
            matrix = ctr_v[9 + n].astype(F32)
            product = dot_nn(
                spread(matrix, diagonal128), ctr_v[2 * n : 2 * n + 2].reshape(LANES, LANES)
            ).astype(BF16)
            rise_v[n, :, :LANES] = product[:RANK]
            rise_v[n, :, LANES:] = product[RANK:]
        duo_matrix = ctr_v[12].astype(F32)
        duo_matrix = jnp.where(in_duo == 0, duo_matrix, flip(duo_matrix)).astype(BF16)
        quad_matrix = ctr_v[13].astype(F32)
        quad_matrix = jnp.where(lax.rem(duo, 2) == 0, quad_matrix, flip(quad_matrix)).astype(BF16)
        fall = both(dot_nn(quad_matrix[:, :RANK], duo_matrix), duo_matrix.astype(F32)).T[:RANK].astype(BF16)

        def chosen(at, node_here):
            rows = []
            for s in range(3):
                step = clist_s[s, at] - node_here
                row = jnp.where(step == -2, 0, jnp.where(step == 2, 1, 2))
                rows.append(jnp.where(s < ccount_s[at], row, 3))
            return [[jnp.where(row == n, 1.0, 0.0).astype(F32) for n in range(3)] for row in rows]

        for base, width, part, node_here, at, matrices in (
            (0, 2 * LANES, 1, quad, HALF + quad, [rise_v.at[n] for n in range(3)]),
            (6, LANES, 0, duo, duo, [ctr_v.at[6 + n] for n in range(3)]),
        ):
            onto = fall[:, (1 - part) * RANK : (2 - part) * RANK]
            first_two = dot_nn(onto, ccp_v[part, :, :LANES])
            third = dot_nn(onto, ccp_v[part, :, LANES:])
            flags = chosen(at, node_here)
            for n in range(3):
                matrix = matrices[n][...]
                kept = first_two * jnp.where(low64, flags[0][n], flags[1][n])
                product = dot_nn(kept.astype(BF16), both(matrix, matrix))
                product += dot_nn((third * flags[2][n]).astype(BF16), matrix)
                start = base * LANES + n * width
                climb_v[:, start : start + width] = product.astype(BF16)

    early = lax.rem(me, COLUMN) < COLUMN // 2
    when(early, compose)
    when(core == 0, far_gate)
    when(core == 1, lambda: pl.semaphore_wait(far_ready, 1))
    when(left_late, lambda: send_points(to_left))
    for first, size, to, place_in, there, source_there in groups:

        def send_root():
            for i in range(size):
                target = cr_v.at[first + place_in]
                remote(cs_v, target, csend_sem, crecv_sem, to + i, core).start()

        def skip_root():
            fetch(blank_v.at[pl.ds(0, size)], spare_v.at[pl.ds(first, size)], csend_sem)

        def blank_root():
            fetch(blank_v.at[pl.ds(0, size)], cr_v.at[pl.ds(first, size)], crecv_sem)

        when(there, send_root)
        when(jnp.logical_not(there), skip_root)
        when(jnp.logical_not(source_there), blank_root)

    when(left_late, lambda: send_pairs(to_left))
    when(jnp.logical_not(early), compose)
    put_near.wait()
    put_far.wait()


    get_coupling.wait()
    matrix = coupling_v[ROWS - 2, :, : 4 * RANK].astype(F32)
    for n in range(3):
        flags = [jnp.where(fid_s[s, ROWS - 2] == n, 1.0, 0.0).astype(F32) for s in range(3)]
        kept = matrix[:, :LANES] * jnp.where(low64, flags[0], flags[1])
        kept += jnp.where(low64, matrix[:, LANES:] * flags[2], 0.0)
        climb_v[:, (9 + n) * LANES : (10 + n) * LANES] = kept.astype(BF16)

    def arrived(buffer, sem):
        remote(buffer, buffer, send_sem.at[2], sem, me, other).wait_recv()

    for _, there, _, slot, _ in (to_left, to_right):
        landing = xr_v.at[pl.ds(slot, 2)]

        def zero_points():
            landing[...] = jnp.zeros((2,) + xs_v.shape, BF16)

        when(there, lambda: arrived(landing, xrecv_sem.at[slot // 2]))
        when(jnp.logical_not(there), zero_points)
    arrived(xr_v.at[4], xrecv_sem.at[2])

    def arrange(base, mine, theirs):
        for p in range(LEAVES // 2):
            a = mine[p].astype(F32)
            b = theirs[p].astype(F32)
            xw_v[base + 2 * p] = both(a[:COLS], b[:COLS]).astype(BF16)
            xw_v[base + 2 * p + 1] = both(a[COLS:], b[COLS:]).astype(BF16)

    arrange(0, xr_v.at[0], xr_v.at[1])
    arrange(LEAVES, xs_v, xr_v.at[4])
    arrange(2 * LEAVES, xr_v.at[2], xr_v.at[3])

    def near_leaves(at):
        def do():
            for k, (slots, leaves) in enumerate(near_kinds(at)):
                used = near_v.at[pl.ds(0, len(leaves)), pl.ds(0, slots)]
                pltpu.make_async_copy(used, used, near_sem.at[k]).wait()
            for j in range(LEAVES):
                slots = near_slots(j, at)
                if slots:
                    points = jnp.concatenate([xw_v[nid_s[j, s]] for s in range(slots)], axis=1)
                    blocks = jnp.concatenate([near_v[j, s] for s in range(slots)], axis=1)
                    total = dot_nt(points, blocks)
                else:
                    total = jnp.zeros((2 * COLS, LANES), F32)
                yown_v[j] = total[:COLS]
                ysend_v[j] = total[COLS:]

        return do

    for at in range(2):
        when(core == at, near_leaves(at))
    send_near = remote(ysend_v, yrecv_v, send_sem.at[2], yrecv_sem, me, other)
    send_near.start()

    for _, there, _, slot, _ in (to_left, to_right):
        landing = ur_v.at[slot // 2]

        def zero_pairs():
            landing[...] = jnp.zeros(us_v.shape, BF16)

        when(there, lambda: arrived(landing, urecv_sem.at[slot // 2]))
        when(jnp.logical_not(there), zero_pairs)
    for slot, base in ((0, 0), (1, 2 * ROWS)):
        for t in range(8):
            tile = ur_v[slot, t].astype(F32)
            for half in range(2):
                pair = tile[half * COLS : (half + 1) * COLS]
                table_v[base + 4 * t + 2 * half] = pair
                table_v[base + 4 * t + 2 * half + 1] = flip(pair)


    def couple(p):
        matrices = coupling_v[2 * p : 2 * p + 2].reshape(LANES, FAR * RANK)
        picked = []
        for node in (2 * p, 2 * p + 1):
            picked.append(
                jnp.concatenate(
                    [
                        meet(table_v[fid_s[2 * t, node]], table_v[fid_s[2 * t + 1, node]])
                        for t in range(FAR // 2)
                    ],
                    axis=1,
                )
            )
        return join(dot_nt(both(*picked).astype(BF16), matrices))

    fields = {14: couple(14)}
    for first, width in ((12, 2), (8, 4), (0, 8)):
        for p in range(width // 2):
            row = first + 2 * p
            matrices = transfer_v[row : row + 2].reshape(LANES, LANES)
            incoming = [couple(row), couple(row + 1)]
            down = dot_nn(spread(fields[first + width + p], diagonal), matrices)
            fields[row] = incoming[0] + down[:COLS]
            fields[row + 1] = incoming[1] + down[COLS:]
    for p in range(LEAVES // 2):
        matrices = basis_v[2 * p : 2 * p + 2].reshape(LANES, LANES)
        far = dot_nn(spread(fields[p], diagonal), matrices)
        out_v[:, 2 * p * LANES : (2 * p + 1) * LANES] = far[:COLS]
        out_v[:, (2 * p + 1) * LANES : (2 * p + 2) * LANES] = far[COLS:]

    arrived(cr_v, crecv_sem)
    def root_of(slot):
        packed = cr_v[slot]
        turned = flip(packed)
        return both(jnp.where(low4, packed, turned), jnp.where(low4, turned, packed))

    gathered = [meet(root_of(i), root_of(i + 1)) for i in range(0, 18, 2)]
    gathered += [root_of(i) for i in range(18, 21)]
    gathered = jnp.concatenate(gathered, axis=1)
    field = dot_nt(both(gathered, gathered).astype(BF16), climb_v[...])
    far = dot_nn(field.astype(BF16), reach_v[...])[:COLS]

    arrived(yrecv_v, yrecv_sem)

    def left_here(buffer, sem):
        remote(buffer, buffer, sem, yrecv_sem, me, other).wait_send()

    when(has_left, lambda: left_here(xr_v.at[pl.ds(0, 3)], send_sem.at[0]))
    when(has_right, lambda: left_here(xr_v.at[pl.ds(0, 3)], send_sem.at[1]))
    left_here(xr_v.at[pl.ds(0, 3)], send_sem.at[2])
    left_here(cr_v, csend_sem)
    for j in range(LEAVES):
        columns = slice(j * LANES, (j + 1) * LANES)
        out_v[:, columns] += far[:, columns] + yown_v[j] + yrecv_v[j]


def body(
    right_sides,
    point_order,
    leaf_basis,
    transfer,
    coupling,
    far_list,
    far_count,
    coarse_transfer,
    coarse_coupling,
    coarse_list,
    coarse_count,
    near_block,
    near_list,
    near_count,
):
    tile = (2 * COLS, LANES)
    dma = pltpu.SemaphoreType.DMA
    return pl.pallas_call(
        kernel,
        out_shape=pltpu.VMEM((COLS, LEAVES * LANES), F32),
        in_specs=[pl.BlockSpec(memory_space=pltpu.HBM)] * 14,
        out_specs=pl.BlockSpec(memory_space=pltpu.VMEM),
        scratch_shapes=[
            pltpu.VMEM((COLS, LEAVES * LANES), F32),
            pltpu.VMEM((LEAVES, LANES), jnp.int32),
            pltpu.VMEM((LEAVES, RANK, LANES), BF16),
            pltpu.VMEM((LEAVES - 1, RANK, LANES), BF16),
            pltpu.VMEM((ROWS - 1, RANK, FAR * RANK), BF16),
            pltpu.VMEM((LEAVES, SLOTS, LANES, LANES), BF16),
            pltpu.VMEM((FAR, ROWS - 1), jnp.int32),
            pltpu.VMEM((1, ROWS - 1), jnp.int32),
            pltpu.VMEM((LEAVES, SLOTS), jnp.int32),
            pltpu.VMEM((1, LEAVES), jnp.int32),
            pltpu.VMEM((14, RANK, LANES), BF16),
            pltpu.VMEM((2, RANK, 3 * RANK), BF16),
            pltpu.SMEM((3, 96), jnp.int32),
            pltpu.SMEM((96,), jnp.int32),
            pltpu.VMEM((FAR, ROWS - 1), jnp.int32),
            pltpu.VMEM((LEAVES, SLOTS), jnp.int32),
            pltpu.SMEM((FAR, ROWS - 1), jnp.int32),
            pltpu.SMEM((LEAVES, SLOTS), jnp.int32),
            pltpu.VMEM((LEAVES // 2,) + tile, BF16),
            pltpu.VMEM((LEAVES // 2,) + tile, BF16),
            pltpu.VMEM((5, LEAVES // 2) + tile, BF16),
            pltpu.VMEM((2, LEAVES // 2) + tile, BF16),
            pltpu.VMEM((COLS // 2, LANES), F32),
            pltpu.VMEM((21, COLS // 2, LANES), F32),
            pltpu.VMEM((3 * LEAVES + 1,) + tile, BF16),
            pltpu.VMEM((ZERO + 1, COLS, LANES), F32),
            pltpu.VMEM((PAIRS, COLS, LANES), F32),
            pltpu.VMEM((4, COLS // 2, LANES), F32),
            pltpu.VMEM((21, COLS // 2, LANES), F32),
            pltpu.VMEM((RANK, LEAVES * LANES), BF16),
            pltpu.VMEM((3, RANK, 2 * LANES), BF16),
            pltpu.VMEM((RANK, 12 * LANES), BF16),
            pltpu.VMEM((LEAVES, COLS, LANES), F32),
            pltpu.VMEM((LEAVES, COLS, LANES), F32),
            pltpu.VMEM((LEAVES, COLS, LANES), F32),
            dma((11,)),
            dma((2,)),
            dma((3,)),
            dma((3,)),
            dma((2,)),
            dma,
            dma,
            dma,
            pltpu.SemaphoreType.REGULAR,
            pltpu.SemaphoreType.REGULAR,
        ],
        compiler_params=pltpu.CompilerParams(
            collective_id=0, has_side_effects=True, vmem_limit_bytes=56 << 20
        ),
    )(
        right_sides,
        point_order.reshape(LEAVES, LANES),
        leaf_basis,
        transfer,
        coupling,
        far_list.T,
        far_count.reshape(1, ROWS - 1),
        coarse_transfer,
        coarse_coupling,
        coarse_list.T,
        coarse_count,
        near_block,
        near_list,
        near_count.reshape(1, LEAVES),
    )


def solution(mesh):
    return jax.shard_map(
        body,
        mesh=mesh,
        in_specs=(
            P("rhs", "leaf"),
            P("leaf"),
            P("leaf", None, None),
            P("leaf", None, None),
            P("leaf", None, None),
            P("leaf", None),
            P("leaf"),
            P(),
            P(),
            P(),
            P(),
            P("leaf", "rhs", None, None),
            P("leaf", "rhs"),
            P("leaf"),
        ),
        out_specs=P("rhs", "leaf"),
        check_vma=False,
    )
```

```python
import jax
import jax.numpy as jnp
from jax import lax
from jax.experimental import pallas as pl
from jax.experimental.pallas import tpu as pltpu
from jax.sharding import PartitionSpec as P

MESH = pl.DeviceIdType.MESH
F32 = jnp.float32
BF16 = jnp.bfloat16

DEVICES = 128
LEAVES = 16
RANK = 64
LANES = 128
COLS = 8
SLOTS = 14
FAR = 8
PAIRS = 15
ROWS = 2 * LEAVES
ZERO = 3 * ROWS
NEAR_ZERO = 3 * LEAVES
COLUMN = 8
HALF = DEVICES // 2
QUARTER = DEVICES // 4


def near_slots(leaf, core, slabs=3):
    at_y = (leaf & 1) + 2 * (leaf >> 2 & 1)
    at_z = (leaf >> 1 & 1) + 2 * (leaf >> 3 & 1)
    touching = (2 if at_y in (0, 3) else 3) * (2 if at_z in (0, 3) else 3)
    return min(max(3 * touching - core * SLOTS, 0), SLOTS, slabs * touching)


def near_kinds(core):
    kinds = {}
    for leaf in range(LEAVES):
        kinds.setdefault(near_slots(leaf, core), []).append(leaf)
    return sorted((slots, leaves) for slots, leaves in kinds.items() if slots)


def dot_nt(left, right):
    return lax.dot_general(left, right, (((1,), (1,)), ((), ())), preferred_element_type=F32)


def dot_nn(left, right):
    return lax.dot_general(left, right, (((1,), (0,)), ((), ())), preferred_element_type=F32)


def wrap(value, size):
    return lax.rem(value + size, size)


def within(value, size):
    return (value >= 0) & (value < size)


def starts_first(device):
    return lax.rem(device + DEVICES, COLUMN) == 0


def when(flag, do):
    if flag is None:
        do()
    else:
        pl.when(flag)(do)


def kernel(
    rs_h,
    order_h,
    basis_h,
    transfer_h,
    coupling_h,
    flist_h,
    fcount_h,
    ctr_h,
    ccp_h,
    clist_h,
    ccount_h,
    near_h,
    nlist_h,
    ncount_h,
    out_v,
    rs_v,
    order_v,
    basis_v,
    transfer_v,
    coupling_v,
    near_v,
    flist_v,
    fcount_v,
    nlist_v,
    ncount_v,
    ctr_v,
    ccp_v,
    clist_s,
    ccount_s,
    fid_v,
    nid_v,
    fid_s,
    nid_s,
    late_v,
    late_s,
    xs_v,
    us_v,
    xr_v,
    ur_v,
    cs_v,
    cr_v,
    xw_v,
    table_v,
    up_v,
    blank_v,
    spare_v,
    reach_v,
    rise_v,
    climb_v,
    yown_v,
    ysend_v,
    yrecv_v,
    in_sem,
    near_sem,
    send_sem,
    xrecv_sem,
    urecv_sem,
    csend_sem,
    crecv_sem,
    yrecv_sem,
    near_ready,
    far_ready,
):
    me = lax.axis_index("leaf")
    core = lax.axis_index("rhs")
    other = 1 - core
    quad = lax.div(me, 4)
    in_quad = lax.rem(me, 4)
    duo = lax.div(me, 2)
    in_duo = lax.rem(me, 2)
    turn = 1 - 2 * in_duo
    duo_turn = 1 - 2 * lax.rem(duo, 2)
    quad_turn = 1 - 2 * lax.rem(quad, 2)
    quad_from = [wrap(quad + d, QUARTER) for d in (-2, 2, 3 * quad_turn)]
    duo_from = [wrap(duo + d, HALF) for d in (-2, 2, 3 * duo_turn)]
    groups = []
    for n, (send_by, get_by) in enumerate(((2, -2), (-2, 2), (0, 0))):
        for base, size, node, node_turn, nodes, place_in in (
            (0, 4, quad, quad_turn, QUARTER, in_quad),
            (12, 2, duo, duo_turn, HALF, in_duo),
            (18, 1, me, turn, DEVICES, 0),
        ):
            to = node + (send_by if n < 2 else 3 * node_turn)
            source = node + (get_by if n < 2 else 3 * node_turn)
            groups.append(
                (base + size * n, size, size * to, place_in, within(to, nodes), within(source, nodes))
            )
    left = me - 1
    right = me + 1
    has_left = left >= 0
    has_right = right < DEVICES
    column_first = lax.rem(me, COLUMN) == 0
    left_near = has_left & jnp.logical_not(column_first)
    left_late = has_left & column_first
    right_late = has_right & (lax.rem(right, COLUMN) == 0)
    late = left_late | right_late
    to_left = (left, has_left, 2, 0, 0)
    to_right = (right, has_right, 0, 2, 1)

    def fetch(source, target, sem):
        copy = pltpu.make_async_copy(source, target, sem)
        copy.start()
        return copy

    get_order = fetch(order_h, order_v, in_sem.at[0])
    for part in range(4):
        columns = pl.ds(part * (LEAVES * LANES // 4), LEAVES * LANES // 4)
        fetch(rs_h.at[:, columns], rs_v.at[:, columns], in_sem.at[1])
    def greet(device_at, device_core):
        pl.semaphore_signal(
            pltpu.get_barrier_semaphore(),
            inc=1,
            device_id=(device_at, device_core),
            device_id_type=MESH,
        )

    when(has_right, lambda: greet(right, jnp.where(lax.rem(right, COLUMN) == 0, 0, 1)))
    when(has_left, lambda: greet(left, 1))
    when(core == 0, lambda: greet(me, 1))
    near_peers = 1 + 2 * jnp.where(has_right, 1, 0) + 2 * jnp.where(left_near, 1, 0)
    far_peers = 2 * jnp.where(left_late, 1, 0)
    for _, size, to, _, there, source_there in groups:

        def greet_all():
            for i in range(size):
                greet(to + i, jnp.where(starts_first(me), 1, 0))

        when(there, greet_all)
        first_ones = jnp.where(starts_first(to), 1, 0)
        near_peers = near_peers + 2 * jnp.where(there, first_ones, 0)
        far_peers = far_peers + 2 * jnp.where(there, size - first_ones, 0)

    get_basis = fetch(basis_h, basis_v, in_sem.at[2])
    get_transfer = fetch(transfer_h, transfer_v, in_sem.at[3])
    get_lists = [
        fetch(nlist_h, nlist_v, in_sem.at[4]),
        fetch(ncount_h, ncount_v, in_sem.at[5]),
        fetch(flist_h, flist_v, in_sem.at[6]),
        fetch(fcount_h, fcount_v, in_sem.at[7]),
    ]
    for n in range(3):
        fetch(ctr_h.at[pl.ds(2 * quad_from[n], 2)], ctr_v.at[pl.ds(2 * n, 2)], in_sem.at[8])
        fetch(ctr_h.at[pl.ds(duo_from[n], 1)], ctr_v.at[pl.ds(6 + n, 1)], in_sem.at[8])
        fetch(ctr_h.at[pl.ds(HALF + quad_from[n], 1)], ctr_v.at[pl.ds(9 + n, 1)], in_sem.at[8])
    fetch(ctr_h.at[pl.ds(duo, 1)], ctr_v.at[pl.ds(12, 1)], in_sem.at[8])
    fetch(ctr_h.at[pl.ds(HALF + quad, 1)], ctr_v.at[pl.ds(13, 1)], in_sem.at[8])
    fetch(ccp_h.at[pl.ds(duo, 1)], ccp_v.at[pl.ds(0, 1)], in_sem.at[9])
    fetch(ccp_h.at[pl.ds(HALF + quad, 1)], ccp_v.at[pl.ds(1, 1)], in_sem.at[9])


    low = lax.broadcasted_iota(jnp.int32, (COLS, LANES), 1) < RANK
    low4 = lax.broadcasted_iota(jnp.int32, (COLS // 2, LANES), 1) < RANK
    low16 = lax.broadcasted_iota(jnp.int32, (2 * COLS, LANES), 1) < RANK
    top16 = lax.broadcasted_iota(jnp.int32, (2 * COLS, LANES), 0) < COLS
    diagonal = low16 == top16

    def both(first, second):
        return jnp.concatenate([first, second], axis=0)

    def meet(first, second):
        return jnp.where(low, first, second)

    def flip(pair):
        return pltpu.roll(pair, RANK, 1)

    def join(product):
        return jnp.where(low, product[:COLS], product[COLS:])

    get_order.wait()
    pltpu.make_async_copy(rs_h, rs_v, in_sem.at[1]).wait()
    place = order_v[...] - me * (LEAVES * LANES)
    for j in range(0, LEAVES, 2):
        blocks = []
        for i in (j, j + 1):
            here = jnp.broadcast_to(place[i : i + 1], (COLS, LANES))
            chunk = here // LANES
            lane = here % LANES
            block = jnp.take_along_axis(rs_v[:, 0:LANES], lane, axis=1, mode="promise_in_bounds")
            for c in range(1, LEAVES):
                found = jnp.take_along_axis(
                    rs_v[:, c * LANES : (c + 1) * LANES], lane, axis=1, mode="promise_in_bounds"
                )
                block = jnp.where(chunk == c, found, block)
            blocks.append(block)
        xs_v[j // 2] = both(*blocks).astype(BF16)

    def remote(source, target, send_sem, recv_sem, device_at, device_core):
        return pltpu.make_async_remote_copy(
            src_ref=source,
            dst_ref=target,
            send_sem=send_sem,
            recv_sem=recv_sem,
            device_id=(device_at, device_core),
            device_id_type=MESH,
        )

    def send_points(side):
        device_at, _, slot, _, sem = side
        for to_core, step in ((core, 0), (other, 1)):
            remote(
                xs_v, xr_v.at[slot + step], send_sem.at[sem], xrecv_sem.at[slot // 2], device_at, to_core
            ).start()

    def send_pairs(side):
        device_at, _, slot, _, sem = side
        remote(us_v, ur_v.at[slot // 2], send_sem.at[sem], urecv_sem.at[slot // 2], device_at, core).start()

    def send_roots(to_first):
        for first, size, to, place_in, there, source_there in groups:

            def send_root(i):
                target = cr_v.at[first + place_in]
                return lambda: remote(cs_v, target, csend_sem, crecv_sem, to + i, core).start()

            def skip_root():
                fetch(blank_v.at[pl.ds(0, size)], spare_v.at[pl.ds(first, size)], csend_sem)

            def blank_root():
                fetch(blank_v.at[pl.ds(0, size)], cr_v.at[pl.ds(first, size)], crecv_sem)

            if to_first:
                when(there & starts_first(to), send_root(0))
                when(jnp.logical_not(there), skip_root)
                when(jnp.logical_not(source_there), blank_root)
            else:
                when(there & jnp.logical_not(starts_first(to)), send_root(0))
                for i in range(1, size):
                    when(there, send_root(i))

    def tell(sem):
        pl.semaphore_signal(sem, inc=1, device_id=(me, other), device_id_type=MESH)

    def near_gate():
        pl.semaphore_wait(pltpu.get_barrier_semaphore(), near_peers)
        tell(near_ready)

    def far_gate():
        pl.semaphore_wait(pltpu.get_barrier_semaphore(), far_peers)
        tell(far_ready)

    get_coarse = [fetch(clist_h, clist_s, in_sem.at[0]), fetch(ccount_h, ccount_s, in_sem.at[1])]

    blank_v[...] = jnp.zeros(blank_v.shape, F32)
    when(core == 1, near_gate)
    when(core == 0, lambda: pl.semaphore_wait(near_ready, 1))
    remote(xs_v, xr_v.at[4], send_sem.at[2], xrecv_sem.at[2], me, other).start()
    when(has_right, lambda: send_points(to_right))
    when(left_near, lambda: send_points(to_left))

    get_basis.wait()
    get_transfer.wait()
    def fetch_near(at):
        def do():
            for k, (slots, leaves) in enumerate(near_kinds(at)):
                for j in leaves:
                    used = pl.ds(0, slots)
                    fetch(near_h.at[j, used], near_v.at[j, used], near_sem.at[k])

        return do

    for at in range(2):
        when(core == at, fetch_near(at))
    get_coupling = fetch(coupling_h, coupling_v, in_sem.at[10])
    own = ROWS
    for p in range(LEAVES // 2):
        matrices = basis_v[2 * p : 2 * p + 2].reshape(LANES, LANES)
        pair = join(dot_nt(xs_v[p], matrices))
        up_v[p] = pair
        table_v[own + 2 * p] = pair
        table_v[own + 2 * p + 1] = flip(pair)
    first = 0
    for width in (8, 4, 2):
        for p in range(width // 2):
            tile = both(up_v[first + 2 * p], up_v[first + 2 * p + 1]).astype(BF16)
            us_v[first // 2 + p] = tile
            row = first + 2 * p
            matrices = transfer_v[row : row + 2].reshape(LANES, LANES)
            pair = join(dot_nt(tile, matrices))
            at = first + width + p
            up_v[at] = pair
            table_v[own + 2 * at] = pair
            table_v[own + 2 * at + 1] = flip(pair)
        first += width
    last = both(up_v[14], jnp.zeros((COLS, LANES), F32)).astype(BF16)
    us_v[7] = last
    root = transfer_v[14]
    mine = dot_nt(last, both(root, root))
    cs_v[...] = jnp.where(low4, mine[: COLS // 2], mine[COLS // 2 : COLS]).astype(BF16).astype(F32)
    send_roots(True)
    when(has_right, lambda: send_pairs(to_right))
    when(left_near, lambda: send_pairs(to_left))

    for copy in get_lists:
        copy.wait()
    square = lax.broadcasted_iota(jnp.int32, (LEAVES, LEAVES), 0) == lax.broadcasted_iota(
        jnp.int32, (LEAVES, LEAVES), 1
    )
    counts = jnp.broadcast_to(ncount_v[...], (LEAVES, LEAVES))
    counts = jnp.sum(jnp.where(square, counts, 0), axis=1, keepdims=True)
    slot_at = lax.broadcasted_iota(jnp.int32, (LEAVES, SLOTS), 1) + core * SLOTS
    near_row = jnp.where(slot_at < counts, nlist_v[...] - (me - 1) * LEAVES, NEAR_ZERO)
    nid_v[...] = near_row

    def list_late():
        first_row = jnp.where(left_late, 0, 2 * LEAVES)
        hits = jnp.where((near_row >= first_row) & (near_row < first_row + LEAVES), 1, 0)
        column = lax.broadcasted_iota(jnp.int32, (LEAVES, LEAVES), 1)
        place_at = jnp.zeros((LEAVES, LEAVES), jnp.int32)
        slots = jnp.zeros((LEAVES, LEAVES), jnp.int32)
        rows = jnp.full((LEAVES, LEAVES), NEAR_ZERO, jnp.int32)
        for s in range(SLOTS):
            hit = jnp.broadcast_to(hits[:, s : s + 1], (LEAVES, LEAVES))
            here = (column == place_at) & (hit == 1)
            slots = jnp.where(here, s, slots)
            rows = jnp.where(here, jnp.broadcast_to(near_row[:, s : s + 1], (LEAVES, LEAVES)), rows)
            place_at = place_at + hit
        late_v[:LEAVES] = slots
        late_v[LEAVES:] = rows
        fetch(late_v, late_s, in_sem.at[5])

    when(late, list_late)
    node = lax.broadcasted_iota(jnp.int32, (FAR, ROWS - 1), 1)
    slot_at = lax.broadcasted_iota(jnp.int32, (FAR, ROWS - 1), 0)
    entry = flist_v[...]
    row = jnp.zeros_like(entry)
    for height in range(4):
        width = LEAVES >> height
        start = ROWS - 2 * width
        side = entry // width - me + 1
        inside = (node >= start) & (node < start + width)
        row = jnp.where(inside, side * ROWS + start + entry % width, row)
    row = row + jnp.where(slot_at % 2 == 0, 0, 1 - 2 * (row % 2))
    step = entry - me
    root_row = jnp.where(step == -2, 0, jnp.where(step == 2, 1, 2))
    row = jnp.where(node == ROWS - 2, root_row, row)
    live = slot_at < fcount_v[...]
    fid_v[...] = jnp.where(live, row, jnp.where(node == ROWS - 2, 3, ZERO))
    put_near = fetch(nid_v, nid_s, in_sem.at[4])
    put_far = fetch(fid_v, fid_s, in_sem.at[6])
    zero = jnp.zeros((COLS, LANES), F32)
    table_v[ZERO] = zero
    xw_v[NEAR_ZERO] = jnp.zeros((2 * COLS, LANES), BF16)

    def spread(pair, mask):
        return jnp.where(mask, both(pair, pair), 0.0).astype(BF16)

    low128 = lax.broadcasted_iota(jnp.int32, (LANES, LANES), 1) < RANK
    top128 = lax.broadcasted_iota(jnp.int32, (LANES, LANES), 0) < RANK
    diagonal128 = low128 == top128
    low64 = low128[:RANK]

    def compose():
        chains = {14: transfer_v[14].astype(F32)}
        for first, width in ((12, 2), (8, 4), (0, 8)):
            for p in range(width // 2):
                row = first + 2 * p
                matrices = transfer_v[row : row + 2].reshape(LANES, LANES)
                product = dot_nn(spread(chains[first + width + p], diagonal128), matrices)
                chains[row] = product[:RANK]
                chains[row + 1] = product[RANK:]
        for p in range(LEAVES // 2):
            matrices = basis_v[2 * p : 2 * p + 2].reshape(LANES, LANES)
            product = dot_nn(spread(chains[p], diagonal128), matrices).astype(BF16)
            reach_v[:, 2 * p * LANES : (2 * p + 1) * LANES] = product[:RANK]
            reach_v[:, (2 * p + 1) * LANES : (2 * p + 2) * LANES] = product[RANK:]
        pltpu.make_async_copy(ctr_h.at[pl.ds(0, 14)], ctr_v, in_sem.at[8]).wait()
        pltpu.make_async_copy(ccp_h.at[pl.ds(0, 2)], ccp_v, in_sem.at[9]).wait()
        for copy in get_coarse:
            copy.wait()
        for n in range(3):
            matrix = ctr_v[9 + n].astype(F32)
            product = dot_nn(
                spread(matrix, diagonal128), ctr_v[2 * n : 2 * n + 2].reshape(LANES, LANES)
            ).astype(BF16)
            rise_v[n, :, :LANES] = product[:RANK]
            rise_v[n, :, LANES:] = product[RANK:]
        duo_matrix = ctr_v[12].astype(F32)
        duo_matrix = jnp.where(in_duo == 0, duo_matrix, flip(duo_matrix)).astype(BF16)
        quad_matrix = ctr_v[13].astype(F32)
        quad_matrix = jnp.where(lax.rem(duo, 2) == 0, quad_matrix, flip(quad_matrix)).astype(BF16)
        fall = both(dot_nn(quad_matrix[:, :RANK], duo_matrix), duo_matrix.astype(F32)).T[:RANK].astype(BF16)

        def chosen(at, node_here):
            rows = []
            for s in range(3):
                step = clist_s[s, at] - node_here
                row = jnp.where(step == -2, 0, jnp.where(step == 2, 1, 2))
                rows.append(jnp.where(s < ccount_s[at], row, 3))
            return [[jnp.where(row == n, 1.0, 0.0).astype(F32) for n in range(3)] for row in rows]

        for base, width, part, node_here, at, matrices in (
            (0, 2 * LANES, 1, quad, HALF + quad, [rise_v.at[n] for n in range(3)]),
            (6, LANES, 0, duo, duo, [ctr_v.at[6 + n] for n in range(3)]),
        ):
            onto = fall[:, (1 - part) * RANK : (2 - part) * RANK]
            first_two = dot_nn(onto, ccp_v[part, :, :LANES])
            third = dot_nn(onto, ccp_v[part, :, LANES:])
            flags = chosen(at, node_here)
            for n in range(3):
                matrix = matrices[n][...]
                kept = first_two * jnp.where(low64, flags[0][n], flags[1][n])
                product = dot_nn(kept.astype(BF16), both(matrix, matrix))
                product += dot_nn((third * flags[2][n]).astype(BF16), matrix)
                start = base * LANES + n * width
                climb_v[:, start : start + width] = product.astype(BF16)

    early = lax.rem(me, COLUMN) < COLUMN // 2
    when(early, compose)
    when(core == 0, far_gate)
    when(core == 1, lambda: pl.semaphore_wait(far_ready, 1))
    when(left_late, lambda: send_points(to_left))
    send_roots(False)
    when(left_late, lambda: send_pairs(to_left))
    when(jnp.logical_not(early), compose)
    put_near.wait()
    put_far.wait()


    get_coupling.wait()
    matrix = coupling_v[ROWS - 2, :, : 4 * RANK].astype(F32)
    for n in range(3):
        flags = [jnp.where(fid_s[s, ROWS - 2] == n, 1.0, 0.0).astype(F32) for s in range(3)]
        kept = matrix[:, :LANES] * jnp.where(low64, flags[0], flags[1])
        kept += jnp.where(low64, matrix[:, LANES:] * flags[2], 0.0)
        climb_v[:, (9 + n) * LANES : (10 + n) * LANES] = kept.astype(BF16)

    def arrived(buffer, sem):
        remote(buffer, buffer, send_sem.at[2], sem, me, other).wait_recv()

    sides = ((to_left, left_late, 0), (to_right, right_late, 2 * LEAVES))
    arrived(xr_v.at[4], xrecv_sem.at[2])

    def arrange(base, mine, theirs):
        for p in range(LEAVES // 2):
            a = mine[p].astype(F32)
            b = theirs[p].astype(F32)
            xw_v[base + 2 * p] = both(a[:COLS], b[:COLS]).astype(BF16)
            xw_v[base + 2 * p + 1] = both(a[COLS:], b[COLS:]).astype(BF16)

    arrange(LEAVES, xs_v, xr_v.at[4])

    def take_side(side, base):
        slot = side[3]
        arrived(xr_v.at[pl.ds(slot, 2)], xrecv_sem.at[slot // 2])
        arrange(base, xr_v.at[slot], xr_v.at[slot + 1])

    def no_side(base):
        xw_v[base : base + LEAVES] = jnp.zeros((LEAVES, 2 * COLS, LANES), BF16)

    for side, side_late, base in sides:
        now = side[1] & jnp.logical_not(side_late)
        when(now, lambda: take_side(side, base))
        when(jnp.logical_not(now), lambda: no_side(base))

    def near_leaves(at):
        def do():
            for k, (slots, leaves) in enumerate(near_kinds(at)):
                used = near_v.at[pl.ds(0, len(leaves)), pl.ds(0, slots)]
                pltpu.make_async_copy(used, used, near_sem.at[k]).wait()
            for j in range(LEAVES):
                slots = near_slots(j, at)
                if slots:
                    points = jnp.concatenate([xw_v[nid_s[j, s]] for s in range(slots)], axis=1)
                    blocks = jnp.concatenate([near_v[j, s] for s in range(slots)], axis=1)
                    total = dot_nt(points, blocks)
                else:
                    total = jnp.zeros((2 * COLS, LANES), F32)
                yown_v[j] = total[:COLS]
                ysend_v[j] = total[COLS:]

        return do

    for at in range(2):
        when(core == at, near_leaves(at))
    for side, side_late, base in sides:
        when(side_late, lambda: take_side(side, base))

    def late_leaves(at):
        def do():
            pltpu.make_async_copy(late_v, late_s, in_sem.at[5]).wait()
            for j in range(LEAVES):
                slots = near_slots(j, at, 1)
                if slots:
                    points = [xw_v[late_s[LEAVES + j, t]] for t in range(slots)]
                    blocks = [near_v[j, late_s[j, t]] for t in range(slots)]
                    total = dot_nt(jnp.concatenate(points, axis=1), jnp.concatenate(blocks, axis=1))
                    yown_v[j] += total[:COLS]
                    ysend_v[j] += total[COLS:]

        return do

    for at in range(2):
        when(late & (core == at), late_leaves(at))
    send_near = remote(ysend_v, yrecv_v, send_sem.at[2], yrecv_sem, me, other)
    send_near.start()

    for _, there, _, slot, _ in (to_left, to_right):
        landing = ur_v.at[slot // 2]

        def zero_pairs():
            landing[...] = jnp.zeros(us_v.shape, BF16)

        when(there, lambda: arrived(landing, urecv_sem.at[slot // 2]))
        when(jnp.logical_not(there), zero_pairs)
    for slot, base in ((0, 0), (1, 2 * ROWS)):
        for t in range(8):
            tile = ur_v[slot, t].astype(F32)
            for half in range(2):
                pair = tile[half * COLS : (half + 1) * COLS]
                table_v[base + 4 * t + 2 * half] = pair
                table_v[base + 4 * t + 2 * half + 1] = flip(pair)


    def couple(p):
        matrices = coupling_v[2 * p : 2 * p + 2].reshape(LANES, FAR * RANK)
        picked = []
        for node in (2 * p, 2 * p + 1):
            picked.append(
                jnp.concatenate(
                    [
                        meet(table_v[fid_s[2 * t, node]], table_v[fid_s[2 * t + 1, node]])
                        for t in range(FAR // 2)
                    ],
                    axis=1,
                )
            )
        return join(dot_nt(both(*picked).astype(BF16), matrices))

    fields = {14: couple(14)}
    for first, width in ((12, 2), (8, 4), (0, 8)):
        for p in range(width // 2):
            row = first + 2 * p
            matrices = transfer_v[row : row + 2].reshape(LANES, LANES)
            incoming = [couple(row), couple(row + 1)]
            down = dot_nn(spread(fields[first + width + p], diagonal), matrices)
            fields[row] = incoming[0] + down[:COLS]
            fields[row + 1] = incoming[1] + down[COLS:]
    for p in range(LEAVES // 2):
        matrices = basis_v[2 * p : 2 * p + 2].reshape(LANES, LANES)
        far = dot_nn(spread(fields[p], diagonal), matrices)
        out_v[:, 2 * p * LANES : (2 * p + 1) * LANES] = far[:COLS]
        out_v[:, (2 * p + 1) * LANES : (2 * p + 2) * LANES] = far[COLS:]

    arrived(cr_v, crecv_sem)
    def root_of(slot):
        packed = cr_v[slot]
        turned = flip(packed)
        return both(jnp.where(low4, packed, turned), jnp.where(low4, turned, packed))

    gathered = [meet(root_of(i), root_of(i + 1)) for i in range(0, 18, 2)]
    gathered += [root_of(i) for i in range(18, 21)]
    gathered = jnp.concatenate(gathered, axis=1)
    field = dot_nt(both(gathered, gathered).astype(BF16), climb_v[...])
    far = dot_nn(field.astype(BF16), reach_v[...])[:COLS]

    arrived(yrecv_v, yrecv_sem)

    def left_here(buffer, sem):
        remote(buffer, buffer, sem, yrecv_sem, me, other).wait_send()

    when(has_left, lambda: left_here(xr_v.at[pl.ds(0, 3)], send_sem.at[0]))
    when(has_right, lambda: left_here(xr_v.at[pl.ds(0, 3)], send_sem.at[1]))
    left_here(xr_v.at[pl.ds(0, 3)], send_sem.at[2])
    left_here(cr_v, csend_sem)
    for j in range(LEAVES):
        columns = slice(j * LANES, (j + 1) * LANES)
        out_v[:, columns] += far[:, columns] + yown_v[j] + yrecv_v[j]


def body(
    right_sides,
    point_order,
    leaf_basis,
    transfer,
    coupling,
    far_list,
    far_count,
    coarse_transfer,
    coarse_coupling,
    coarse_list,
    coarse_count,
    near_block,
    near_list,
    near_count,
):
    tile = (2 * COLS, LANES)
    dma = pltpu.SemaphoreType.DMA
    return pl.pallas_call(
        kernel,
        out_shape=pltpu.VMEM((COLS, LEAVES * LANES), F32),
        in_specs=[pl.BlockSpec(memory_space=pltpu.HBM)] * 14,
        out_specs=pl.BlockSpec(memory_space=pltpu.VMEM),
        scratch_shapes=[
            pltpu.VMEM((COLS, LEAVES * LANES), F32),
            pltpu.VMEM((LEAVES, LANES), jnp.int32),
            pltpu.VMEM((LEAVES, RANK, LANES), BF16),
            pltpu.VMEM((LEAVES - 1, RANK, LANES), BF16),
            pltpu.VMEM((ROWS - 1, RANK, FAR * RANK), BF16),
            pltpu.VMEM((LEAVES, SLOTS, LANES, LANES), BF16),
            pltpu.VMEM((FAR, ROWS - 1), jnp.int32),
            pltpu.VMEM((1, ROWS - 1), jnp.int32),
            pltpu.VMEM((LEAVES, SLOTS), jnp.int32),
            pltpu.VMEM((1, LEAVES), jnp.int32),
            pltpu.VMEM((14, RANK, LANES), BF16),
            pltpu.VMEM((2, RANK, 3 * RANK), BF16),
            pltpu.SMEM((3, 96), jnp.int32),
            pltpu.SMEM((96,), jnp.int32),
            pltpu.VMEM((FAR, ROWS - 1), jnp.int32),
            pltpu.VMEM((LEAVES, SLOTS), jnp.int32),
            pltpu.SMEM((FAR, ROWS - 1), jnp.int32),
            pltpu.SMEM((LEAVES, SLOTS), jnp.int32),
            pltpu.VMEM((2 * LEAVES, LEAVES), jnp.int32),
            pltpu.SMEM((2 * LEAVES, LEAVES), jnp.int32),
            pltpu.VMEM((LEAVES // 2,) + tile, BF16),
            pltpu.VMEM((LEAVES // 2,) + tile, BF16),
            pltpu.VMEM((5, LEAVES // 2) + tile, BF16),
            pltpu.VMEM((2, LEAVES // 2) + tile, BF16),
            pltpu.VMEM((COLS // 2, LANES), F32),
            pltpu.VMEM((21, COLS // 2, LANES), F32),
            pltpu.VMEM((3 * LEAVES + 1,) + tile, BF16),
            pltpu.VMEM((ZERO + 1, COLS, LANES), F32),
            pltpu.VMEM((PAIRS, COLS, LANES), F32),
            pltpu.VMEM((4, COLS // 2, LANES), F32),
            pltpu.VMEM((21, COLS // 2, LANES), F32),
            pltpu.VMEM((RANK, LEAVES * LANES), BF16),
            pltpu.VMEM((3, RANK, 2 * LANES), BF16),
            pltpu.VMEM((RANK, 12 * LANES), BF16),
            pltpu.VMEM((LEAVES, COLS, LANES), F32),
            pltpu.VMEM((LEAVES, COLS, LANES), F32),
            pltpu.VMEM((LEAVES, COLS, LANES), F32),
            dma((11,)),
            dma((2,)),
            dma((3,)),
            dma((3,)),
            dma((2,)),
            dma,
            dma,
            dma,
            pltpu.SemaphoreType.REGULAR,
            pltpu.SemaphoreType.REGULAR,
        ],
        compiler_params=pltpu.CompilerParams(
            collective_id=0, has_side_effects=True, vmem_limit_bytes=56 << 20
        ),
    )(
        right_sides,
        point_order.reshape(LEAVES, LANES),
        leaf_basis,
        transfer,
        coupling,
        far_list.T,
        far_count.reshape(1, ROWS - 1),
        coarse_transfer,
        coarse_coupling,
        coarse_list.T,
        coarse_count,
        near_block,
        near_list,
        near_count.reshape(1, LEAVES),
    )


def solution(mesh):
    return jax.shard_map(
        body,
        mesh=mesh,
        in_specs=(
            P("rhs", "leaf"),
            P("leaf"),
            P("leaf", None, None),
            P("leaf", None, None),
            P("leaf", None, None),
            P("leaf", None),
            P("leaf"),
            P(),
            P(),
            P(),
            P(),
            P("leaf", "rhs", None, None),
            P("leaf", "rhs"),
            P("leaf"),
        ),
        out_specs=P("rhs", "leaf"),
        check_vma=False,
    )
```

```python
import jax
import jax.numpy as jnp
from jax import lax
from jax.experimental import pallas as pl
from jax.experimental.pallas import tpu as pltpu
from jax.sharding import PartitionSpec as P

MESH = pl.DeviceIdType.MESH
F32 = jnp.float32
BF16 = jnp.bfloat16

DEVICES = 128
LEAVES = 16
RANK = 64
LANES = 128
COLS = 8
SLOTS = 14
FAR = 8
PAIRS = 15
ROWS = 2 * LEAVES
ZERO = 3 * ROWS
NEAR_ZERO = 3 * LEAVES
COLUMN = 8
PLANE = 32
HALF = DEVICES // 2
QUARTER = DEVICES // 4


def near_slots(leaf, core, slabs=3):
    at_y = (leaf & 1) + 2 * (leaf >> 2 & 1)
    at_z = (leaf >> 1 & 1) + 2 * (leaf >> 3 & 1)
    touching = (2 if at_y in (0, 3) else 3) * (2 if at_z in (0, 3) else 3)
    return min(max(3 * touching - core * SLOTS, 0), SLOTS, slabs * touching)


def near_kinds(core):
    kinds = {}
    for leaf in range(LEAVES):
        kinds.setdefault(near_slots(leaf, core), []).append(leaf)
    return sorted((slots, leaves) for slots, leaves in kinds.items() if slots)


def dot_nt(left, right):
    return lax.dot_general(left, right, (((1,), (1,)), ((), ())), preferred_element_type=F32)


def dot_nn(left, right):
    return lax.dot_general(left, right, (((1,), (0,)), ((), ())), preferred_element_type=F32)


def wrap(value, size):
    return lax.rem(value + size, size)


def within(value, size):
    return (value >= 0) & (value < size)


def starts_first(device):
    return lax.rem(device + DEVICES, COLUMN) == 0


def when(flag, do):
    if flag is None:
        do()
    else:
        pl.when(flag)(do)


def kernel(
    rs_h,
    order_h,
    basis_h,
    transfer_h,
    coupling_h,
    flist_h,
    fcount_h,
    ctr_h,
    ccp_h,
    clist_h,
    ccount_h,
    near_h,
    nlist_h,
    ncount_h,
    out_v,
    rs_v,
    order_v,
    basis_v,
    transfer_v,
    coupling_v,
    near_v,
    flist_v,
    fcount_v,
    nlist_v,
    ncount_v,
    ctr_v,
    ccp_v,
    clist_s,
    ccount_s,
    fid_v,
    nid_v,
    fid_s,
    nid_s,
    late_v,
    late_s,
    xs_v,
    us_v,
    xr_v,
    ur_v,
    cs_v,
    cr_v,
    xw_v,
    table_v,
    up_v,
    blank_v,
    spare_v,
    reach_v,
    rise_v,
    climb_v,
    yown_v,
    ysend_v,
    yrecv_v,
    in_sem,
    near_sem,
    send_sem,
    xrecv_sem,
    urecv_sem,
    csend_sem,
    crecv_sem,
    yrecv_sem,
    ahead_sem,
    near_ready,
    far_ready,
):
    me = lax.axis_index("leaf")
    core = lax.axis_index("rhs")
    other = 1 - core
    quad = lax.div(me, 4)
    in_quad = lax.rem(me, 4)
    duo = lax.div(me, 2)
    in_duo = lax.rem(me, 2)
    turn = 1 - 2 * in_duo
    duo_turn = 1 - 2 * lax.rem(duo, 2)
    quad_turn = 1 - 2 * lax.rem(quad, 2)
    quad_from = [wrap(quad + d, QUARTER) for d in (-2, 2, 3 * quad_turn)]
    duo_from = [wrap(duo + d, HALF) for d in (-2, 2, 3 * duo_turn)]
    groups = []
    for n, (send_by, get_by) in enumerate(((2, -2), (-2, 2), (0, 0))):
        for base, size, node, node_turn, nodes, place_in in (
            (0, 4, quad, quad_turn, QUARTER, in_quad),
            (12, 2, duo, duo_turn, HALF, in_duo),
            (18, 1, me, turn, DEVICES, 0),
        ):
            to = node + (send_by if n < 2 else 3 * node_turn)
            source = node + (get_by if n < 2 else 3 * node_turn)
            groups.append(
                (base + size * n, size, size * to, place_in, within(to, nodes), within(source, nodes))
            )
    left = me - 1
    right = me + 1
    has_left = left >= 0
    has_right = right < DEVICES
    column_first = lax.rem(me, COLUMN) == 0
    left_near = has_left & jnp.logical_not(column_first)
    left_late = has_left & column_first
    right_late = has_right & (lax.rem(right, COLUMN) == 0)
    late = left_late | right_late
    far_left = left_late & (lax.rem(me, PLANE) == 0)
    far_right = right_late & (lax.rem(right, PLANE) == 0)
    to_left = (left, has_left, 2, 0, 0)
    to_right = (right, has_right, 0, 2, 1)

    def fetch(source, target, sem):
        copy = pltpu.make_async_copy(source, target, sem)
        copy.start()
        return copy

    get_order = fetch(order_h, order_v, in_sem.at[0])
    for part in range(4):
        columns = pl.ds(part * (LEAVES * LANES // 4), LEAVES * LANES // 4)
        fetch(rs_h.at[:, columns], rs_v.at[:, columns], in_sem.at[1])
    def greet(device_at, device_core):
        pl.semaphore_signal(
            pltpu.get_barrier_semaphore(),
            inc=1,
            device_id=(device_at, device_core),
            device_id_type=MESH,
        )

    when(has_right, lambda: greet(right, jnp.where(lax.rem(right, COLUMN) == 0, 0, 1)))
    when(has_left, lambda: greet(left, 1))
    when(core == 0, lambda: greet(me, 1))
    near_peers = 1 + 2 * jnp.where(has_right, 1, 0) + 2 * jnp.where(left_near, 1, 0)
    far_peers = 2 * jnp.where(left_late, 1, 0)
    for _, size, to, _, there, source_there in groups:

        def greet_all():
            for i in range(size):
                greet(to + i, jnp.where(starts_first(me), 1, 0))

        when(there, greet_all)
        first_ones = jnp.where(starts_first(to), 1, 0)
        near_peers = near_peers + 2 * jnp.where(there, first_ones, 0)
        far_peers = far_peers + 2 * jnp.where(there, size - first_ones, 0)

    get_basis = fetch(basis_h, basis_v, in_sem.at[2])
    get_transfer = fetch(transfer_h, transfer_v, in_sem.at[3])
    get_lists = [
        fetch(nlist_h, nlist_v, in_sem.at[4]),
        fetch(ncount_h, ncount_v, in_sem.at[5]),
        fetch(flist_h, flist_v, in_sem.at[6]),
        fetch(fcount_h, fcount_v, in_sem.at[7]),
    ]
    for n in range(3):
        fetch(ctr_h.at[pl.ds(2 * quad_from[n], 2)], ctr_v.at[pl.ds(2 * n, 2)], in_sem.at[8])
        fetch(ctr_h.at[pl.ds(duo_from[n], 1)], ctr_v.at[pl.ds(6 + n, 1)], in_sem.at[8])
        fetch(ctr_h.at[pl.ds(HALF + quad_from[n], 1)], ctr_v.at[pl.ds(9 + n, 1)], in_sem.at[8])
    fetch(ctr_h.at[pl.ds(duo, 1)], ctr_v.at[pl.ds(12, 1)], in_sem.at[8])
    fetch(ctr_h.at[pl.ds(HALF + quad, 1)], ctr_v.at[pl.ds(13, 1)], in_sem.at[8])
    fetch(ccp_h.at[pl.ds(duo, 1)], ccp_v.at[pl.ds(0, 1)], in_sem.at[9])
    fetch(ccp_h.at[pl.ds(HALF + quad, 1)], ccp_v.at[pl.ds(1, 1)], in_sem.at[9])


    low = lax.broadcasted_iota(jnp.int32, (COLS, LANES), 1) < RANK
    low4 = lax.broadcasted_iota(jnp.int32, (COLS // 2, LANES), 1) < RANK
    low16 = lax.broadcasted_iota(jnp.int32, (2 * COLS, LANES), 1) < RANK
    top16 = lax.broadcasted_iota(jnp.int32, (2 * COLS, LANES), 0) < COLS
    diagonal = low16 == top16

    def both(first, second):
        return jnp.concatenate([first, second], axis=0)

    def meet(first, second):
        return jnp.where(low, first, second)

    def flip(pair):
        return pltpu.roll(pair, RANK, 1)

    def join(product):
        return jnp.where(low, product[:COLS], product[COLS:])

    get_order.wait()
    pltpu.make_async_copy(rs_h, rs_v, in_sem.at[1]).wait()
    place = order_v[...] - me * (LEAVES * LANES)
    for j in range(0, LEAVES, 2):
        blocks = []
        for i in (j, j + 1):
            here = jnp.broadcast_to(place[i : i + 1], (COLS, LANES))
            chunk = here // LANES
            lane = here % LANES
            block = jnp.take_along_axis(rs_v[:, 0:LANES], lane, axis=1, mode="promise_in_bounds")
            for c in range(1, LEAVES):
                found = jnp.take_along_axis(
                    rs_v[:, c * LANES : (c + 1) * LANES], lane, axis=1, mode="promise_in_bounds"
                )
                block = jnp.where(chunk == c, found, block)
            blocks.append(block)
        xs_v[j // 2] = both(*blocks).astype(BF16)

    def remote(source, target, send_sem, recv_sem, device_at, device_core):
        return pltpu.make_async_remote_copy(
            src_ref=source,
            dst_ref=target,
            send_sem=send_sem,
            recv_sem=recv_sem,
            device_id=(device_at, device_core),
            device_id_type=MESH,
        )

    def send_points(side, steps=(0, 1), sem_there=None):
        device_at, _, slot, _, sem = side
        sem_there = xrecv_sem.at[slot // 2] if sem_there is None else sem_there
        for step in steps:
            to_core = other if step else core
            remote(xs_v, xr_v.at[slot + step], send_sem.at[sem], sem_there, device_at, to_core).start()

    def send_pairs(side):
        device_at, _, slot, _, sem = side
        remote(us_v, ur_v.at[slot // 2], send_sem.at[sem], urecv_sem.at[slot // 2], device_at, core).start()

    def send_roots(to_first):
        for first, size, to, place_in, there, source_there in groups:

            def send_root(i):
                target = cr_v.at[first + place_in]
                return lambda: remote(cs_v, target, csend_sem, crecv_sem, to + i, core).start()

            def skip_root():
                fetch(blank_v.at[pl.ds(0, size)], spare_v.at[pl.ds(first, size)], csend_sem)

            def blank_root():
                fetch(blank_v.at[pl.ds(0, size)], cr_v.at[pl.ds(first, size)], crecv_sem)

            if to_first:
                when(there & starts_first(to), send_root(0))
                when(jnp.logical_not(there), skip_root)
                when(jnp.logical_not(source_there), blank_root)
            else:
                when(there & jnp.logical_not(starts_first(to)), send_root(0))
                for i in range(1, size):
                    when(there, send_root(i))

    def tell(sem):
        pl.semaphore_signal(sem, inc=1, device_id=(me, other), device_id_type=MESH)

    def near_gate():
        pl.semaphore_wait(pltpu.get_barrier_semaphore(), near_peers)
        tell(near_ready)

    def far_gate():
        pl.semaphore_wait(pltpu.get_barrier_semaphore(), far_peers)
        tell(far_ready)

    get_coarse = [fetch(clist_h, clist_s, in_sem.at[0]), fetch(ccount_h, ccount_s, in_sem.at[1])]

    blank_v[...] = jnp.zeros(blank_v.shape, F32)
    when(core == 1, near_gate)
    when(core == 0, lambda: pl.semaphore_wait(near_ready, 1))
    remote(xs_v, xr_v.at[4], send_sem.at[2], xrecv_sem.at[2], me, other).start()
    when(far_right & (core == 1), lambda: send_points(to_right, (0,), ahead_sem))
    when(has_right & jnp.logical_not(far_right & (core == 1)), lambda: send_points(to_right))
    when(left_near, lambda: send_points(to_left))

    get_basis.wait()
    get_transfer.wait()
    def fetch_near(at):
        def do():
            for k, (slots, leaves) in enumerate(near_kinds(at)):
                for j in leaves:
                    used = pl.ds(0, slots)
                    fetch(near_h.at[j, used], near_v.at[j, used], near_sem.at[k])

        return do

    for at in range(2):
        when(core == at, fetch_near(at))
    get_coupling = fetch(coupling_h, coupling_v, in_sem.at[10])
    own = ROWS
    for p in range(LEAVES // 2):
        matrices = basis_v[2 * p : 2 * p + 2].reshape(LANES, LANES)
        pair = join(dot_nt(xs_v[p], matrices))
        up_v[p] = pair
        table_v[own + 2 * p] = pair
        table_v[own + 2 * p + 1] = flip(pair)
    first = 0
    for width in (8, 4, 2):
        for p in range(width // 2):
            tile = both(up_v[first + 2 * p], up_v[first + 2 * p + 1]).astype(BF16)
            us_v[first // 2 + p] = tile
            row = first + 2 * p
            matrices = transfer_v[row : row + 2].reshape(LANES, LANES)
            pair = join(dot_nt(tile, matrices))
            at = first + width + p
            up_v[at] = pair
            table_v[own + 2 * at] = pair
            table_v[own + 2 * at + 1] = flip(pair)
        first += width
    last = both(up_v[14], jnp.zeros((COLS, LANES), F32)).astype(BF16)
    us_v[7] = last
    root = transfer_v[14]
    mine = dot_nt(last, both(root, root))
    cs_v[...] = jnp.where(low4, mine[: COLS // 2], mine[COLS // 2 : COLS]).astype(BF16).astype(F32)
    send_roots(True)
    when(has_right, lambda: send_pairs(to_right))
    when(left_near, lambda: send_pairs(to_left))

    for copy in get_lists:
        copy.wait()
    square = lax.broadcasted_iota(jnp.int32, (LEAVES, LEAVES), 0) == lax.broadcasted_iota(
        jnp.int32, (LEAVES, LEAVES), 1
    )
    counts = jnp.broadcast_to(ncount_v[...], (LEAVES, LEAVES))
    counts = jnp.sum(jnp.where(square, counts, 0), axis=1, keepdims=True)
    slot_at = lax.broadcasted_iota(jnp.int32, (LEAVES, SLOTS), 1) + core * SLOTS
    near_row = jnp.where(slot_at < counts, nlist_v[...] - (me - 1) * LEAVES, NEAR_ZERO)
    nid_v[...] = near_row

    def list_late():
        first_row = jnp.where(left_late, 0, 2 * LEAVES)
        hits = jnp.where((near_row >= first_row) & (near_row < first_row + LEAVES), 1, 0)
        column = lax.broadcasted_iota(jnp.int32, (LEAVES, LEAVES), 1)
        place_at = jnp.zeros((LEAVES, LEAVES), jnp.int32)
        slots = jnp.zeros((LEAVES, LEAVES), jnp.int32)
        rows = jnp.full((LEAVES, LEAVES), NEAR_ZERO, jnp.int32)
        for s in range(SLOTS):
            hit = jnp.broadcast_to(hits[:, s : s + 1], (LEAVES, LEAVES))
            here = (column == place_at) & (hit == 1)
            slots = jnp.where(here, s, slots)
            rows = jnp.where(here, jnp.broadcast_to(near_row[:, s : s + 1], (LEAVES, LEAVES)), rows)
            place_at = place_at + hit
        late_v[:LEAVES] = slots
        late_v[LEAVES:] = rows
        fetch(late_v, late_s, in_sem.at[5])

    when(late, list_late)
    node = lax.broadcasted_iota(jnp.int32, (FAR, ROWS - 1), 1)
    slot_at = lax.broadcasted_iota(jnp.int32, (FAR, ROWS - 1), 0)
    entry = flist_v[...]
    row = jnp.zeros_like(entry)
    for height in range(4):
        width = LEAVES >> height
        start = ROWS - 2 * width
        side = entry // width - me + 1
        inside = (node >= start) & (node < start + width)
        row = jnp.where(inside, side * ROWS + start + entry % width, row)
    row = row + jnp.where(slot_at % 2 == 0, 0, 1 - 2 * (row % 2))
    step = entry - me
    root_row = jnp.where(step == -2, 0, jnp.where(step == 2, 1, 2))
    row = jnp.where(node == ROWS - 2, root_row, row)
    live = slot_at < fcount_v[...]
    fid_v[...] = jnp.where(live, row, jnp.where(node == ROWS - 2, 3, ZERO))
    put_near = fetch(nid_v, nid_s, in_sem.at[4])
    put_far = fetch(fid_v, fid_s, in_sem.at[6])
    zero = jnp.zeros((COLS, LANES), F32)
    table_v[ZERO] = zero
    xw_v[NEAR_ZERO] = jnp.zeros((2 * COLS, LANES), BF16)

    def spread(pair, mask):
        return jnp.where(mask, both(pair, pair), 0.0).astype(BF16)

    low128 = lax.broadcasted_iota(jnp.int32, (LANES, LANES), 1) < RANK
    top128 = lax.broadcasted_iota(jnp.int32, (LANES, LANES), 0) < RANK
    diagonal128 = low128 == top128
    low64 = low128[:RANK]

    def compose():
        chains = {14: transfer_v[14].astype(F32)}
        for first, width in ((12, 2), (8, 4), (0, 8)):
            for p in range(width // 2):
                row = first + 2 * p
                matrices = transfer_v[row : row + 2].reshape(LANES, LANES)
                product = dot_nn(spread(chains[first + width + p], diagonal128), matrices)
                chains[row] = product[:RANK]
                chains[row + 1] = product[RANK:]
        for p in range(LEAVES // 2):
            matrices = basis_v[2 * p : 2 * p + 2].reshape(LANES, LANES)
            product = dot_nn(spread(chains[p], diagonal128), matrices).astype(BF16)
            reach_v[:, 2 * p * LANES : (2 * p + 1) * LANES] = product[:RANK]
            reach_v[:, (2 * p + 1) * LANES : (2 * p + 2) * LANES] = product[RANK:]
        pltpu.make_async_copy(ctr_h.at[pl.ds(0, 14)], ctr_v, in_sem.at[8]).wait()
        pltpu.make_async_copy(ccp_h.at[pl.ds(0, 2)], ccp_v, in_sem.at[9]).wait()
        for copy in get_coarse:
            copy.wait()
        for n in range(3):
            matrix = ctr_v[9 + n].astype(F32)
            product = dot_nn(
                spread(matrix, diagonal128), ctr_v[2 * n : 2 * n + 2].reshape(LANES, LANES)
            ).astype(BF16)
            rise_v[n, :, :LANES] = product[:RANK]
            rise_v[n, :, LANES:] = product[RANK:]
        duo_matrix = ctr_v[12].astype(F32)
        duo_matrix = jnp.where(in_duo == 0, duo_matrix, flip(duo_matrix)).astype(BF16)
        quad_matrix = ctr_v[13].astype(F32)
        quad_matrix = jnp.where(lax.rem(duo, 2) == 0, quad_matrix, flip(quad_matrix)).astype(BF16)
        fall = both(dot_nn(quad_matrix[:, :RANK], duo_matrix), duo_matrix.astype(F32)).T[:RANK].astype(BF16)

        def chosen(at, node_here):
            rows = []
            for s in range(3):
                step = clist_s[s, at] - node_here
                row = jnp.where(step == -2, 0, jnp.where(step == 2, 1, 2))
                rows.append(jnp.where(s < ccount_s[at], row, 3))
            return [[jnp.where(row == n, 1.0, 0.0).astype(F32) for n in range(3)] for row in rows]

        for base, width, part, node_here, at, matrices in (
            (0, 2 * LANES, 1, quad, HALF + quad, [rise_v.at[n] for n in range(3)]),
            (6, LANES, 0, duo, duo, [ctr_v.at[6 + n] for n in range(3)]),
        ):
            onto = fall[:, (1 - part) * RANK : (2 - part) * RANK]
            first_two = dot_nn(onto, ccp_v[part, :, :LANES])
            third = dot_nn(onto, ccp_v[part, :, LANES:])
            flags = chosen(at, node_here)
            for n in range(3):
                matrix = matrices[n][...]
                kept = first_two * jnp.where(low64, flags[0][n], flags[1][n])
                product = dot_nn(kept.astype(BF16), both(matrix, matrix))
                product += dot_nn((third * flags[2][n]).astype(BF16), matrix)
                start = base * LANES + n * width
                climb_v[:, start : start + width] = product.astype(BF16)

    early = lax.rem(me, COLUMN) < COLUMN // 2
    when(early, compose)
    def arrived(buffer, sem):
        remote(buffer, buffer, send_sem.at[2], sem, me, other).wait_recv()

    sides = ((to_left, left_late, 0), (to_right, right_late, 2 * LEAVES))

    def arrange(base, mine, theirs):
        for p in range(LEAVES // 2):
            a = mine[p].astype(F32)
            b = theirs[p].astype(F32)
            xw_v[base + 2 * p] = both(a[:COLS], b[:COLS]).astype(BF16)
            xw_v[base + 2 * p + 1] = both(a[COLS:], b[COLS:]).astype(BF16)

    def take_side(side, base):
        slot = side[3]
        arrived(xr_v.at[pl.ds(slot, 2)], xrecv_sem.at[slot // 2])
        arrange(base, xr_v.at[slot], xr_v.at[slot + 1])

    def no_side(base):
        xw_v[base : base + LEAVES] = jnp.zeros((LEAVES, 2 * COLS, LANES), BF16)

    def near_leaves(at):
        def do():
            for k, (slots, leaves) in enumerate(near_kinds(at)):
                used = near_v.at[pl.ds(0, len(leaves)), pl.ds(0, slots)]
                pltpu.make_async_copy(used, used, near_sem.at[k]).wait()
            for j in range(LEAVES):
                slots = near_slots(j, at)
                if slots:
                    points = jnp.concatenate([xw_v[nid_s[j, s]] for s in range(slots)], axis=1)
                    blocks = jnp.concatenate([near_v[j, s] for s in range(slots)], axis=1)
                    total = dot_nt(points, blocks)
                else:
                    total = jnp.zeros((2 * COLS, LANES), F32)
                yown_v[j] = total[:COLS]
                ysend_v[j] = total[COLS:]

        return do

    def near_first():
        put_near.wait()
        arrived(xr_v.at[4], xrecv_sem.at[2])

        arrange(LEAVES, xs_v, xr_v.at[4])

        for side, side_late, base in sides:
            now = side[1] & jnp.logical_not(side_late)
            when(now, lambda: take_side(side, base))
            when(jnp.logical_not(now), lambda: no_side(base))

        for at in range(2):
            when(core == at, near_leaves(at))

    when(far_left, near_first)
    when(core == 0, far_gate)
    when(core == 1, lambda: pl.semaphore_wait(far_ready, 1))
    when(left_late, lambda: send_points(to_left))
    send_roots(False)
    when(left_late, lambda: send_pairs(to_left))
    when(jnp.logical_not(early), compose)
    put_far.wait()


    get_coupling.wait()
    matrix = coupling_v[ROWS - 2, :, : 4 * RANK].astype(F32)
    for n in range(3):
        flags = [jnp.where(fid_s[s, ROWS - 2] == n, 1.0, 0.0).astype(F32) for s in range(3)]
        kept = matrix[:, :LANES] * jnp.where(low64, flags[0], flags[1])
        kept += jnp.where(low64, matrix[:, LANES:] * flags[2], 0.0)
        climb_v[:, (9 + n) * LANES : (10 + n) * LANES] = kept.astype(BF16)

    when(jnp.logical_not(far_left), near_first)
    def take_far():
        slot = to_left[3]
        arrived(xr_v.at[slot], ahead_sem)
        remote(
            xr_v.at[slot], xr_v.at[slot + 1], send_sem.at[2], xrecv_sem.at[slot // 2], me, other
        ).start()
        arrived(xr_v.at[slot + 1], xrecv_sem.at[slot // 2])
        arrange(0, xr_v.at[slot], xr_v.at[slot + 1])

    far_one = far_left & (core == 1)
    when(far_one, take_far)
    when(left_late & jnp.logical_not(far_one), lambda: take_side(to_left, 0))
    when(right_late, lambda: take_side(to_right, 2 * LEAVES))

    def late_leaves(at):
        def do():
            pltpu.make_async_copy(late_v, late_s, in_sem.at[5]).wait()
            for j in range(LEAVES):
                slots = near_slots(j, at, 1)
                if slots:
                    points = [xw_v[late_s[LEAVES + j, t]] for t in range(slots)]
                    blocks = [near_v[j, late_s[j, t]] for t in range(slots)]
                    total = dot_nt(jnp.concatenate(points, axis=1), jnp.concatenate(blocks, axis=1))
                    yown_v[j] += total[:COLS]
                    ysend_v[j] += total[COLS:]

        return do

    for at in range(2):
        when(late & (core == at), late_leaves(at))
    send_near = remote(ysend_v, yrecv_v, send_sem.at[2], yrecv_sem, me, other)
    send_near.start()

    for _, there, _, slot, _ in (to_left, to_right):
        landing = ur_v.at[slot // 2]

        def zero_pairs():
            landing[...] = jnp.zeros(us_v.shape, BF16)

        when(there, lambda: arrived(landing, urecv_sem.at[slot // 2]))
        when(jnp.logical_not(there), zero_pairs)
    for slot, base in ((0, 0), (1, 2 * ROWS)):
        for t in range(8):
            tile = ur_v[slot, t].astype(F32)
            for half in range(2):
                pair = tile[half * COLS : (half + 1) * COLS]
                table_v[base + 4 * t + 2 * half] = pair
                table_v[base + 4 * t + 2 * half + 1] = flip(pair)


    def couple(p):
        matrices = coupling_v[2 * p : 2 * p + 2].reshape(LANES, FAR * RANK)
        picked = []
        for node in (2 * p, 2 * p + 1):
            picked.append(
                jnp.concatenate(
                    [
                        meet(table_v[fid_s[2 * t, node]], table_v[fid_s[2 * t + 1, node]])
                        for t in range(FAR // 2)
                    ],
                    axis=1,
                )
            )
        return join(dot_nt(both(*picked).astype(BF16), matrices))

    fields = {14: couple(14)}
    for first, width in ((12, 2), (8, 4), (0, 8)):
        for p in range(width // 2):
            row = first + 2 * p
            matrices = transfer_v[row : row + 2].reshape(LANES, LANES)
            incoming = [couple(row), couple(row + 1)]
            down = dot_nn(spread(fields[first + width + p], diagonal), matrices)
            fields[row] = incoming[0] + down[:COLS]
            fields[row + 1] = incoming[1] + down[COLS:]
    for p in range(LEAVES // 2):
        matrices = basis_v[2 * p : 2 * p + 2].reshape(LANES, LANES)
        far = dot_nn(spread(fields[p], diagonal), matrices)
        out_v[:, 2 * p * LANES : (2 * p + 1) * LANES] = far[:COLS]
        out_v[:, (2 * p + 1) * LANES : (2 * p + 2) * LANES] = far[COLS:]

    arrived(cr_v, crecv_sem)
    def root_of(slot):
        packed = cr_v[slot]
        turned = flip(packed)
        return both(jnp.where(low4, packed, turned), jnp.where(low4, turned, packed))

    gathered = [meet(root_of(i), root_of(i + 1)) for i in range(0, 18, 2)]
    gathered += [root_of(i) for i in range(18, 21)]
    gathered = jnp.concatenate(gathered, axis=1)
    field = dot_nt(both(gathered, gathered).astype(BF16), climb_v[...])
    far = dot_nn(field.astype(BF16), reach_v[...])[:COLS]

    arrived(yrecv_v, yrecv_sem)

    def left_here(buffer, sem):
        remote(buffer, buffer, sem, yrecv_sem, me, other).wait_send()

    when(has_left, lambda: left_here(xr_v.at[pl.ds(0, 3)], send_sem.at[0]))
    for flag, there, sem, units in (
        (far_right & (core == 1), has_right, send_sem.at[1], 2),
        (far_one, True, send_sem.at[2], 4),
    ):
        when(flag, lambda: left_here(xr_v.at[pl.ds(0, units)], sem))
        when(there & jnp.logical_not(flag), lambda: left_here(xr_v.at[pl.ds(0, 3)], sem))
    left_here(cr_v, csend_sem)
    for j in range(LEAVES):
        columns = slice(j * LANES, (j + 1) * LANES)
        out_v[:, columns] += far[:, columns] + yown_v[j] + yrecv_v[j]


def body(
    right_sides,
    point_order,
    leaf_basis,
    transfer,
    coupling,
    far_list,
    far_count,
    coarse_transfer,
    coarse_coupling,
    coarse_list,
    coarse_count,
    near_block,
    near_list,
    near_count,
):
    tile = (2 * COLS, LANES)
    dma = pltpu.SemaphoreType.DMA
    return pl.pallas_call(
        kernel,
        out_shape=pltpu.VMEM((COLS, LEAVES * LANES), F32),
        in_specs=[pl.BlockSpec(memory_space=pltpu.HBM)] * 14,
        out_specs=pl.BlockSpec(memory_space=pltpu.VMEM),
        scratch_shapes=[
            pltpu.VMEM((COLS, LEAVES * LANES), F32),
            pltpu.VMEM((LEAVES, LANES), jnp.int32),
            pltpu.VMEM((LEAVES, RANK, LANES), BF16),
            pltpu.VMEM((LEAVES - 1, RANK, LANES), BF16),
            pltpu.VMEM((ROWS - 1, RANK, FAR * RANK), BF16),
            pltpu.VMEM((LEAVES, SLOTS, LANES, LANES), BF16),
            pltpu.VMEM((FAR, ROWS - 1), jnp.int32),
            pltpu.VMEM((1, ROWS - 1), jnp.int32),
            pltpu.VMEM((LEAVES, SLOTS), jnp.int32),
            pltpu.VMEM((1, LEAVES), jnp.int32),
            pltpu.VMEM((14, RANK, LANES), BF16),
            pltpu.VMEM((2, RANK, 3 * RANK), BF16),
            pltpu.SMEM((3, 96), jnp.int32),
            pltpu.SMEM((96,), jnp.int32),
            pltpu.VMEM((FAR, ROWS - 1), jnp.int32),
            pltpu.VMEM((LEAVES, SLOTS), jnp.int32),
            pltpu.SMEM((FAR, ROWS - 1), jnp.int32),
            pltpu.SMEM((LEAVES, SLOTS), jnp.int32),
            pltpu.VMEM((2 * LEAVES, LEAVES), jnp.int32),
            pltpu.SMEM((2 * LEAVES, LEAVES), jnp.int32),
            pltpu.VMEM((LEAVES // 2,) + tile, BF16),
            pltpu.VMEM((LEAVES // 2,) + tile, BF16),
            pltpu.VMEM((5, LEAVES // 2) + tile, BF16),
            pltpu.VMEM((2, LEAVES // 2) + tile, BF16),
            pltpu.VMEM((COLS // 2, LANES), F32),
            pltpu.VMEM((21, COLS // 2, LANES), F32),
            pltpu.VMEM((3 * LEAVES + 1,) + tile, BF16),
            pltpu.VMEM((ZERO + 1, COLS, LANES), F32),
            pltpu.VMEM((PAIRS, COLS, LANES), F32),
            pltpu.VMEM((4, COLS // 2, LANES), F32),
            pltpu.VMEM((21, COLS // 2, LANES), F32),
            pltpu.VMEM((RANK, LEAVES * LANES), BF16),
            pltpu.VMEM((3, RANK, 2 * LANES), BF16),
            pltpu.VMEM((RANK, 12 * LANES), BF16),
            pltpu.VMEM((LEAVES, COLS, LANES), F32),
            pltpu.VMEM((LEAVES, COLS, LANES), F32),
            pltpu.VMEM((LEAVES, COLS, LANES), F32),
            dma((11,)),
            dma((2,)),
            dma((3,)),
            dma((3,)),
            dma((2,)),
            dma,
            dma,
            dma,
            dma,
            pltpu.SemaphoreType.REGULAR,
            pltpu.SemaphoreType.REGULAR,
        ],
        compiler_params=pltpu.CompilerParams(
            collective_id=0, has_side_effects=True, vmem_limit_bytes=56 << 20
        ),
    )(
        right_sides,
        point_order.reshape(LEAVES, LANES),
        leaf_basis,
        transfer,
        coupling,
        far_list.T,
        far_count.reshape(1, ROWS - 1),
        coarse_transfer,
        coarse_coupling,
        coarse_list.T,
        coarse_count,
        near_block,
        near_list,
        near_count.reshape(1, LEAVES),
    )


def solution(mesh):
    return jax.shard_map(
        body,
        mesh=mesh,
        in_specs=(
            P("rhs", "leaf"),
            P("leaf"),
            P("leaf", None, None),
            P("leaf", None, None),
            P("leaf", None, None),
            P("leaf", None),
            P("leaf"),
            P(),
            P(),
            P(),
            P(),
            P("leaf", "rhs", None, None),
            P("leaf", "rhs"),
            P("leaf"),
        ),
        out_specs=P("rhs", "leaf"),
        check_vma=False,
    )
```

```python
import jax
import jax.numpy as jnp
from jax import lax
from jax.experimental import pallas as pl
from jax.experimental.pallas import tpu as pltpu
from jax.sharding import PartitionSpec as P

MESH = pl.DeviceIdType.MESH
F32 = jnp.float32
BF16 = jnp.bfloat16

DEVICES = 128
LEAVES = 16
RANK = 64
LANES = 128
COLS = 8
SLOTS = 14
FAR = 8
PAIRS = 15
ROWS = 2 * LEAVES
ZERO = 3 * ROWS
NEAR_ZERO = 3 * LEAVES
COLUMN = 8
PLANE = 32
HALF = DEVICES // 2
QUARTER = DEVICES // 4


def near_slots(leaf, core, slabs=3):
    at_y = (leaf & 1) + 2 * (leaf >> 2 & 1)
    at_z = (leaf >> 1 & 1) + 2 * (leaf >> 3 & 1)
    touching = (2 if at_y in (0, 3) else 3) * (2 if at_z in (0, 3) else 3)
    return min(max(3 * touching - core * SLOTS, 0), SLOTS, slabs * touching)


def near_kinds(core):
    kinds = {}
    for leaf in range(LEAVES):
        kinds.setdefault(near_slots(leaf, core), []).append(leaf)
    return sorted((slots, leaves) for slots, leaves in kinds.items() if slots)


def dot_nt(left, right):
    return lax.dot_general(left, right, (((1,), (1,)), ((), ())), preferred_element_type=F32)


def dot_nn(left, right):
    return lax.dot_general(left, right, (((1,), (0,)), ((), ())), preferred_element_type=F32)


def wrap(value, size):
    return lax.rem(value + size, size)


def within(value, size):
    return (value >= 0) & (value < size)


def starts_first(device):
    return lax.rem(device + DEVICES, COLUMN) == 0


def when(flag, do):
    if flag is None:
        do()
    else:
        pl.when(flag)(do)


def kernel(
    rs_h,
    order_h,
    basis_h,
    transfer_h,
    coupling_h,
    flist_h,
    fcount_h,
    ctr_h,
    ccp_h,
    clist_h,
    ccount_h,
    near_h,
    nlist_h,
    ncount_h,
    out_v,
    rs_v,
    order_v,
    basis_v,
    transfer_v,
    coupling_v,
    near_v,
    flist_v,
    fcount_v,
    nlist_v,
    ncount_v,
    ctr_v,
    ccp_v,
    clist_s,
    ccount_s,
    fid_v,
    nid_v,
    fid_s,
    nid_s,
    late_v,
    late_s,
    xs_v,
    us_v,
    xr_v,
    ur_v,
    cs_v,
    cr_v,
    xw_v,
    table_v,
    up_v,
    blank_v,
    spare_v,
    reach_v,
    rise_v,
    climb_v,
    yown_v,
    ysend_v,
    yrecv_v,
    in_sem,
    near_sem,
    send_sem,
    xrecv_sem,
    urecv_sem,
    csend_sem,
    crecv_sem,
    yrecv_sem,
    ahead_sem,
    ready,
):
    me = lax.axis_index("leaf")
    core = lax.axis_index("rhs")
    other = 1 - core
    quad = lax.div(me, 4)
    in_quad = lax.rem(me, 4)
    duo = lax.div(me, 2)
    in_duo = lax.rem(me, 2)
    turn = 1 - 2 * in_duo
    duo_turn = 1 - 2 * lax.rem(duo, 2)
    quad_turn = 1 - 2 * lax.rem(quad, 2)
    quad_from = [wrap(quad + d, QUARTER) for d in (-2, 2, 3 * quad_turn)]
    duo_from = [wrap(duo + d, HALF) for d in (-2, 2, 3 * duo_turn)]
    groups = []
    for n, (send_by, get_by) in enumerate(((2, -2), (-2, 2), (0, 0))):
        for base, size, node, node_turn, nodes, place_in in (
            (0, 4, quad, quad_turn, QUARTER, in_quad),
            (12, 2, duo, duo_turn, HALF, in_duo),
            (18, 1, me, turn, DEVICES, 0),
        ):
            to = node + (send_by if n < 2 else 3 * node_turn)
            source = node + (get_by if n < 2 else 3 * node_turn)
            groups.append(
                (base + size * n, size, size * to, place_in, within(to, nodes), within(source, nodes))
            )
    left = me - 1
    right = me + 1
    has_left = left >= 0
    has_right = right < DEVICES
    column_first = lax.rem(me, COLUMN) == 0
    left_near = has_left & jnp.logical_not(column_first)
    left_late = has_left & column_first
    right_late = has_right & (lax.rem(right, COLUMN) == 0)
    late = left_late | right_late
    far_left = left_late & (lax.rem(me, PLANE) == 0)
    far_right = right_late & (lax.rem(right, PLANE) == 0)
    to_left = (left, has_left, 2, 0, 0)
    to_right = (right, has_right, 0, 2, 1)

    def fetch(source, target, sem):
        copy = pltpu.make_async_copy(source, target, sem)
        copy.start()
        return copy

    get_order = fetch(order_h, order_v, in_sem.at[0])
    for part in range(4):
        columns = pl.ds(part * (LEAVES * LANES // 4), LEAVES * LANES // 4)
        fetch(rs_h.at[:, columns], rs_v.at[:, columns], in_sem.at[1])
    def greet(device_at, device_core):
        pl.semaphore_signal(
            pltpu.get_barrier_semaphore(),
            inc=1,
            device_id=(device_at, device_core),
            device_id_type=MESH,
        )

    when(has_right, lambda: greet(right, jnp.where(lax.rem(right, COLUMN) == 0, 0, 1)))
    when(has_left, lambda: greet(left, 1))
    when(core == 0, lambda: greet(me, 1))
    near_peers = 1 + 2 * jnp.where(has_right, 1, 0) + 2 * jnp.where(left_near, 1, 0)
    far_peers = 2 * jnp.where(left_late, 1, 0)
    for _, size, to, _, there, source_there in groups:

        def greet_all():
            for i in range(size):
                greet(to + i, jnp.where(starts_first(me), 1, 0))

        when(there, greet_all)
        first_ones = jnp.where(starts_first(to), 1, 0)
        near_peers = near_peers + 2 * jnp.where(there, first_ones, 0)
        far_peers = far_peers + 2 * jnp.where(there, size - first_ones, 0)

    get_basis = fetch(basis_h, basis_v, in_sem.at[2])
    get_transfer = fetch(transfer_h, transfer_v, in_sem.at[3])
    get_lists = [
        fetch(nlist_h, nlist_v, in_sem.at[4]),
        fetch(ncount_h, ncount_v, in_sem.at[5]),
        fetch(flist_h, flist_v, in_sem.at[6]),
        fetch(fcount_h, fcount_v, in_sem.at[7]),
    ]


    low = lax.broadcasted_iota(jnp.int32, (COLS, LANES), 1) < RANK
    low4 = lax.broadcasted_iota(jnp.int32, (COLS // 2, LANES), 1) < RANK
    low16 = lax.broadcasted_iota(jnp.int32, (2 * COLS, LANES), 1) < RANK
    top16 = lax.broadcasted_iota(jnp.int32, (2 * COLS, LANES), 0) < COLS
    diagonal = low16 == top16

    def both(first, second):
        return jnp.concatenate([first, second], axis=0)

    def meet(first, second):
        return jnp.where(low, first, second)

    def flip(pair):
        return pltpu.roll(pair, RANK, 1)

    def join(product):
        return jnp.where(low, product[:COLS], product[COLS:])

    get_order.wait()
    pltpu.make_async_copy(rs_h, rs_v, in_sem.at[1]).wait()
    place = order_v[...] - me * (LEAVES * LANES)
    for j in range(0, LEAVES, 2):
        blocks = []
        for i in (j, j + 1):
            here = jnp.broadcast_to(place[i : i + 1], (COLS, LANES))
            chunk = here // LANES
            lane = here % LANES
            block = jnp.take_along_axis(rs_v[:, 0:LANES], lane, axis=1, mode="promise_in_bounds")
            for c in range(1, LEAVES):
                found = jnp.take_along_axis(
                    rs_v[:, c * LANES : (c + 1) * LANES], lane, axis=1, mode="promise_in_bounds"
                )
                block = jnp.where(chunk == c, found, block)
            blocks.append(block)
        xs_v[j // 2] = both(*blocks).astype(BF16)

    def remote(source, target, send_sem, recv_sem, device_at, device_core):
        return pltpu.make_async_remote_copy(
            src_ref=source,
            dst_ref=target,
            send_sem=send_sem,
            recv_sem=recv_sem,
            device_id=(device_at, device_core),
            device_id_type=MESH,
        )

    def send_points(side, steps=(0, 1), sem_there=None):
        device_at, _, slot, _, sem = side
        sem_there = xrecv_sem.at[slot // 2] if sem_there is None else sem_there
        for step in steps:
            to_core = other if step else core
            remote(xs_v, xr_v.at[slot + step], send_sem.at[sem], sem_there, device_at, to_core).start()

    def send_pairs(side):
        device_at, _, slot, _, sem = side
        remote(us_v, ur_v.at[slot // 2], send_sem.at[sem], urecv_sem.at[slot // 2], device_at, core).start()

    def send_roots(to_first):
        for first, size, to, place_in, there, source_there in groups:

            def send_root(i):
                target = cr_v.at[first + place_in]
                return lambda: remote(cs_v, target, csend_sem, crecv_sem, to + i, core).start()

            def skip_root():
                fetch(blank_v.at[pl.ds(0, size)], spare_v.at[pl.ds(first, size)], csend_sem)

            def blank_root():
                fetch(blank_v.at[pl.ds(0, size)], cr_v.at[pl.ds(first, size)], crecv_sem)

            if to_first:
                when(there & starts_first(to), send_root(0))
                when(jnp.logical_not(there), skip_root)
                when(jnp.logical_not(source_there), blank_root)
            else:
                when(there & jnp.logical_not(starts_first(to)), send_root(0))
                for i in range(1, size):
                    when(there, send_root(i))

    def tell(sem):
        pl.semaphore_signal(sem, inc=1, device_id=(me, other), device_id_type=MESH)

    def near_gate():
        pl.semaphore_wait(pltpu.get_barrier_semaphore(), near_peers)
        tell(ready)

    def far_gate():
        pl.semaphore_wait(pltpu.get_barrier_semaphore(), far_peers)
        tell(ready)

    get_coarse = [fetch(clist_h, clist_s, in_sem.at[0]), fetch(ccount_h, ccount_s, in_sem.at[1])]

    blank_v[...] = jnp.zeros(blank_v.shape, F32)
    when(core == 1, near_gate)
    when(core == 0, lambda: pl.semaphore_wait(ready, 1))
    remote(xs_v, xr_v.at[4], send_sem.at[2], xrecv_sem.at[2], me, other).start()
    when(far_right & (core == 1), lambda: send_points(to_right, (0,), ahead_sem))
    when(has_right & jnp.logical_not(far_right & (core == 1)), lambda: send_points(to_right))
    when(left_near, lambda: send_points(to_left))

    get_basis.wait()
    get_transfer.wait()
    for n in range(3):
        fetch(ctr_h.at[pl.ds(2 * quad_from[n], 2)], ctr_v.at[pl.ds(2 * n, 2)], in_sem.at[2])
        fetch(ctr_h.at[pl.ds(duo_from[n], 1)], ctr_v.at[pl.ds(6 + n, 1)], in_sem.at[2])
        fetch(ctr_h.at[pl.ds(HALF + quad_from[n], 1)], ctr_v.at[pl.ds(9 + n, 1)], in_sem.at[2])
    fetch(ctr_h.at[pl.ds(duo, 1)], ctr_v.at[pl.ds(12, 1)], in_sem.at[2])
    fetch(ctr_h.at[pl.ds(HALF + quad, 1)], ctr_v.at[pl.ds(13, 1)], in_sem.at[2])
    fetch(ccp_h.at[pl.ds(duo, 1)], ccp_v.at[pl.ds(0, 1)], in_sem.at[3])
    fetch(ccp_h.at[pl.ds(HALF + quad, 1)], ccp_v.at[pl.ds(1, 1)], in_sem.at[3])
    def fetch_near(at):
        def do():
            for k, (slots, leaves) in enumerate(near_kinds(at)):
                for j in leaves:
                    used = pl.ds(0, slots)
                    fetch(near_h.at[j, used], near_v.at[j, used], near_sem.at[k])

        return do

    for at in range(2):
        when(core == at, fetch_near(at))
    get_coupling = fetch(coupling_h, coupling_v, in_sem.at[8])
    own = ROWS
    for p in range(LEAVES // 2):
        matrices = basis_v[2 * p : 2 * p + 2].reshape(LANES, LANES)
        pair = join(dot_nt(xs_v[p], matrices))
        up_v[p] = pair
        table_v[own + 2 * p] = pair
        table_v[own + 2 * p + 1] = flip(pair)
    first = 0
    for width in (8, 4, 2):
        for p in range(width // 2):
            tile = both(up_v[first + 2 * p], up_v[first + 2 * p + 1]).astype(BF16)
            us_v[first // 2 + p] = tile
            row = first + 2 * p
            matrices = transfer_v[row : row + 2].reshape(LANES, LANES)
            pair = join(dot_nt(tile, matrices))
            at = first + width + p
            up_v[at] = pair
            table_v[own + 2 * at] = pair
            table_v[own + 2 * at + 1] = flip(pair)
        first += width
    last = both(up_v[14], jnp.zeros((COLS, LANES), F32)).astype(BF16)
    us_v[7] = last
    root = transfer_v[14]
    mine = dot_nt(last, both(root, root))
    cs_v[...] = jnp.where(low4, mine[: COLS // 2], mine[COLS // 2 : COLS]).astype(BF16).astype(F32)
    send_roots(True)
    when(has_right, lambda: send_pairs(to_right))
    when(left_near, lambda: send_pairs(to_left))

    for copy in get_lists:
        copy.wait()
    square = lax.broadcasted_iota(jnp.int32, (LEAVES, LEAVES), 0) == lax.broadcasted_iota(
        jnp.int32, (LEAVES, LEAVES), 1
    )
    counts = jnp.broadcast_to(ncount_v[...], (LEAVES, LEAVES))
    counts = jnp.sum(jnp.where(square, counts, 0), axis=1, keepdims=True)
    slot_at = lax.broadcasted_iota(jnp.int32, (LEAVES, SLOTS), 1) + core * SLOTS
    near_row = jnp.where(slot_at < counts, nlist_v[...] - (me - 1) * LEAVES, NEAR_ZERO)
    nid_v[...] = near_row

    def list_late():
        first_row = jnp.where(left_late, 0, 2 * LEAVES)
        hits = jnp.where((near_row >= first_row) & (near_row < first_row + LEAVES), 1, 0)
        column = lax.broadcasted_iota(jnp.int32, (LEAVES, LEAVES), 1)
        place_at = jnp.zeros((LEAVES, LEAVES), jnp.int32)
        slots = jnp.zeros((LEAVES, LEAVES), jnp.int32)
        rows = jnp.full((LEAVES, LEAVES), NEAR_ZERO, jnp.int32)
        for s in range(SLOTS):
            hit = jnp.broadcast_to(hits[:, s : s + 1], (LEAVES, LEAVES))
            here = (column == place_at) & (hit == 1)
            slots = jnp.where(here, s, slots)
            rows = jnp.where(here, jnp.broadcast_to(near_row[:, s : s + 1], (LEAVES, LEAVES)), rows)
            place_at = place_at + hit
        late_v[:LEAVES] = slots
        late_v[LEAVES:] = rows
        fetch(late_v, late_s, in_sem.at[5])

    when(late, list_late)
    node = lax.broadcasted_iota(jnp.int32, (FAR, ROWS - 1), 1)
    slot_at = lax.broadcasted_iota(jnp.int32, (FAR, ROWS - 1), 0)
    entry = flist_v[...]
    row = jnp.zeros_like(entry)
    for height in range(4):
        width = LEAVES >> height
        start = ROWS - 2 * width
        side = entry // width - me + 1
        inside = (node >= start) & (node < start + width)
        row = jnp.where(inside, side * ROWS + start + entry % width, row)
    row = row + jnp.where(slot_at % 2 == 0, 0, 1 - 2 * (row % 2))
    step = entry - me
    root_row = jnp.where(step == -2, 0, jnp.where(step == 2, 1, 2))
    row = jnp.where(node == ROWS - 2, root_row, row)
    live = slot_at < fcount_v[...]
    fid_v[...] = jnp.where(live, row, jnp.where(node == ROWS - 2, 3, ZERO))
    put_near = fetch(nid_v, nid_s, in_sem.at[4])
    put_far = fetch(fid_v, fid_s, in_sem.at[6])
    zero = jnp.zeros((COLS, LANES), F32)
    table_v[ZERO] = zero
    xw_v[NEAR_ZERO] = jnp.zeros((2 * COLS, LANES), BF16)

    def spread(pair, mask):
        return jnp.where(mask, both(pair, pair), 0.0).astype(BF16)

    low128 = lax.broadcasted_iota(jnp.int32, (LANES, LANES), 1) < RANK
    top128 = lax.broadcasted_iota(jnp.int32, (LANES, LANES), 0) < RANK
    diagonal128 = low128 == top128
    low64 = low128[:RANK]

    def compose():
        chains = {14: transfer_v[14].astype(F32)}
        for first, width in ((12, 2), (8, 4), (0, 8)):
            for p in range(width // 2):
                row = first + 2 * p
                matrices = transfer_v[row : row + 2].reshape(LANES, LANES)
                product = dot_nn(spread(chains[first + width + p], diagonal128), matrices)
                chains[row] = product[:RANK]
                chains[row + 1] = product[RANK:]
        for p in range(LEAVES // 2):
            matrices = basis_v[2 * p : 2 * p + 2].reshape(LANES, LANES)
            product = dot_nn(spread(chains[p], diagonal128), matrices).astype(BF16)
            reach_v[:, 2 * p * LANES : (2 * p + 1) * LANES] = product[:RANK]
            reach_v[:, (2 * p + 1) * LANES : (2 * p + 2) * LANES] = product[RANK:]
        pltpu.make_async_copy(ctr_h.at[pl.ds(0, 14)], ctr_v, in_sem.at[2]).wait()
        pltpu.make_async_copy(ccp_h.at[pl.ds(0, 2)], ccp_v, in_sem.at[3]).wait()
        for copy in get_coarse:
            copy.wait()
        for n in range(3):
            matrix = ctr_v[9 + n].astype(F32)
            product = dot_nn(
                spread(matrix, diagonal128), ctr_v[2 * n : 2 * n + 2].reshape(LANES, LANES)
            ).astype(BF16)
            rise_v[n, :, :LANES] = product[:RANK]
            rise_v[n, :, LANES:] = product[RANK:]
        duo_matrix = ctr_v[12].astype(F32)
        duo_matrix = jnp.where(in_duo == 0, duo_matrix, flip(duo_matrix)).astype(BF16)
        quad_matrix = ctr_v[13].astype(F32)
        quad_matrix = jnp.where(lax.rem(duo, 2) == 0, quad_matrix, flip(quad_matrix)).astype(BF16)
        fall = both(dot_nn(quad_matrix[:, :RANK], duo_matrix), duo_matrix.astype(F32)).T[:RANK].astype(BF16)

        def chosen(at, node_here):
            rows = []
            for s in range(3):
                step = clist_s[s, at] - node_here
                row = jnp.where(step == -2, 0, jnp.where(step == 2, 1, 2))
                rows.append(jnp.where(s < ccount_s[at], row, 3))
            return [[jnp.where(row == n, 1.0, 0.0).astype(F32) for n in range(3)] for row in rows]

        for base, width, part, node_here, at, matrices in (
            (0, 2 * LANES, 1, quad, HALF + quad, [rise_v.at[n] for n in range(3)]),
            (6, LANES, 0, duo, duo, [ctr_v.at[6 + n] for n in range(3)]),
        ):
            onto = fall[:, (1 - part) * RANK : (2 - part) * RANK]
            first_two = dot_nn(onto, ccp_v[part, :, :LANES])
            third = dot_nn(onto, ccp_v[part, :, LANES:])
            flags = chosen(at, node_here)
            for n in range(3):
                matrix = matrices[n][...]
                kept = first_two * jnp.where(low64, flags[0][n], flags[1][n])
                product = dot_nn(kept.astype(BF16), both(matrix, matrix))
                product += dot_nn((third * flags[2][n]).astype(BF16), matrix)
                start = base * LANES + n * width
                climb_v[:, start : start + width] = product.astype(BF16)

    early = lax.rem(me, COLUMN) < COLUMN // 2
    when(early, compose)
    def arrived(buffer, sem):
        remote(buffer, buffer, send_sem.at[2], sem, me, other).wait_recv()

    sides = ((to_left, left_late, 0), (to_right, right_late, 2 * LEAVES))

    def arrange(base, mine, theirs):
        for p in range(LEAVES // 2):
            a = mine[p].astype(F32)
            b = theirs[p].astype(F32)
            xw_v[base + 2 * p] = both(a[:COLS], b[:COLS]).astype(BF16)
            xw_v[base + 2 * p + 1] = both(a[COLS:], b[COLS:]).astype(BF16)

    def take_side(side, base):
        slot = side[3]
        arrived(xr_v.at[pl.ds(slot, 2)], xrecv_sem.at[slot // 2])
        arrange(base, xr_v.at[slot], xr_v.at[slot + 1])

    def no_side(base):
        xw_v[base : base + LEAVES] = jnp.zeros((LEAVES, 2 * COLS, LANES), BF16)

    def near_leaves(at):
        def do():
            for k, (slots, leaves) in enumerate(near_kinds(at)):
                used = near_v.at[pl.ds(0, len(leaves)), pl.ds(0, slots)]
                pltpu.make_async_copy(used, used, near_sem.at[k]).wait()
            for j in range(LEAVES):
                slots = near_slots(j, at)
                if slots:
                    points = jnp.concatenate([xw_v[nid_s[j, s]] for s in range(slots)], axis=1)
                    blocks = jnp.concatenate([near_v[j, s] for s in range(slots)], axis=1)
                    total = dot_nt(points, blocks)
                else:
                    total = jnp.zeros((2 * COLS, LANES), F32)
                yown_v[j] = total[:COLS]
                ysend_v[j] = total[COLS:]

        return do

    def near_first():
        put_near.wait()
        arrived(xr_v.at[4], xrecv_sem.at[2])

        arrange(LEAVES, xs_v, xr_v.at[4])

        for side, side_late, base in sides:
            now = side[1] & jnp.logical_not(side_late)
            when(now, lambda: take_side(side, base))
            when(jnp.logical_not(now), lambda: no_side(base))

        for at in range(2):
            when(core == at, near_leaves(at))

    when(far_left, near_first)
    when(core == 0, far_gate)
    when(core == 1, lambda: pl.semaphore_wait(ready, 1))
    when(left_late, lambda: send_points(to_left))
    send_roots(False)
    when(left_late, lambda: send_pairs(to_left))
    when(jnp.logical_not(early), compose)
    put_far.wait()


    get_coupling.wait()
    matrix = coupling_v[ROWS - 2, :, : 4 * RANK].astype(F32)
    for n in range(3):
        flags = [jnp.where(fid_s[s, ROWS - 2] == n, 1.0, 0.0).astype(F32) for s in range(3)]
        kept = matrix[:, :LANES] * jnp.where(low64, flags[0], flags[1])
        kept += jnp.where(low64, matrix[:, LANES:] * flags[2], 0.0)
        climb_v[:, (9 + n) * LANES : (10 + n) * LANES] = kept.astype(BF16)

    when(jnp.logical_not(far_left), near_first)
    def take_far():
        slot = to_left[3]
        arrived(xr_v.at[slot], ahead_sem)
        remote(
            xr_v.at[slot], xr_v.at[slot + 1], send_sem.at[2], xrecv_sem.at[slot // 2], me, other
        ).start()
        arrived(xr_v.at[slot + 1], xrecv_sem.at[slot // 2])
        arrange(0, xr_v.at[slot], xr_v.at[slot + 1])

    far_one = far_left & (core == 1)
    when(far_one, take_far)
    when(left_late & jnp.logical_not(far_one), lambda: take_side(to_left, 0))
    when(right_late, lambda: take_side(to_right, 2 * LEAVES))

    def late_leaves(at):
        def do():
            pltpu.make_async_copy(late_v, late_s, in_sem.at[5]).wait()
            for j in range(LEAVES):
                slots = near_slots(j, at, 1)
                if slots:
                    points = [xw_v[late_s[LEAVES + j, t]] for t in range(slots)]
                    blocks = [near_v[j, late_s[j, t]] for t in range(slots)]
                    total = dot_nt(jnp.concatenate(points, axis=1), jnp.concatenate(blocks, axis=1))
                    yown_v[j] += total[:COLS]
                    ysend_v[j] += total[COLS:]

        return do

    for at in range(2):
        when(late & (core == at), late_leaves(at))
    send_near = remote(ysend_v, yrecv_v, send_sem.at[2], yrecv_sem, me, other)
    send_near.start()

    for _, there, _, slot, _ in (to_left, to_right):
        landing = ur_v.at[slot // 2]

        def zero_pairs():
            landing[...] = jnp.zeros(us_v.shape, BF16)

        when(there, lambda: arrived(landing, urecv_sem.at[slot // 2]))
        when(jnp.logical_not(there), zero_pairs)
    for slot, base in ((0, 0), (1, 2 * ROWS)):
        for t in range(8):
            tile = ur_v[slot, t].astype(F32)
            for half in range(2):
                pair = tile[half * COLS : (half + 1) * COLS]
                table_v[base + 4 * t + 2 * half] = pair
                table_v[base + 4 * t + 2 * half + 1] = flip(pair)


    def couple(p):
        matrices = coupling_v[2 * p : 2 * p + 2].reshape(LANES, FAR * RANK)
        picked = []
        for node in (2 * p, 2 * p + 1):
            picked.append(
                jnp.concatenate(
                    [
                        meet(table_v[fid_s[2 * t, node]], table_v[fid_s[2 * t + 1, node]])
                        for t in range(FAR // 2)
                    ],
                    axis=1,
                )
            )
        return join(dot_nt(both(*picked).astype(BF16), matrices))

    fields = {14: couple(14)}

    def sweep(parent, row, incoming):
        matrices = transfer_v[row : row + 2].reshape(LANES, LANES)
        down = dot_nn(spread(fields[parent], diagonal), matrices)
        fields[row] = incoming[0] + down[:COLS]
        fields[row + 1] = incoming[1] + down[COLS:]

    ahead = None
    for first, width in ((12, 2), (8, 4), (0, 8)):
        for p in range(width // 2):
            row = first + 2 * p
            coupled = (first + width + p, row, [couple(row), couple(row + 1)])
            if ahead is not None:
                sweep(*ahead)
            ahead = coupled
    sweep(*ahead)
    for p in range(LEAVES // 2):
        matrices = basis_v[2 * p : 2 * p + 2].reshape(LANES, LANES)
        far = dot_nn(spread(fields[p], diagonal), matrices)
        out_v[:, 2 * p * LANES : (2 * p + 1) * LANES] = far[:COLS]
        out_v[:, (2 * p + 1) * LANES : (2 * p + 2) * LANES] = far[COLS:]

    arrived(cr_v, crecv_sem)
    def root_of(slot):
        packed = cr_v[slot]
        turned = flip(packed)
        return both(jnp.where(low4, packed, turned), jnp.where(low4, turned, packed))

    gathered = [meet(root_of(i), root_of(i + 1)) for i in range(0, 18, 2)]
    gathered += [root_of(i) for i in range(18, 21)]
    gathered = jnp.concatenate(gathered, axis=1)
    field = dot_nt(both(gathered, gathered).astype(BF16), climb_v[...])
    far = dot_nn(field.astype(BF16), reach_v[...])[:COLS]

    arrived(yrecv_v, yrecv_sem)

    def left_here(buffer, sem):
        remote(buffer, buffer, sem, yrecv_sem, me, other).wait_send()

    when(has_left, lambda: left_here(xr_v.at[pl.ds(0, 3)], send_sem.at[0]))
    for flag, there, sem, units in (
        (far_right & (core == 1), has_right, send_sem.at[1], 2),
        (far_one, True, send_sem.at[2], 4),
    ):
        when(flag, lambda: left_here(xr_v.at[pl.ds(0, units)], sem))
        when(there & jnp.logical_not(flag), lambda: left_here(xr_v.at[pl.ds(0, 3)], sem))
    left_here(cr_v, csend_sem)
    for j in range(LEAVES):
        columns = slice(j * LANES, (j + 1) * LANES)
        out_v[:, columns] += far[:, columns] + yown_v[j] + yrecv_v[j]


def body(
    right_sides,
    point_order,
    leaf_basis,
    transfer,
    coupling,
    far_list,
    far_count,
    coarse_transfer,
    coarse_coupling,
    coarse_list,
    coarse_count,
    near_block,
    near_list,
    near_count,
):
    tile = (2 * COLS, LANES)
    dma = pltpu.SemaphoreType.DMA
    return pl.pallas_call(
        kernel,
        out_shape=pltpu.VMEM((COLS, LEAVES * LANES), F32),
        in_specs=[pl.BlockSpec(memory_space=pltpu.HBM)] * 14,
        out_specs=pl.BlockSpec(memory_space=pltpu.VMEM),
        scratch_shapes=[
            pltpu.VMEM((COLS, LEAVES * LANES), F32),
            pltpu.VMEM((LEAVES, LANES), jnp.int32),
            pltpu.VMEM((LEAVES, RANK, LANES), BF16),
            pltpu.VMEM((LEAVES - 1, RANK, LANES), BF16),
            pltpu.VMEM((ROWS - 1, RANK, FAR * RANK), BF16),
            pltpu.VMEM((LEAVES, SLOTS, LANES, LANES), BF16),
            pltpu.VMEM((FAR, ROWS - 1), jnp.int32),
            pltpu.VMEM((1, ROWS - 1), jnp.int32),
            pltpu.VMEM((LEAVES, SLOTS), jnp.int32),
            pltpu.VMEM((1, LEAVES), jnp.int32),
            pltpu.VMEM((14, RANK, LANES), BF16),
            pltpu.VMEM((2, RANK, 3 * RANK), BF16),
            pltpu.SMEM((3, 96), jnp.int32),
            pltpu.SMEM((96,), jnp.int32),
            pltpu.VMEM((FAR, ROWS - 1), jnp.int32),
            pltpu.VMEM((LEAVES, SLOTS), jnp.int32),
            pltpu.SMEM((FAR, ROWS - 1), jnp.int32),
            pltpu.SMEM((LEAVES, SLOTS), jnp.int32),
            pltpu.VMEM((2 * LEAVES, LEAVES), jnp.int32),
            pltpu.SMEM((2 * LEAVES, LEAVES), jnp.int32),
            pltpu.VMEM((LEAVES // 2,) + tile, BF16),
            pltpu.VMEM((LEAVES // 2,) + tile, BF16),
            pltpu.VMEM((5, LEAVES // 2) + tile, BF16),
            pltpu.VMEM((2, LEAVES // 2) + tile, BF16),
            pltpu.VMEM((COLS // 2, LANES), F32),
            pltpu.VMEM((21, COLS // 2, LANES), F32),
            pltpu.VMEM((3 * LEAVES + 1,) + tile, BF16),
            pltpu.VMEM((ZERO + 1, COLS, LANES), F32),
            pltpu.VMEM((PAIRS, COLS, LANES), F32),
            pltpu.VMEM((4, COLS // 2, LANES), F32),
            pltpu.VMEM((21, COLS // 2, LANES), F32),
            pltpu.VMEM((RANK, LEAVES * LANES), BF16),
            pltpu.VMEM((3, RANK, 2 * LANES), BF16),
            pltpu.VMEM((RANK, 12 * LANES), BF16),
            pltpu.VMEM((LEAVES, COLS, LANES), F32),
            pltpu.VMEM((LEAVES, COLS, LANES), F32),
            pltpu.VMEM((LEAVES, COLS, LANES), F32),
            dma((9,)),
            dma((2,)),
            dma((3,)),
            dma((3,)),
            dma((2,)),
            dma,
            dma,
            dma,
            dma,
            pltpu.SemaphoreType.REGULAR,
        ],
        compiler_params=pltpu.CompilerParams(
            collective_id=0, has_side_effects=True, vmem_limit_bytes=56 << 20
        ),
    )(
        right_sides,
        point_order.reshape(LEAVES, LANES),
        leaf_basis,
        transfer,
        coupling,
        far_list.T,
        far_count.reshape(1, ROWS - 1),
        coarse_transfer,
        coarse_coupling,
        coarse_list.T,
        coarse_count,
        near_block,
        near_list,
        near_count.reshape(1, LEAVES),
    )


def solution(mesh):
    return jax.shard_map(
        body,
        mesh=mesh,
        in_specs=(
            P("rhs", "leaf"),
            P("leaf"),
            P("leaf", None, None),
            P("leaf", None, None),
            P("leaf", None, None),
            P("leaf", None),
            P("leaf"),
            P(),
            P(),
            P(),
            P(),
            P("leaf", "rhs", None, None),
            P("leaf", "rhs"),
            P("leaf"),
        ),
        out_specs=P("rhs", "leaf"),
        check_vma=False,
    )
```
